32 devices in a mesh: exp: 8 (over z, x), sub: 4 (over y, core).
Axes of the slice: x: 2, y: 2, z: 4, core: 2. Of those that a mesh axis runs over, the one named last changes fastest.
Arguments:
- sky_map: float32 [32, 8, 8, 128], P(('exp', 'sub')), may hold values from -6 to 6
- coeffs: bfloat16 [16, 12, 512, 512], P('exp', None, 'sub'), may hold values from -1.75 to 1.75
- observed: float32 [16, 512, 512], P('exp', 'sub'), may hold values from -6 to 6
- vert_taps: bfloat16 [12, 21], replicated, may hold values from -1.25 to 1.25
- horiz_taps: bfloat16 [12, 21], replicated, may hold values from -1.25 to 1.25
- owner_ids: int32 [16, 64, 4, 1], P('exp', 'sub'), may hold values from 0 to 7; in each aligned block of 64 rows (0 to 63, 64 to 127, ..., all dimensions but the last counted through in order) at most 16 rows name the same one
- offset: int32 [16, 64, 4], P('exp', 'sub'), may hold values from 0 to 7
Outputs:
- sky_final: float32 [32, 8, 8, 128], P(('exp', 'sub'))
- clipped: float32 [16, 512, 512], P('exp', 'sub')
The draws below stay inside these ranges and needn't reach their ends.
Inputs may be any that keep to these rules, and one draw needn't show every extreme that they name: Patch (e, r, q) reads sky tile owner_ids[e, r, q, 0] * 4 + r // 16. Among the 64 patches of one band of one piece (the rows of one device's piece) no owner is named more than 16 times, and in every draw some band names one owner exactly 16 times.
All inputs are finite; a program needn't handle non-finite values.
Results may differ from the reference program's by a relative error of at most 0.0035.
Values may be sent and summed in bfloat16 or wider, within the bound.
No kernel may reach another device: no remote copies, remote signals or barrier semaphores. Data moves between devices by JAX's collectives and lax.ppermute only.
A program may use at most 64 MiB of HBM per device.

```python
import math
from functools import partial
import jax
import jax.numpy as jnp
import numpy as np
from jax import lax

PIX = 512
MODES = 12
TAPS = 21
PH = 8
PW = 128
SKY_DEV = 8
STEPS = 2
BANDS = 4
PROWS = 64
PCOLS = 4
BANDP = 64
CAP = 16
PIECES = 16
TILES = 32
N_EXP = 8


def touch_ends(array, own_key, smallest, largest):
    index_at = [jax.random.randint(jax.random.fold_in(own_key, axis), (), 0, length) for axis, length in enumerate(array.shape)]
    main_axis = array.shape.index(max(array.shape))
    neighbour = index_at[:main_axis] + [(index_at[main_axis] + 1) % array.shape[main_axis]] + index_at[main_axis + 1:]
    return array.at[tuple(index_at)].set(smallest).at[tuple(neighbour)].set(largest)


def level_of(key, extent, shards, smallest, largest):
    def one(position, parts):
        steps = jax.random.uniform(jax.random.fold_in(jax.random.fold_in(key, 6), position), (parts,), jnp.float32, smallest / len(shards), largest / len(shards))
        return jnp.repeat(jnp.exp(steps), extent[position] // parts).reshape((-1,) + (1,) * (len(extent) - position - 1))

    loudness = one(*shards[0])
    for cut in shards[1:]:
        loudness = loudness * one(*cut)
    return loudness


def shared_out(stream_key, own, number, rows, amount, top, bound, lean):
    ranking = jax.random.permutation(stream_key, amount)
    heavy_load, ordinary = load_shares(amount, rows * top, bound, lean, True), load_shares(amount, rows * top, bound, lean, False)
    places = jnp.arange(amount)

    def named(lengths, offset_by):
        used = int((lengths > 0).sum())
        fixed = max(1, used // 4)
        moved = fixed + (places - fixed + offset_by * (used - fixed)) % max(1, amount - fixed)
        return jnp.zeros((amount,), jnp.int32).at[ranking[jnp.where(places < fixed, places, moved)]].set(jnp.asarray(lengths, jnp.int32))

    lengths = jnp.where(number % 4 == 0, named(heavy_load, number // 4), named(ordinary, number - number // 4 - 1))
    mixed = jax.random.permutation(jax.random.fold_in(own, 3), amount)
    source_of, sink = mixed[0:amount // 2 * 2:2], mixed[1:amount // 2 * 2:2]
    room = jnp.minimum(lengths[source_of] - 1, bound - lengths[sink]) // 2
    room = jnp.where((source_of == ranking[0]) | (sink == ranking[0]) | (lengths[sink] == 0), 0, jnp.maximum(room, 0))
    moved = jax.random.randint(jax.random.fold_in(own, 4), (amount // 2,), 0, 1 << 20) % (room + 1)
    lengths = lengths.at[source_of].add(-moved).at[sink].add(moved)
    members = jnp.searchsorted(jnp.cumsum(lengths), jnp.arange(rows * top), side="right").astype(jnp.int32)
    listing = members.reshape(top, rows).T
    listing = listing[jax.random.permutation(jax.random.fold_in(own, 1), rows)]
    offset_by = jax.random.randint(jax.random.fold_in(own, 2), (rows, 1), 0, top)
    return jnp.take_along_axis(listing, (jnp.arange(top)[None, :] + offset_by) % top, axis=1)


def load_shares(count, total, bound, lean, full):
    loads = [(1 << 20) // math.isqrt(rank ** lean) + 1 for rank in range(1, count + 1)]
    largest = bound if full else min(bound, max(-(-total // count), total * loads[0] // sum(loads)))
    least = 1 if total - largest >= count - 1 else 0
    holding, rest = [largest] + [least] * (count - 1), total - largest - least * (count - 1)
    while rest > 0:
        movable = [i for i in range(1, count) if holding[i] < largest] or [i for i in range(1, count) if holding[i] < bound]
        mass, budget = sum([loads[i] for i in movable]), rest
        for i in movable:
            addition = min(bound - holding[i], max(1, budget * loads[i] // mass), rest)
            holding[i] = holding[i] + addition
            rest = rest - addition
    return np.array(holding)


def gaussian(own_key, dims, width, limit, pieces=(), kind=jnp.bfloat16):
    entries = jax.random.normal(own_key, dims, jnp.float32) * width
    if len(pieces) > 0:
        entries = level_of(own_key, dims, pieces, -0.22, 0.18) * entries
    return jnp.clip(entries, min=-limit, max=limit).astype(kind)


def setup_inputs(seed: int = 0) -> dict:
    key_list = jax.random.split(jax.random.key(seed), 8)
    sky_map = gaussian(key_list[0], (TILES, SKY_DEV, PH, PW), 1.0, 6.0, ((0, 32),), jnp.float32)
    coeffs = gaussian(key_list[1], (PIECES, MODES, PIX, PIX), MODES ** -0.5, 1.75, ((0, 8), (2, 4)))
    observed = gaussian(key_list[2], (PIECES, PIX, PIX), 1.0, 6.0, ((0, 8), (1, 4)), jnp.float32)
    vert_taps = gaussian(key_list[3], (MODES, TAPS), TAPS ** -0.5, 1.25)
    horiz_taps = gaussian(key_list[4], (MODES, TAPS), TAPS ** -0.5, 1.25)
    owner_ids_keys = jax.random.split(jax.random.fold_in(key_list[5], 1), PIECES * PROWS * PCOLS // BANDP)
    owner_ids_turns = jax.random.permutation(jax.random.fold_in(key_list[5], 3), PIECES * PROWS * PCOLS // BANDP)
    owner_ids = jax.vmap(lambda own, number: shared_out(jax.random.fold_in(key_list[5], 2), own, number, BANDP, N_EXP, 1, CAP, 2))(owner_ids_keys, owner_ids_turns).reshape((PIECES, PROWS, PCOLS, 1))
    offset = touch_ends(jax.random.randint(key_list[6], (PIECES, PROWS, PCOLS), 0, SKY_DEV), jax.random.fold_in(key_list[6], 1), 0, SKY_DEV - 1).astype(jnp.int32)
    return dict(sky_map=sky_map, coeffs=coeffs, observed=observed, vert_taps=vert_taps, horiz_taps=horiz_taps, owner_ids=owner_ids, offset=offset)


ETA = 0.5
DELTA = 1.0


def correlate(filters, picture, axis_dim, reverse):
    margin = (filters.shape[1] - 1) // 2
    widths = [(0, 0), (0, 0), (0, 0)]
    widths[axis_dim] = (margin, margin)
    padded = jnp.pad(picture, widths)
    length = picture.shape[axis_dim]
    result = jnp.zeros(picture.shape, jnp.float32)
    for lag_index in range(filters.shape[1]):
        start_at = 2 * margin - lag_index if reverse else lag_index
        window = lax.slice_in_dim(padded, start_at, start_at + length, axis=axis_dim)
        result = result + filters[:, lag_index][:, None, None] * window
    return result


def patch_ids(owner_ids, offset):
    rows_band = PROWS // BANDS
    row_index = lax.broadcasted_iota(jnp.int32, offset.shape, 1)
    tile_index = owner_ids[..., 0] * BANDS + row_index // rows_band
    return (tile_index * SKY_DEV + offset).astype(jnp.int32).reshape(-1)


def to_image(patches):
    stacked = patches.reshape(PIECES, PROWS, PCOLS, PH, PW)
    return stacked.transpose(0, 1, 3, 2, 4).reshape(PIECES, PIX, PIX)


def to_patches(picture):
    stacked = picture.reshape(PIECES, PROWS, PH, PCOLS, PW)
    return stacked.transpose(0, 1, 3, 2, 4).reshape(PIECES * PROWS * PCOLS, PH * PW)


def piece_step(vertical, horizontal, inputs):
    picture, coeff_piece, observed_piece = inputs
    coeff_f = coeff_piece.astype(jnp.float32)
    stacked = jnp.broadcast_to(picture.astype(jnp.float32)[None], (MODES, PIX, PIX))
    smoothed = lax.optimization_barrier(correlate(vertical, stacked, 1, False).astype(jnp.bfloat16))
    blurred = correlate(horizontal, smoothed.astype(jnp.float32), 2, False)
    modeled = jnp.sum(coeff_f * blurred, axis=0)
    clipped = jnp.clip(modeled - observed_piece, -DELTA, DELTA)
    weighted = lax.optimization_barrier((coeff_f * clipped[None]).astype(jnp.bfloat16))
    back_rows = lax.optimization_barrier(correlate(horizontal, weighted.astype(jnp.float32), 2, True).astype(jnp.bfloat16))
    gradient = jnp.sum(correlate(vertical, back_rows.astype(jnp.float32), 1, True), axis=0)
    return clipped, gradient


def reference(sky_map, coeffs, observed, vert_taps, horiz_taps, owner_ids, offset):
    vertical = vert_taps.astype(jnp.float32)
    horizontal = horiz_taps.astype(jnp.float32)
    indices = patch_ids(owner_ids, offset)
    segments = TILES * SKY_DEV
    counts = jax.ops.segment_sum(jnp.ones(indices.shape, jnp.float32), indices, num_segments=segments)
    current = sky_map.reshape(segments, PH * PW)
    clipped = jnp.zeros(observed.shape, jnp.float32)
    for step_index in range(STEPS):
        rounded = lax.optimization_barrier(current.astype(jnp.bfloat16))
        pictures = to_image(rounded[indices])
        clipped, gradient = lax.map(partial(piece_step, vertical, horizontal), (pictures, coeffs, observed))
        summed = jax.ops.segment_sum(to_patches(gradient), indices, num_segments=segments)
        current = current - ETA * summed / jnp.maximum(counts, 1.0)[:, None]
    return current.reshape(TILES, SKY_DEV, PH, PW), clipped
```

```python
import functools

import jax
import jax.numpy as jnp
from jax import lax
from jax.experimental import pallas as pl
from jax.experimental.pallas import tpu as pltpu
from jax.sharding import PartitionSpec as P

STEPS = 2
ETA = 0.5
DELTA = 1.0
ROWS = 16
F32 = jnp.float32
BF16 = jnp.bfloat16


def round_up(value, unit):
    return -(-value // unit) * unit


def divisor(value, most):
    return max(k for k in range(1, most + 1) if value % k == 0)


def band_table(filters, height, breadth, direction, shift):
    row_ids = lax.broadcasted_iota(jnp.int32, (height, breadth), 0)
    col_ids = lax.broadcasted_iota(jnp.int32, (height, breadth), 1)
    lag_ids = direction * (col_ids - row_ids) + shift
    tap_ids = lax.broadcasted_iota(jnp.int32, (filters.shape[1], height, breadth), 0)
    select = (tap_ids == lag_ids[None]).astype(BF16)
    return jnp.einsum("mt,tij->mij", filters, select, preferred_element_type=F32).astype(BF16)


def side_table(filters, height, breadth, shift):
    modes, taps = filters.shape
    spread = jnp.repeat(filters.astype(F32).T, breadth, axis=1)
    places = lax.broadcasted_iota(jnp.int32, (height, modes * breadth), 1) % breadth
    lags = lax.broadcasted_iota(jnp.int32, (height, modes * breadth), 0) + shift - places
    table = jnp.zeros((height, modes * breadth), F32)
    for tap in range(taps):
        table = jnp.where(lags == tap, spread[tap][None], table)
    return table.astype(BF16)


def swap_rims(upper, lower, axis):
    count = lax.axis_size(axis)
    even = lax.axis_index(axis) % 2 == 0
    routes = []
    for first in (0, 1):
        pairs = [(k, k + 1) for k in range(first, count - 1, 2)]
        routes.append(pairs + [(b, a) for a, b in pairs])
    near = lax.ppermute(jnp.where(even, lower, upper), axis, routes[0])
    far = lax.ppermute(jnp.where(even, upper, lower), axis, routes[1])
    return near, far


def picture_kernel(even_ref, ids_ref, tiles_ref, picture_ref, near_ref, far_ref, wide_ref, *, patch, rim):
    pieces, height, breadth = picture_ref.shape
    patch_rows, patch_cols = patch
    wide_ref[...] = tiles_ref[...].astype(F32)
    cols = breadth // patch_cols
    rows = height // patch_rows
    together = ROWS // patch_rows
    for piece in range(pieces):
        for row in range(0, rows, together):
            for col in range(cols):
                parts = []
                for inner in range(together):
                    index = ids_ref[(piece * rows + row + inner) * cols + col]
                    start = pl.multiple_of(index * patch_rows, patch_rows)
                    parts.append(wide_ref[pl.ds(start, patch_rows), :])
                picture_ref[
                    piece, row * patch_rows : (row + together) * patch_rows, col * patch_cols : (col + 1) * patch_cols
                ] = jnp.concatenate(parts, axis=0).astype(BF16)

    @pl.when(even_ref[0] == 1)
    def _():
        near_ref[...] = picture_ref[:, height - rim :, :]
        far_ref[...] = picture_ref[:, :rim, :]

    @pl.when(even_ref[0] == 0)
    def _():
        near_ref[...] = picture_ref[:, :rim, :]
        far_ref[...] = picture_ref[:, height - rim :, :]


def windows_of(block, width, stride):
    count = max(1, (block.shape[1] - width) // stride + 1)
    return [block[:, k * stride : k * stride + width] for k in range(count)]


def joined(outs, width, stride):
    if len(outs) == 1:
        return [outs[0][:, k : k + stride] for k in range(0, width, stride)]
    lane = lax.broadcasted_iota(jnp.int32, (outs[0].shape[0], stride), 1)
    blocks = [outs[0][:, :stride]]
    for left, right in zip(outs[:-1], outs[1:]):
        blocks.append(jnp.where(lane < stride // 2, left[:, stride:], right[:, :stride]))
    blocks.append(outs[-1][:, stride:])
    return blocks


def step_kernel(
    even_ref, ids_ref, picture_ref, near_ref, far_ref, coeffs_ref, coeffs_up_ref, coeffs_down_ref, observed_ref,
    observed_up_ref, observed_down_ref, vertical_ref, side_ref, forward_ref, backward_ref, counted_ref,
    clipped_ref, sums_ref, image_ref, field_ref, model_ref, gradient_ref, *, patch, per_tile, with_counts,
):
    pieces, height, breadth = picture_ref.shape
    modes = coeffs_ref.shape[1]
    rim = near_ref.shape[1]
    ext = coeffs_up_ref.shape[2]
    tall = height + 2 * ext
    patch_rows, patch_cols = patch
    width = forward_ref.shape[1]
    stride = patch_cols
    image_ref[:, rim : rim + height, :] = picture_ref[...]

    @pl.when(even_ref[0] == 1)
    def _():
        image_ref[:, :rim, :] = far_ref[...]
        image_ref[:, rim + height :, :] = near_ref[...]

    @pl.when(even_ref[0] == 0)
    def _():
        image_ref[:, :rim, :] = near_ref[...]
        image_ref[:, rim + height :, :] = far_ref[...]

    group = divisor(modes, 4)
    chunk = group * tall

    def smooth(index, carry):
        start = pl.multiple_of(index * chunk, ROWS)
        table = vertical_ref[pl.ds(start, chunk), :]
        for piece in range(pieces):
            for low in range(0, breadth, width):
                field_ref[piece, pl.ds(start, chunk), low : low + width] = jnp.dot(
                    table, image_ref[piece, :, low : low + width], preferred_element_type=F32
                ).astype(BF16)
        return carry

    lax.fori_loop(0, modes // group, smooth, 0)
    model_ref[...] = jnp.zeros(model_ref.shape, F32)

    def coefficient(piece, mode):
        return jnp.concatenate(
            [coeffs_up_ref[piece, mode], coeffs_ref[piece, mode], coeffs_down_ref[piece, mode]], axis=0
        ).astype(F32)

    def blur(table, blocks):
        cuts = [cut for block in blocks for cut in windows_of(block, width, stride)]
        result = jnp.dot(jnp.concatenate(cuts, axis=0), table, preferred_element_type=F32)
        per = len(cuts) // len(blocks)
        outs = [result[k * tall : (k + 1) * tall] for k in range(len(cuts))]
        return [joined(outs[k * per : (k + 1) * per], width, stride) for k in range(len(blocks))]

    def forward(mode, carry):
        start = pl.multiple_of(mode * tall, ROWS)
        blocks = [field_ref[piece, pl.ds(start, tall), :] for piece in range(pieces)]
        for piece, columns in enumerate(blur(forward_ref[mode], blocks)):
            weight = coefficient(piece, mode)
            for k, column in enumerate(columns):
                place = slice(k * stride, (k + 1) * stride)
                model_ref[piece, :, place] += weight[:, place] * column
        return carry

    lax.fori_loop(0, modes, forward, 0)
    for piece in range(pieces):
        seen = jnp.concatenate([observed_up_ref[piece], observed_ref[piece], observed_down_ref[piece]], axis=0)
        model_ref[piece] = jnp.clip(model_ref[piece] - seen, -DELTA, DELTA)
        clipped_ref[piece] = model_ref[piece, ext : ext + height, :]

    def backward(mode, carry):
        start = pl.multiple_of(mode * tall, ROWS)
        blocks = [(coefficient(piece, mode) * model_ref[piece]).astype(BF16) for piece in range(pieces)]
        for piece, columns in enumerate(blur(backward_ref[mode], blocks)):
            for k, column in enumerate(columns):
                field_ref[piece, pl.ds(start, tall), k * stride : (k + 1) * stride] = column.astype(BF16)
        return carry

    lax.fori_loop(0, modes, backward, 0)
    for piece in range(pieces):
        for low in range(0, breadth, width):
            gradient_ref[piece, :, low : low + width] = jnp.dot(
                side_ref[...], field_ref[piece, :, low : low + width], preferred_element_type=F32
            )
    sums_ref[...] = jnp.zeros(sums_ref.shape, F32)
    cols = breadth // patch_cols
    rows = height // patch_rows
    for row in range(rows):
        for col in range(cols):
            for piece in range(pieces):
                index = ids_ref[(piece * rows + row) * cols + col]
                place = pl.ds(pl.multiple_of(index * patch_rows, patch_rows), patch_rows)
                sums_ref[place, :] += gradient_ref[
                    piece, row * patch_rows : (row + 1) * patch_rows, col * patch_cols : (col + 1) * patch_cols
                ]


def update_kernel(sky_ref, parts_ref, counts_ref, next_ref, spread_ref, *, sources, patch_rows):
    held = sky_ref.shape[0]
    total = parts_ref[:held, :]
    for source in range(1, sources):
        total = total + parts_ref[source * held : (source + 1) * held, :]
    fresh = sky_ref[...] - ETA * total / jnp.maximum(counts_ref[...], 1.0)
    next_ref[...] = fresh
    for source in range(sources):
        spread_ref[source * held : (source + 1) * held, :] = fresh.astype(BF16)


def per_device(sky_map, coeffs, observed, vert_taps, horiz_taps, owner_ids, offset):
    pieces, height, breadth = observed.shape
    modes = coeffs.shape[1]
    per_tile, patch_rows, patch_cols = sky_map.shape[1:]
    patch = (patch_rows, patch_cols)
    margin = (vert_taps.shape[1] - 1) // 2
    exp_count = lax.axis_size("exp")
    held = per_tile * patch_rows
    known = exp_count * held
    ext = round_up(margin, ROWS)
    rim = round_up(ext + margin, ROWS)
    tall = height + 2 * ext
    width = min(breadth, 2 * patch_cols)

    sky = sky_map.reshape(held, patch_cols)
    spread = jnp.broadcast_to(sky.astype(BF16)[None], (exp_count, held, patch_cols)).reshape(known, patch_cols)

    def exchange(block):
        return lax.all_to_all(block, "exp", split_axis=0, concat_axis=0, tiled=True)

    tiles = exchange(spread)

    even = (lax.axis_index("sub") % 2 == 0).astype(jnp.int32).reshape(1)
    is_even = lax.axis_index("sub") % 2 == 0
    ids = (owner_ids.reshape(offset.shape) * per_tile + offset).reshape(-1)
    c_near, c_far = swap_rims(coeffs[:, :, :ext], coeffs[:, :, height - ext :], "sub")
    o_near, o_far = swap_rims(observed[:, :ext], observed[:, height - ext :], "sub")
    c_up, c_down = jnp.where(is_even, c_far, c_near), jnp.where(is_even, c_near, c_far)
    o_up, o_down = jnp.where(is_even, o_far, o_near), jnp.where(is_even, o_near, o_far)
    vertical = band_table(vert_taps, tall, height + 2 * rim, 1, margin + ext - rim).reshape(modes * tall, -1)
    side = side_table(vert_taps, height, tall, ext + margin)
    forward = band_table(horiz_taps, width, width, -1, margin)
    backward = band_table(horiz_taps, width, width, 1, margin)

    named = ids[None, :] == lax.broadcasted_iota(jnp.int32, (exp_count * per_tile, ids.shape[0]), 0)
    counted = jnp.sum(named.astype(F32), axis=1)
    counted = jnp.broadcast_to(counted[:, None], (exp_count * per_tile, patch_cols))
    counts = jnp.sum(exchange(counted).reshape(exp_count, per_tile, patch_cols), axis=0)
    counts = jnp.broadcast_to(counts[:, None], (per_tile, patch_rows, patch_cols)).reshape(held, patch_cols)

    vmem = pl.BlockSpec(memory_space=pltpu.VMEM)
    smem = pl.BlockSpec(memory_space=pltpu.SMEM)
    clipped = None
    for step in range(STEPS):
        picture, near, far = pl.pallas_call(
            functools.partial(picture_kernel, patch=patch, rim=rim),
            out_shape=(
                jax.ShapeDtypeStruct((pieces, height, breadth), BF16),
                jax.ShapeDtypeStruct((pieces, rim, breadth), BF16),
                jax.ShapeDtypeStruct((pieces, rim, breadth), BF16),
            ),
            in_specs=[smem, smem, vmem],
            out_specs=(vmem, vmem, vmem),
            scratch_shapes=[pltpu.VMEM((known, patch_cols), F32)],
            compiler_params=pltpu.CompilerParams(vmem_limit_bytes=8 << 20),
            name="picture",
        )(even, ids, tiles)
        count = lax.axis_size("sub")
        routes = []
        for first in (0, 1):
            pairs = [(k, k + 1) for k in range(first, count - 1, 2)]
            routes.append(pairs + [(b, a) for a, b in pairs])
        far = lax.ppermute(far, "sub", routes[1])
        near = lax.ppermute(near, "sub", routes[0])
        clipped, sums = pl.pallas_call(
            functools.partial(step_kernel, patch=patch, per_tile=per_tile, with_counts=step == 0),
            out_shape=(
                jax.ShapeDtypeStruct((pieces, height, breadth), F32),
                jax.ShapeDtypeStruct((known, patch_cols), F32),
            ),
            in_specs=[smem, smem] + [vmem] * 14,
            out_specs=(vmem, vmem),
            scratch_shapes=[
                pltpu.VMEM((pieces, height + 2 * rim, breadth), BF16),
                pltpu.VMEM((pieces, modes * tall, breadth), BF16),
                pltpu.VMEM((pieces, tall, breadth), F32),
                pltpu.VMEM((pieces, height, breadth), F32),
            ],
            compiler_params=pltpu.CompilerParams(vmem_limit_bytes=40 << 20),
            name="step",
        )(
            even, ids, picture, near, far, coeffs, c_up, c_down, observed, o_up, o_down,
            vertical, side, forward, backward, counts,
        )
        parts = exchange(sums)
        sky, spread = pl.pallas_call(
            functools.partial(update_kernel, sources=exp_count, patch_rows=patch_rows),
            out_shape=(
                jax.ShapeDtypeStruct((held, patch_cols), F32),
                jax.ShapeDtypeStruct((known, patch_cols), BF16),
            ),
            in_specs=[vmem] * 3,
            out_specs=(vmem, vmem),
            name="update",
        )(sky, parts, counts)
        if step + 1 < STEPS:
            tiles = exchange(spread)
    return sky.reshape(sky_map.shape), clipped


def solution(mesh):
    return jax.shard_map(
        per_device,
        mesh=mesh,
        in_specs=(
            P(("exp", "sub"), None, None, None),
            P("exp", None, "sub", None),
            P("exp", "sub", None),
            P(),
            P(),
            P("exp", "sub", None, None),
            P("exp", "sub", None),
        ),
        out_specs=(P(("exp", "sub"), None, None, None), P("exp", "sub", None)),
        check_vma=False,
    )
```

```python
import functools

import jax
import jax.numpy as jnp
from jax import lax
from jax.experimental import pallas as pl
from jax.experimental.pallas import tpu as pltpu
from jax.sharding import PartitionSpec as P

STEPS = 2
ETA = 0.5
DELTA = 1.0
ROWS = 16
LANES = 128
PARTS = 3
F32 = jnp.float32
BF16 = jnp.bfloat16


def round_up(value, unit):
    return -(-value // unit) * unit


def divisor(value, most):
    return max(k for k in range(1, most + 1) if value % k == 0)


def pair_routes(axis):
    count = lax.axis_size(axis)
    routes = []
    for first in (0, 1):
        pairs = [(k, k + 1) for k in range(first, count - 1, 2)]
        routes.append(pairs + [(b, a) for a, b in pairs])
    return routes


def rims_kernel(even_ref, coeffs_ref, observed_ref, near_ref, far_ref, seen_ref, sems):
    modes, height = coeffs_ref.shape[1:3]
    ext = near_ref.shape[2]
    even = even_ref[0]
    near_at = pl.multiple_of(even * (height - ext), ROWS)
    far_at = pl.multiple_of((1 - even) * (height - ext), ROWS)
    copies = []
    for side, (start, out_ref) in enumerate(((near_at, near_ref), (far_at, far_ref))):
        copies.append(
            pltpu.make_async_copy(observed_ref.at[:, pl.ds(start, ext), :], seen_ref.at[side], sems.at[2 * side])
        )
        copies.append(
            pltpu.make_async_copy(
                coeffs_ref.at[:, :, pl.ds(start, ext), :], out_ref.at[:, pl.ds(0, modes)], sems.at[2 * side + 1]
            )
        )
    for copy in copies:
        copy.start()
    for side, out_ref in enumerate((near_ref, far_ref)):
        copies[2 * side].wait()
        rest = seen_ref[side]
        for part in range(PARTS):
            piece = rest.astype(BF16)
            out_ref[:, modes + part] = piece
            rest = rest - piece.astype(F32)
    copies[1].wait()
    copies[3].wait()


def prep_kernel(
    owners_ref, offset_ref, vert_ref, horiz_ref, vertical_ref, side_ref, forward_ref, backward_ref, counted_ref,
    taps_ref, turned_ref, *, ext, rim, per_tile,
):
    modes, taps = vert_ref.shape
    margin = (taps - 1) // 2
    width = forward_ref.shape[1]
    height = side_ref.shape[0]
    tall = vertical_ref.shape[0] // modes
    reach = vertical_ref.shape[1]

    taps_ref[...] = jnp.zeros(taps_ref.shape, F32)
    taps_ref[0, :modes, :taps] = vert_ref[...].astype(F32)
    taps_ref[1, :modes, :taps] = horiz_ref[...].astype(F32)
    turn = lax.broadcasted_iota(jnp.int32, (LANES, LANES), 0) + lax.broadcasted_iota(jnp.int32, (LANES, LANES), 1)
    flipped = jnp.dot(
        taps_ref[1].astype(BF16), (turn == taps - 1).astype(F32).astype(BF16), preferred_element_type=F32
    )
    taps_ref[2] = flipped

    def banded(row, shift, rows, cols):
        turned = pltpu.roll(jnp.broadcast_to(row, (8, LANES)), (-shift) % LANES, 1)
        ring = pltpu.roll(jnp.broadcast_to(turned[:1], (LANES, LANES)), 0, 1, stride=1, stride_axis=0)
        lag = (
            lax.broadcasted_iota(jnp.int32, (rows, cols), 1) - lax.broadcasted_iota(jnp.int32, (rows, cols), 0) + shift
        )
        across = jnp.concatenate([ring] * (-(-cols // LANES)), axis=1)[:, :cols]
        whole = jnp.concatenate([across] * (-(-rows // LANES)), axis=0)[:rows]
        return jnp.where((lag >= 0) & (lag < taps), whole, 0.0)

    for mode in range(modes):
        row = taps_ref[0, mode : mode + 1]
        place = slice(mode * tall, (mode + 1) * tall)
        vertical_ref[place, :] = banded(row, margin + ext - rim, tall, reach).astype(BF16)
        turned_ref[place, :] = banded(row, margin + ext, tall, height)
        backward_ref[mode] = banded(taps_ref[1, mode : mode + 1], margin, width, width).astype(BF16)
        forward_ref[mode] = banded(taps_ref[2, mode : mode + 1], margin, width, width).astype(BF16)
    side_ref[...] = turned_ref[...].T.astype(BF16)

    counted_ref[...] = jnp.zeros(counted_ref.shape, F32)
    for piece in range(offset_ref.shape[0]):
        for row in range(offset_ref.shape[1]):
            for col in range(offset_ref.shape[2]):
                index = owners_ref[piece, row, col, 0] * per_tile + offset_ref[piece, row, col]
                counted_ref[pl.ds(index, 1), :] += 1.0


def picture_kernel(even_ref, owners_ref, offset_ref, tiles_ref, picture_ref, near_ref, far_ref, wide_ref, *, patch, per_tile):
    pieces, height, breadth = picture_ref.shape
    rim = near_ref.shape[1]
    patch_rows, patch_cols = patch
    wide_ref[...] = tiles_ref[...].astype(F32)
    cols = breadth // patch_cols
    rows = height // patch_rows
    together = ROWS // patch_rows
    for piece in range(pieces):
        for row in range(0, rows, together):
            for col in range(cols):
                parts = []
                for inner in range(row, row + together):
                    index = owners_ref[piece, inner, col, 0] * per_tile + offset_ref[piece, inner, col]
                    start = pl.multiple_of(index * patch_rows, patch_rows)
                    parts.append(wide_ref[pl.ds(start, patch_rows), :])
                picture_ref[
                    piece, row * patch_rows : (row + together) * patch_rows, col * patch_cols : (col + 1) * patch_cols
                ] = jnp.concatenate(parts, axis=0).astype(BF16)
    even = even_ref[0]
    near_ref[...] = picture_ref[:, pl.ds(pl.multiple_of(even * (height - rim), ROWS), rim), :]
    far_ref[...] = picture_ref[:, pl.ds(pl.multiple_of((1 - even) * (height - rim), ROWS), rim), :]


def windows_of(block, width, stride):
    count = max(1, (block.shape[1] - width) // stride + 1)
    return [block[:, k * stride : k * stride + width] for k in range(count)]


def joined(outs, width, stride):
    if len(outs) == 1:
        return [outs[0][:, k : k + stride] for k in range(0, width, stride)]
    lane = lax.broadcasted_iota(jnp.int32, (outs[0].shape[0], stride), 1)
    blocks = [outs[0][:, :stride]]
    for left, right in zip(outs[:-1], outs[1:]):
        blocks.append(jnp.where(lane < stride // 2, left[:, stride:], right[:, :stride]))
    blocks.append(outs[-1][:, stride:])
    return blocks


def step_kernel(
    even_ref, owners_ref, offset_ref, picture_ref, near_ref, far_ref, counted_ref, coeffs_any, rims_near_any,
    rims_far_any, observed_any, vertical_any, side_any, forward_any, backward_any,
    clipped_ref, sums_ref, image_ref, field_ref, model_ref, gradient_ref, coeffs_ref, seen_ref, seen_rims_ref,
    vertical_ref, side_ref, forward_ref, backward_ref, sems, *, patch, per_tile, slot,
):
    pieces, height, breadth = picture_ref.shape
    modes = coeffs_ref.shape[1]
    rim = near_ref.shape[1]
    tall = coeffs_ref.shape[2]
    ext = (tall - height) // 2
    patch_rows, patch_cols = patch
    width = forward_ref.shape[1]
    stride = patch_cols
    even = even_ref[0]
    near_at = pl.multiple_of(even * (ext + height), ROWS)
    far_at = pl.multiple_of((1 - even) * (ext + height), ROWS)

    moves = [
        (vertical_any, vertical_ref),
        (forward_any, forward_ref),
        (coeffs_any, coeffs_ref.at[:, :, pl.ds(ext, height), :]),
        (rims_near_any.at[:, pl.ds(0, modes)], coeffs_ref.at[:, :, pl.ds(near_at, ext), :]),
        (rims_far_any.at[:, pl.ds(0, modes)], coeffs_ref.at[:, :, pl.ds(far_at, ext), :]),
        (observed_any, seen_ref.at[:, pl.ds(ext, height), :]),
        (rims_near_any.at[:, pl.ds(modes, PARTS)], seen_rims_ref.at[0]),
        (rims_far_any.at[:, pl.ds(modes, PARTS)], seen_rims_ref.at[1]),
        (backward_any, backward_ref),
        (side_any, side_ref),
    ]
    copies = [pltpu.make_async_copy(source, target, sems.at[k]) for k, (source, target) in enumerate(moves)]
    for copy in copies:
        copy.start()

    image_ref[:, rim : rim + height, :] = picture_ref[...]
    image_ref[:, pl.ds(pl.multiple_of(even * (rim + height), ROWS), rim), :] = near_ref[...]
    image_ref[:, pl.ds(pl.multiple_of((1 - even) * (rim + height), ROWS), rim), :] = far_ref[...]

    group = divisor(modes, 4)
    chunk = group * tall
    copies[0].wait()
    for start in range(0, modes * tall, chunk):
        table = vertical_ref[start : start + chunk, :]
        for piece in range(pieces):
            for low in range(0, breadth, width):
                field_ref[piece, start : start + chunk, low : low + width] = jnp.dot(
                    table, image_ref[piece, :, low : low + width], preferred_element_type=F32
                ).astype(BF16)

    def blur(table, blocks):
        cuts = [cut for block in blocks for cut in windows_of(block, width, stride)]
        result = jnp.dot(jnp.concatenate(cuts, axis=0), table, preferred_element_type=F32)
        per = len(cuts) // len(blocks)
        outs = [result[k * tall : (k + 1) * tall] for k in range(len(cuts))]
        return [joined(outs[k * per : (k + 1) * per], width, stride) for k in range(len(blocks))]

    for k in range(1, 5):
        copies[k].wait()
    for mode in range(modes):
        start = mode * tall
        blocks = [field_ref[piece, start : start + tall, :] for piece in range(pieces)]
        for piece, columns in enumerate(blur(forward_ref[mode], blocks)):
            weight = coeffs_ref[piece, mode].astype(F32)
            for k, column in enumerate(columns):
                place = slice(k * stride, (k + 1) * stride)
                if mode == 0:
                    model_ref[piece, :, place] = weight[:, place] * column
                else:
                    model_ref[piece, :, place] += weight[:, place] * column
    for k in range(5, 8):
        copies[k].wait()
    for side, start in enumerate((near_at, far_at)):
        total = seen_rims_ref[side, :, 0].astype(F32)
        for part in range(1, PARTS):
            total = total + seen_rims_ref[side, :, part].astype(F32)
        seen_ref[:, pl.ds(start, ext), :] = total
    model_ref[...] = jnp.clip(model_ref[...] - seen_ref[...], -DELTA, DELTA)
    clipped_ref[...] = model_ref[:, ext : ext + height, :]

    copies[8].wait()
    for mode in range(modes):
        start = mode * tall
        blocks = [(coeffs_ref[piece, mode].astype(F32) * model_ref[piece]).astype(BF16) for piece in range(pieces)]
        for piece, columns in enumerate(blur(backward_ref[mode], blocks)):
            for k, column in enumerate(columns):
                field_ref[piece, start : start + tall, k * stride : (k + 1) * stride] = column.astype(BF16)
    copies[9].wait()
    for piece in range(pieces):
        for low in range(0, breadth, width):
            gradient_ref[piece, :, low : low + width] = jnp.dot(
                side_ref[...], field_ref[piece, :, low : low + width], preferred_element_type=F32
            )
    sums_ref[...] = jnp.zeros(sums_ref.shape, F32)
    if slot > per_tile * patch_rows:
        for owner in range(sums_ref.shape[0] // slot):
            start = owner * slot + per_tile * patch_rows
            sums_ref[start : start + per_tile, :] = counted_ref[owner * per_tile : (owner + 1) * per_tile, :]
    cols = breadth // patch_cols
    rows = height // patch_rows
    for row in range(rows):
        for col in range(cols):
            for piece in range(pieces):
                index = owners_ref[piece, row, col, 0] * slot + offset_ref[piece, row, col] * patch_rows
                place = pl.ds(pl.multiple_of(index, patch_rows), patch_rows)
                sums_ref[place, :] += gradient_ref[
                    piece, row * patch_rows : (row + 1) * patch_rows, col * patch_cols : (col + 1) * patch_cols
                ]


def update_kernel(sky_ref, parts_ref, *refs, slot, first, last):
    refs = list(refs)
    held = sky_ref.shape[0]
    total = parts_ref[:slot, :]
    for start in range(slot, parts_ref.shape[0], slot):
        total = total + parts_ref[start : start + slot, :]
    if first:
        named = total[held:]
        repeat = held // named.shape[0]
        counts = jnp.broadcast_to(named[:, None, :], (named.shape[0], repeat, named.shape[1])).reshape(sky_ref.shape)
        refs.pop()[...] = counts
    else:
        counts = refs.pop(0)[...]
    fresh = sky_ref[...] - ETA * total[:held] / jnp.maximum(counts, 1.0)
    refs[0][...] = fresh
    if not last:
        for start in range(0, refs[1].shape[0], held):
            refs[1][start : start + held, :] = fresh.astype(BF16)


def per_device(sky_map, coeffs, observed, vert_taps, horiz_taps, owner_ids, offset):
    pieces, height, breadth = observed.shape
    modes = coeffs.shape[1]
    per_tile, patch_rows, patch_cols = sky_map.shape[1:]
    patch = (patch_rows, patch_cols)
    margin = (vert_taps.shape[1] - 1) // 2
    exp_count = lax.axis_size("exp")
    held = per_tile * patch_rows
    known = exp_count * held
    ext = round_up(margin, ROWS)
    rim = round_up(ext + margin, ROWS)
    tall = height + 2 * ext
    width = min(breadth, 2 * patch_cols)
    routes = pair_routes("sub")
    vmem = pl.BlockSpec(memory_space=pltpu.VMEM)
    smem = pl.BlockSpec(memory_space=pltpu.SMEM)
    somewhere = pl.BlockSpec(memory_space=pl.ANY)

    def exchange(block):
        return lax.all_to_all(block, "exp", split_axis=0, concat_axis=0, tiled=True)

    sky = sky_map.reshape(held, patch_cols)
    spread = jnp.broadcast_to(sky.astype(BF16)[None], (exp_count, held, patch_cols)).reshape(known, patch_cols)
    tiles = exchange(spread)
    even = (1 - lax.axis_index("sub") % 2).astype(jnp.int32).reshape(1)

    rim_shape = jax.ShapeDtypeStruct((pieces, modes + PARTS, ext, breadth), BF16)
    rims_near, rims_far = pl.pallas_call(
        rims_kernel,
        out_shape=(rim_shape, rim_shape),
        in_specs=[smem, somewhere, somewhere],
        out_specs=(vmem, vmem),
        scratch_shapes=[pltpu.VMEM((2, pieces, ext, breadth), F32), pltpu.SemaphoreType.DMA((4,))],
        compiler_params=pltpu.CompilerParams(vmem_limit_bytes=8 << 20),
        name="rims",
    )(even, coeffs, observed)
    rims_far = lax.ppermute(rims_far, "sub", routes[1])
    rims_near = lax.ppermute(rims_near, "sub", routes[0])
    vertical, side, forward, backward, counted = pl.pallas_call(
        functools.partial(prep_kernel, ext=ext, rim=rim, per_tile=per_tile),
        out_shape=(
            jax.ShapeDtypeStruct((modes * tall, height + 2 * rim), BF16),
            jax.ShapeDtypeStruct((height, modes * tall), BF16),
            jax.ShapeDtypeStruct((modes, width, width), BF16),
            jax.ShapeDtypeStruct((modes, width, width), BF16),
            jax.ShapeDtypeStruct((exp_count * per_tile, patch_cols), F32),
        ),
        in_specs=[smem, smem, vmem, vmem],
        out_specs=(vmem,) * 5,
        scratch_shapes=[
            pltpu.VMEM((3, round_up(modes, 8), LANES), F32),
            pltpu.VMEM((modes * tall, height), F32),
        ],
        compiler_params=pltpu.CompilerParams(vmem_limit_bytes=16 << 20),
        name="prep",
    )(owner_ids, offset, vert_taps, horiz_taps)

    clipped, counts = None, None
    for step in range(STEPS):
        first, last = step == 0, step + 1 == STEPS
        picture, near, far = pl.pallas_call(
            functools.partial(picture_kernel, patch=patch, per_tile=per_tile),
            out_shape=(
                jax.ShapeDtypeStruct((pieces, height, breadth), BF16),
                jax.ShapeDtypeStruct((pieces, rim, breadth), BF16),
                jax.ShapeDtypeStruct((pieces, rim, breadth), BF16),
            ),
            in_specs=[smem, smem, smem, vmem],
            out_specs=(vmem, vmem, vmem),
            scratch_shapes=[pltpu.VMEM((known, patch_cols), F32)],
            compiler_params=pltpu.CompilerParams(vmem_limit_bytes=8 << 20),
            name="picture",
        )(even, owner_ids, offset, tiles)
        far = lax.ppermute(far, "sub", routes[1])
        near = lax.ppermute(near, "sub", routes[0])
        slot = held + (round_up(per_tile, 8) if first else 0)
        clipped, sums = pl.pallas_call(
            functools.partial(step_kernel, patch=patch, per_tile=per_tile, slot=slot),
            out_shape=(
                jax.ShapeDtypeStruct((pieces, height, breadth), F32),
                jax.ShapeDtypeStruct((exp_count * slot, patch_cols), F32),
            ),
            in_specs=[smem] * 3 + [vmem] * 4 + [somewhere] * 8,
            out_specs=(vmem, vmem),
            scratch_shapes=[
                pltpu.VMEM((pieces, height + 2 * rim, breadth), BF16),
                pltpu.VMEM((pieces, modes * tall, breadth), BF16),
                pltpu.VMEM((pieces, tall, breadth), F32),
                pltpu.VMEM((pieces, height, breadth), F32),
                pltpu.VMEM((pieces, modes, tall, breadth), BF16),
                pltpu.VMEM((pieces, tall, breadth), F32),
                pltpu.VMEM((2, pieces, PARTS, ext, breadth), BF16),
                pltpu.VMEM(vertical.shape, BF16),
                pltpu.VMEM(side.shape, BF16),
                pltpu.VMEM(forward.shape, BF16),
                pltpu.VMEM(backward.shape, BF16),
                pltpu.SemaphoreType.DMA((10,)),
            ],
            compiler_params=pltpu.CompilerParams(vmem_limit_bytes=28 << 20),
            name="step",
        )(
            even, owner_ids, offset, picture, near, far, counted, coeffs, rims_near, rims_far, observed,
            vertical, side, forward, backward,
        )
        parts = exchange(sums)
        sky_shape = jax.ShapeDtypeStruct((held, patch_cols), F32)
        results = [sky_shape]
        if not last:
            results.append(jax.ShapeDtypeStruct((known, patch_cols), BF16))
        if first:
            results.append(sky_shape)
        operands = [sky, parts] if first else [sky, parts, counts]
        answer = pl.pallas_call(
            functools.partial(update_kernel, slot=slot, first=first, last=last),
            out_shape=tuple(results),
            in_specs=[vmem] * len(operands),
            out_specs=(vmem,) * len(results),
            name="update",
        )(*operands)
        sky = answer[0]
        if first:
            counts = answer[-1]
        if not last:
            tiles = exchange(answer[1])
    return sky.reshape(sky_map.shape), clipped


def solution(mesh):
    return jax.shard_map(
        per_device,
        mesh=mesh,
        in_specs=(
            P(("exp", "sub"), None, None, None),
            P("exp", None, "sub", None),
            P("exp", "sub", None),
            P(),
            P(),
            P("exp", "sub", None, None),
            P("exp", "sub", None),
        ),
        out_specs=(P(("exp", "sub"), None, None, None), P("exp", "sub", None)),
        check_vma=False,
    )
```

```python
import functools

import jax
import jax.numpy as jnp
from jax import lax
from jax.experimental import pallas as pl
from jax.experimental.pallas import tpu as pltpu
from jax.sharding import PartitionSpec as P

STEPS = 2
ETA = 0.5
DELTA = 1.0
ROWS = 16
LANES = 128
PARTS = 3
F32 = jnp.float32
BF16 = jnp.bfloat16


def round_up(value, unit):
    return -(-value // unit) * unit


def divisor(value, most):
    return max(k for k in range(1, most + 1) if value % k == 0)


def pair_routes(axis):
    count = lax.axis_size(axis)
    routes = []
    for first in (0, 1):
        pairs = [(k, k + 1) for k in range(first, count - 1, 2)]
        routes.append(pairs + [(b, a) for a, b in pairs])
    return routes


def rims_kernel(even_ref, coeffs_ref, observed_ref, near_ref, far_ref, seen_ref, sems):
    modes, height = coeffs_ref.shape[1:3]
    ext = near_ref.shape[2]
    even = even_ref[0]
    near_at = pl.multiple_of(even * (height - ext), ROWS)
    far_at = pl.multiple_of((1 - even) * (height - ext), ROWS)
    copies = []
    for side, (start, out_ref) in enumerate(((near_at, near_ref), (far_at, far_ref))):
        copies.append(
            pltpu.make_async_copy(observed_ref.at[:, pl.ds(start, ext), :], seen_ref.at[side], sems.at[2 * side])
        )
        copies.append(
            pltpu.make_async_copy(
                coeffs_ref.at[:, :, pl.ds(start, ext), :], out_ref.at[:, pl.ds(0, modes)], sems.at[2 * side + 1]
            )
        )
    for copy in copies:
        copy.start()
    for side, out_ref in enumerate((near_ref, far_ref)):
        copies[2 * side].wait()
        rest = seen_ref[side]
        for part in range(PARTS):
            piece = rest.astype(BF16)
            out_ref[:, modes + part] = piece
            rest = rest - piece.astype(F32)
    copies[1].wait()
    copies[3].wait()


def prep_kernel(owners_ref, offset_ref, vert_ref, horiz_ref, ids_ref, counted_ref, taps_ref, *, per_tile):
    modes, taps = vert_ref.shape
    taps_ref[...] = jnp.zeros(taps_ref.shape, F32)
    taps_ref[0, :modes, :taps] = vert_ref[...].astype(F32)
    taps_ref[1, :modes, :taps] = horiz_ref[...].astype(F32)
    turn = lax.broadcasted_iota(jnp.int32, (LANES, LANES), 0) + lax.broadcasted_iota(jnp.int32, (LANES, LANES), 1)
    taps_ref[2] = jnp.dot(
        taps_ref[0].astype(BF16), (turn == taps - 1).astype(F32).astype(BF16), preferred_element_type=F32
    )
    counted_ref[...] = jnp.zeros(counted_ref.shape, F32)
    pieces, rows, cols = offset_ref.shape
    for piece in range(pieces):
        for row in range(rows):
            for col in range(cols):
                index = owners_ref[piece, row, col, 0] * per_tile + offset_ref[piece, row, col]
                ids_ref[(piece * rows + row) * cols + col] = index
                counted_ref[pl.ds(index, 1), :] += 1.0


def picture_kernel(even_ref, ids_ref, tiles_ref, picture_ref, near_ref, far_ref, wide_ref, *, patch):
    pieces, height, breadth = picture_ref.shape
    rim = near_ref.shape[1]
    patch_rows, patch_cols = patch
    wide_ref[...] = tiles_ref[...].astype(F32)
    cols = breadth // patch_cols
    rows = height // patch_rows
    together = ROWS // patch_rows
    for piece in range(pieces):
        for row in range(0, rows, together):
            for col in range(cols):
                parts = []
                for inner in range(row, row + together):
                    index = ids_ref[(piece * rows + inner) * cols + col]
                    start = pl.multiple_of(index * patch_rows, patch_rows)
                    parts.append(wide_ref[pl.ds(start, patch_rows), :])
                picture_ref[
                    piece, row * patch_rows : (row + together) * patch_rows, col * patch_cols : (col + 1) * patch_cols
                ] = jnp.concatenate(parts, axis=0).astype(BF16)
    even = even_ref[0]
    near_ref[...] = picture_ref[:, pl.ds(pl.multiple_of(even * (height - rim), ROWS), rim), :]
    far_ref[...] = picture_ref[:, pl.ds(pl.multiple_of((1 - even) * (height - rim), ROWS), rim), :]


def windows_of(block, width, stride):
    count = max(1, (block.shape[1] - width) // stride + 1)
    return [block[:, k * stride : k * stride + width] for k in range(count)]


def joined(outs, width, stride):
    if len(outs) == 1:
        return [outs[0][:, k : k + stride] for k in range(0, width, stride)]
    lane = lax.broadcasted_iota(jnp.int32, (outs[0].shape[0], stride), 1)
    blocks = [outs[0][:, :stride]]
    for left, right in zip(outs[:-1], outs[1:]):
        blocks.append(jnp.where(lane < stride // 2, left[:, stride:], right[:, :stride]))
    blocks.append(outs[-1][:, stride:])
    return blocks


def lags(rows, cols, shift):
    return (
        lax.broadcasted_iota(jnp.int32, (rows, cols), 1) - lax.broadcasted_iota(jnp.int32, (rows, cols), 0) + shift
    )


def within(lag, taps):
    return ((lag >= 0) & (lag < taps)).astype(F32)


def ring_of(row, shift):
    turned = pltpu.roll(jnp.broadcast_to(row, (8, LANES)), (-shift) % LANES, 1)
    return pltpu.roll(jnp.broadcast_to(turned[:1], (LANES, LANES)), 0, 1, stride=1, stride_axis=0)


def tiled(ring, rows, cols):
    across = jnp.concatenate([ring] * (-(-cols // LANES)), axis=1)[:, :cols]
    return jnp.concatenate([across] * (-(-rows // LANES)), axis=0)[:rows]


def step_kernel(
    even_ref, ids_ref, picture_ref, near_ref, far_ref, counted_ref, taps_ref, coeffs_any, rims_near_any,
    rims_far_any, observed_any, *refs, patch, per_tile, slot, taps, with_clipped,
):
    refs = list(refs)
    clipped_ref = refs.pop(0) if with_clipped else None
    (
        sums_ref, image_ref, field_ref, model_ref, gradient_ref, coeffs_ref, seen_ref, seen_rims_ref,
        vertical_ref, side_ref, across_ref, band_ref, sems,
    ) = refs
    pieces, height, breadth = picture_ref.shape
    modes = coeffs_ref.shape[1]
    rim = near_ref.shape[1]
    tall = coeffs_ref.shape[2]
    ext = (tall - height) // 2
    margin = (taps - 1) // 2
    patch_rows, patch_cols = patch
    width = across_ref.shape[1]
    stride = patch_cols
    even = even_ref[0]
    near_at = pl.multiple_of(even * (ext + height), ROWS)
    far_at = pl.multiple_of((1 - even) * (ext + height), ROWS)

    moves = [
        (coeffs_any, coeffs_ref.at[:, :, pl.ds(ext, height), :]),
        (rims_near_any.at[:, pl.ds(0, modes)], coeffs_ref.at[:, :, pl.ds(near_at, ext), :]),
        (rims_far_any.at[:, pl.ds(0, modes)], coeffs_ref.at[:, :, pl.ds(far_at, ext), :]),
        (observed_any, seen_ref.at[:, pl.ds(ext, height), :]),
        (rims_near_any.at[:, pl.ds(modes, PARTS)], seen_rims_ref.at[0]),
        (rims_far_any.at[:, pl.ds(modes, PARTS)], seen_rims_ref.at[1]),
    ]
    copies = [pltpu.make_async_copy(source, target, sems.at[k]) for k, (source, target) in enumerate(moves)]
    for copy in copies:
        copy.start()

    image_ref[:, rim : rim + height, :] = picture_ref[...]
    image_ref[:, pl.ds(pl.multiple_of(even * (rim + height), ROWS), rim), :] = near_ref[...]
    image_ref[:, pl.ds(pl.multiple_of((1 - even) * (rim + height), ROWS), rim), :] = far_ref[...]

    reach = vertical_ref.shape[1]
    band_ref[...] = within(lags(width, width, margin), taps)
    skew = margin + ext - rim
    inside = within(lags(tall, reach, skew), taps)
    for mode in range(modes):
        ring = ring_of(taps_ref[0, mode : mode + 1], skew)
        vertical_ref[mode * tall : (mode + 1) * tall, :] = (tiled(ring, tall, reach) * inside).astype(BF16)

    group = divisor(modes, 4)
    chunk = group * tall
    for start in range(0, modes * tall, chunk):
        table = vertical_ref[start : start + chunk, :]
        for piece in range(pieces):
            for low in range(0, breadth, width):
                field_ref[piece, start : start + chunk, low : low + width] = jnp.dot(
                    table, image_ref[piece, :, low : low + width], preferred_element_type=F32
                ).astype(BF16)

    def blur(blocks, table, side):
        cuts = [cut for block in blocks for cut in windows_of(block, width, stride)]
        result = lax.dot_general(
            jnp.concatenate(cuts, axis=0), table, (((1,), (side,)), ((), ())), preferred_element_type=F32
        )
        per = len(cuts) // len(blocks)
        outs = [result[k * tall : (k + 1) * tall] for k in range(len(cuts))]
        return [joined(outs[k * per : (k + 1) * per], width, stride) for k in range(len(blocks))]

    for k in range(3):
        copies[k].wait()
    for mode in range(modes):
        start = mode * tall
        across_ref[mode] = (tiled(ring_of(taps_ref[1, mode : mode + 1], margin), width, width) * band_ref[...]).astype(BF16)
        blocks = [field_ref[piece, start : start + tall, :] for piece in range(pieces)]
        for piece, columns in enumerate(blur(blocks, across_ref[mode], 1)):
            weight = coeffs_ref[piece, mode].astype(F32)
            for k, column in enumerate(columns):
                place = slice(k * stride, (k + 1) * stride)
                if mode == 0:
                    model_ref[piece, :, place] = weight[:, place] * column
                else:
                    model_ref[piece, :, place] += weight[:, place] * column
    for k in range(3, 6):
        copies[k].wait()
    for side, start in enumerate((near_at, far_at)):
        total = seen_rims_ref[side, :, 0].astype(F32)
        for part in range(1, PARTS):
            total = total + seen_rims_ref[side, :, part].astype(F32)
        seen_ref[:, pl.ds(start, ext), :] = total
    model_ref[...] = jnp.clip(model_ref[...] - seen_ref[...], -DELTA, DELTA)
    if with_clipped:
        clipped_ref[...] = model_ref[:, ext : ext + height, :]

    total = modes * tall
    for low in range(0, total, LANES):
        high = min(low + LANES, total)
        parts = None
        for mode in range(low // tall, (high - 1) // tall + 1):
            back = taps - 1 - (ext + margin) - mode * tall
            lag = lags(height, LANES, low + back)
            ring = tiled(ring_of(taps_ref[2, mode : mode + 1], low + back), height, LANES) * within(lag, taps)
            parts = ring if parts is None else parts + ring
        side_ref[:, low:high] = parts[:, : high - low].astype(BF16)

    for mode in range(modes):
        start = mode * tall
        blocks = [(coeffs_ref[piece, mode].astype(F32) * model_ref[piece]).astype(BF16) for piece in range(pieces)]
        for piece, columns in enumerate(blur(blocks, across_ref[mode], 0)):
            for k, column in enumerate(columns):
                field_ref[piece, start : start + tall, k * stride : (k + 1) * stride] = column.astype(BF16)
    for piece in range(pieces):
        for low in range(0, breadth, width):
            gradient_ref[piece, :, low : low + width] = jnp.dot(
                side_ref[...], field_ref[piece, :, low : low + width], preferred_element_type=F32
            )
    sums_ref[...] = jnp.zeros(sums_ref.shape, F32)
    held = per_tile * patch_rows
    if slot > held:
        for owner in range(sums_ref.shape[0] // slot):
            start = owner * slot + held
            sums_ref[start : start + per_tile, :] = counted_ref[owner * per_tile : (owner + 1) * per_tile, :]
    cols = breadth // patch_cols
    rows = height // patch_rows
    for row in range(rows):
        for col in range(cols):
            for piece in range(pieces):
                index = ids_ref[(piece * rows + row) * cols + col]
                start = index * patch_rows + (index // per_tile) * (slot - held)
                place = pl.ds(pl.multiple_of(start, patch_rows), patch_rows)
                sums_ref[place, :] += gradient_ref[
                    piece, row * patch_rows : (row + 1) * patch_rows, col * patch_cols : (col + 1) * patch_cols
                ]


def update_kernel(sky_ref, parts_ref, *refs, slot, first, last):
    refs = list(refs)
    held = sky_ref.shape[0]
    total = parts_ref[:slot, :]
    for start in range(slot, parts_ref.shape[0], slot):
        total = total + parts_ref[start : start + slot, :]
    if first:
        named = total[held:]
        repeat = held // named.shape[0]
        counts = jnp.broadcast_to(named[:, None, :], (named.shape[0], repeat, named.shape[1])).reshape(sky_ref.shape)
        refs.pop()[...] = counts
    else:
        counts = refs.pop(0)[...]
    fresh = sky_ref[...] - ETA * total[:held] / jnp.maximum(counts, 1.0)
    refs[0][...] = fresh
    if not last:
        for start in range(0, refs[1].shape[0], held):
            refs[1][start : start + held, :] = fresh.astype(BF16)


def per_device(sky_map, coeffs, observed, vert_taps, horiz_taps, owner_ids, offset):
    pieces, height, breadth = observed.shape
    modes = coeffs.shape[1]
    per_tile, patch_rows, patch_cols = sky_map.shape[1:]
    patch = (patch_rows, patch_cols)
    margin = (vert_taps.shape[1] - 1) // 2
    exp_count = lax.axis_size("exp")
    held = per_tile * patch_rows
    known = exp_count * held
    ext = round_up(margin, ROWS)
    rim = round_up(ext + margin, ROWS)
    tall = height + 2 * ext
    width = min(breadth, 2 * patch_cols)
    routes = pair_routes("sub")
    vmem = pl.BlockSpec(memory_space=pltpu.VMEM)
    smem = pl.BlockSpec(memory_space=pltpu.SMEM)
    somewhere = pl.BlockSpec(memory_space=pl.ANY)

    def exchange(block):
        return lax.all_to_all(block, "exp", split_axis=0, concat_axis=0, tiled=True)

    sky = sky_map.reshape(held, patch_cols)
    spread = jnp.broadcast_to(sky.astype(BF16)[None], (exp_count, held, patch_cols)).reshape(known, patch_cols)
    tiles = exchange(spread)
    even = (1 - lax.axis_index("sub") % 2).astype(jnp.int32).reshape(1)

    rim_shape = jax.ShapeDtypeStruct((pieces, modes + PARTS, ext, breadth), BF16)
    rims_near, rims_far = pl.pallas_call(
        rims_kernel,
        out_shape=(rim_shape, rim_shape),
        in_specs=[smem, somewhere, somewhere],
        out_specs=(vmem, vmem),
        scratch_shapes=[pltpu.VMEM((2, pieces, ext, breadth), F32), pltpu.SemaphoreType.DMA((4,))],
        compiler_params=pltpu.CompilerParams(vmem_limit_bytes=8 << 20),
        name="rims",
    )(even, coeffs, observed)
    rims_far = lax.ppermute(rims_far, "sub", routes[1])
    rims_near = lax.ppermute(rims_near, "sub", routes[0])
    ids, counted, taps = pl.pallas_call(
        functools.partial(prep_kernel, per_tile=per_tile),
        out_shape=(
            jax.ShapeDtypeStruct((offset.size,), jnp.int32),
            jax.ShapeDtypeStruct((exp_count * per_tile, patch_cols), F32),
            jax.ShapeDtypeStruct((3, round_up(modes, 8), LANES), F32),
        ),
        in_specs=[smem, smem, vmem, vmem],
        out_specs=(smem, vmem, vmem),
        compiler_params=pltpu.CompilerParams(vmem_limit_bytes=4 << 20),
        name="prep",
    )(owner_ids, offset, vert_taps, horiz_taps)

    clipped, counts = None, None
    for step in range(STEPS):
        first, last = step == 0, step + 1 == STEPS
        picture, near, far = pl.pallas_call(
            functools.partial(picture_kernel, patch=patch),
            out_shape=(
                jax.ShapeDtypeStruct((pieces, height, breadth), BF16),
                jax.ShapeDtypeStruct((pieces, rim, breadth), BF16),
                jax.ShapeDtypeStruct((pieces, rim, breadth), BF16),
            ),
            in_specs=[smem, smem, vmem],
            out_specs=(vmem, vmem, vmem),
            scratch_shapes=[pltpu.VMEM((known, patch_cols), F32)],
            compiler_params=pltpu.CompilerParams(vmem_limit_bytes=8 << 20),
            name="picture",
        )(even, ids, tiles)
        far = lax.ppermute(far, "sub", routes[1])
        near = lax.ppermute(near, "sub", routes[0])
        slot = held + (round_up(per_tile, 8) if first else 0)
        results = [jax.ShapeDtypeStruct((exp_count * slot, patch_cols), F32)]
        if last:
            results.insert(0, jax.ShapeDtypeStruct((pieces, height, breadth), F32))
        answer = pl.pallas_call(
            functools.partial(
                step_kernel, patch=patch, per_tile=per_tile, slot=slot, taps=vert_taps.shape[1], with_clipped=last
            ),
            out_shape=tuple(results),
            in_specs=[smem] * 2 + [vmem] * 5 + [somewhere] * 4,
            out_specs=(vmem,) * len(results),
            scratch_shapes=[
                pltpu.VMEM((pieces, height + 2 * rim, breadth), BF16),
                pltpu.VMEM((pieces, modes * tall, breadth), BF16),
                pltpu.VMEM((pieces, tall, breadth), F32),
                pltpu.VMEM((pieces, height, breadth), F32),
                pltpu.VMEM((pieces, modes, tall, breadth), BF16),
                pltpu.VMEM((pieces, tall, breadth), F32),
                pltpu.VMEM((2, pieces, PARTS, ext, breadth), BF16),
                pltpu.VMEM((modes * tall, height + 2 * rim), BF16),
                pltpu.VMEM((height, modes * tall), BF16),
                pltpu.VMEM((modes, width, width), BF16),
                pltpu.VMEM((width, width), F32),
                pltpu.SemaphoreType.DMA((6,)),
            ],
            compiler_params=pltpu.CompilerParams(vmem_limit_bytes=56 << 20),
            name="step",
        )(even, ids, picture, near, far, counted, taps, coeffs, rims_near, rims_far, observed)
        sums = answer[-1]
        if last:
            clipped = answer[0]
        parts = exchange(sums)
        sky_shape = jax.ShapeDtypeStruct((held, patch_cols), F32)
        results = [sky_shape]
        if not last:
            results.append(jax.ShapeDtypeStruct((known, patch_cols), BF16))
        if first:
            results.append(sky_shape)
        operands = [sky, parts] if first else [sky, parts, counts]
        answer = pl.pallas_call(
            functools.partial(update_kernel, slot=slot, first=first, last=last),
            out_shape=tuple(results),
            in_specs=[vmem] * len(operands),
            out_specs=(vmem,) * len(results),
            name="update",
        )(*operands)
        sky = answer[0]
        if first:
            counts = answer[-1]
        if not last:
            tiles = exchange(answer[1])
    return sky.reshape(sky_map.shape), clipped


def solution(mesh):
    return jax.shard_map(
        per_device,
        mesh=mesh,
        in_specs=(
            P(("exp", "sub"), None, None, None),
            P("exp", None, "sub", None),
            P("exp", "sub", None),
            P(),
            P(),
            P("exp", "sub", None, None),
            P("exp", "sub", None),
        ),
        out_specs=(P(("exp", "sub"), None, None, None), P("exp", "sub", None)),
        check_vma=False,
    )
```

```python
import functools

import jax
import jax.numpy as jnp
from jax import lax
from jax.experimental import pallas as pl
from jax.experimental.pallas import tpu as pltpu
from jax.sharding import PartitionSpec as P

STEPS = 2
ETA = 0.5
DELTA = 1.0
ROWS = 16
LANES = 128
PARTS = 3
F32 = jnp.float32
BF16 = jnp.bfloat16


def round_up(value, unit):
    return -(-value // unit) * unit


def divisor(value, most):
    return max(k for k in range(1, most + 1) if value % k == 0)


def pair_routes(axis):
    count = lax.axis_size(axis)
    routes = []
    for first in (0, 1):
        pairs = [(k, k + 1) for k in range(first, count - 1, 2)]
        routes.append(pairs + [(b, a) for a, b in pairs])
    return routes


def begin_kernel(even_ref, sky_any, coeffs_ref, observed_ref, spread_any, near_ref, far_ref, seen_ref, sky_ref, spread_ref, sems):
    modes, height = coeffs_ref.shape[1:3]
    ext = near_ref.shape[2]
    held = sky_ref.shape[0]
    even = even_ref[0]
    near_at = pl.multiple_of(even * (height - ext), ROWS)
    far_at = pl.multiple_of((1 - even) * (height - ext), ROWS)
    copies = []
    sky_copy = pltpu.make_async_copy(sky_any, sky_ref, sems.at[4])
    sky_copy.start()
    for side, (start, out_ref) in enumerate(((near_at, near_ref), (far_at, far_ref))):
        copies.append(
            pltpu.make_async_copy(observed_ref.at[:, pl.ds(start, ext), :], seen_ref.at[side], sems.at[2 * side])
        )
        copies.append(
            pltpu.make_async_copy(
                coeffs_ref.at[:, :, pl.ds(start, ext), :], out_ref.at[:, pl.ds(0, modes)], sems.at[2 * side + 1]
            )
        )
    for copy in copies:
        copy.start()
    sky_copy.wait()
    rounded = sky_ref[...].astype(BF16)
    for start in range(0, spread_ref.shape[0], held):
        spread_ref[start : start + held, :] = rounded
    spread_copy = pltpu.make_async_copy(spread_ref, spread_any, sems.at[5])
    spread_copy.start()
    for side, out_ref in enumerate((near_ref, far_ref)):
        copies[2 * side].wait()
        rest = seen_ref[side]
        for part in range(PARTS):
            piece = rest.astype(BF16)
            out_ref[:, modes + part] = piece
            rest = rest - piece.astype(F32)
    copies[1].wait()
    copies[3].wait()
    spread_copy.wait()


def prep_kernel(ids_ref, vert_any, horiz_any, counted_ref, taps_ref, vert_ref, horiz_ref, sems):
    copies = [
        pltpu.make_async_copy(vert_any, vert_ref, sems.at[0]),
        pltpu.make_async_copy(horiz_any, horiz_ref, sems.at[1]),
    ]
    for copy in copies:
        copy.start()
    modes, taps = vert_ref.shape
    counted_ref[...] = jnp.zeros(counted_ref.shape, F32)
    for place in range(ids_ref.shape[0]):
        counted_ref[pl.ds(ids_ref[place], 1), :] += 1.0
    taps_ref[...] = jnp.zeros(taps_ref.shape, F32)
    for copy in copies:
        copy.wait()
    taps_ref[0, :modes, :taps] = vert_ref[...].astype(F32)
    taps_ref[1, :modes, :taps] = horiz_ref[...].astype(F32)
    turn = lax.broadcasted_iota(jnp.int32, (LANES, LANES), 0) + lax.broadcasted_iota(jnp.int32, (LANES, LANES), 1)
    taps_ref[2] = jnp.dot(
        taps_ref[0].astype(BF16), (turn == taps - 1).astype(F32).astype(BF16), preferred_element_type=F32
    )


def picture_kernel(even_ref, ids_ref, tiles_ref, picture_ref, near_ref, far_ref, wide_ref, *, patch):
    pieces, height, breadth = picture_ref.shape
    rim = near_ref.shape[1]
    patch_rows, patch_cols = patch
    wide_ref[...] = tiles_ref[...].astype(F32)
    cols = breadth // patch_cols
    rows = height // patch_rows
    together = ROWS // patch_rows
    for piece in range(pieces):
        for row in range(0, rows, together):
            for col in range(cols):
                parts = []
                for inner in range(row, row + together):
                    index = ids_ref[(piece * rows + inner) * cols + col]
                    start = pl.multiple_of(index * patch_rows, patch_rows)
                    parts.append(wide_ref[pl.ds(start, patch_rows), :])
                picture_ref[
                    piece, row * patch_rows : (row + together) * patch_rows, col * patch_cols : (col + 1) * patch_cols
                ] = jnp.concatenate(parts, axis=0).astype(BF16)
    even = even_ref[0]
    near_ref[...] = picture_ref[:, pl.ds(pl.multiple_of(even * (height - rim), ROWS), rim), :]
    far_ref[...] = picture_ref[:, pl.ds(pl.multiple_of((1 - even) * (height - rim), ROWS), rim), :]


def windows_of(block, width, stride):
    count = max(1, (block.shape[1] - width) // stride + 1)
    return [block[:, k * stride : k * stride + width] for k in range(count)]


def joined(outs, width, stride):
    if len(outs) == 1:
        return [outs[0][:, k : k + stride] for k in range(0, width, stride)]
    lane = lax.broadcasted_iota(jnp.int32, (outs[0].shape[0], stride), 1)
    blocks = [outs[0][:, :stride]]
    for left, right in zip(outs[:-1], outs[1:]):
        blocks.append(jnp.where(lane < stride // 2, left[:, stride:], right[:, :stride]))
    blocks.append(outs[-1][:, stride:])
    return blocks


def lags(rows, cols, shift):
    return (
        lax.broadcasted_iota(jnp.int32, (rows, cols), 1) - lax.broadcasted_iota(jnp.int32, (rows, cols), 0) + shift
    )


def within(lag, taps):
    return ((lag >= 0) & (lag < taps)).astype(F32)


def ring_of(row, shift):
    turned = pltpu.roll(jnp.broadcast_to(row, (8, LANES)), (-shift) % LANES, 1)
    return pltpu.roll(jnp.broadcast_to(turned[:1], (LANES, LANES)), 0, 1, stride=1, stride_axis=0)


def tiled(ring, rows, cols):
    across = jnp.concatenate([ring] * (-(-cols // LANES)), axis=1)[:, :cols]
    return jnp.concatenate([across] * (-(-rows // LANES)), axis=0)[:rows]


def step_kernel(
    even_ref, ids_ref, picture_ref, near_ref, far_ref, counted_ref, taps_ref, coeffs_any, rims_near_any,
    rims_far_any, observed_any, *refs, patch, per_tile, slot, taps, with_clipped,
):
    refs = list(refs)
    clipped_ref = refs.pop(0) if with_clipped else None
    (
        sums_ref, image_ref, field_ref, model_ref, gradient_ref, coeffs_ref, seen_ref, seen_rims_ref,
        vertical_ref, side_ref, across_ref, band_ref, sems, *totals,
    ) = refs
    pieces, height, breadth = picture_ref.shape
    modes = coeffs_ref.shape[1]
    rim = near_ref.shape[1]
    tall = coeffs_ref.shape[2]
    ext = (tall - height) // 2
    margin = (taps - 1) // 2
    patch_rows, patch_cols = patch
    width = across_ref.shape[1]
    stride = patch_cols
    even = even_ref[0]
    near_at = pl.multiple_of(even * (ext + height), ROWS)
    far_at = pl.multiple_of((1 - even) * (ext + height), ROWS)

    moves = [
        (coeffs_any, coeffs_ref.at[:, :, pl.ds(ext, height), :]),
        (rims_near_any.at[:, pl.ds(0, modes)], coeffs_ref.at[:, :, pl.ds(near_at, ext), :]),
        (rims_far_any.at[:, pl.ds(0, modes)], coeffs_ref.at[:, :, pl.ds(far_at, ext), :]),
        (observed_any, seen_ref.at[:, pl.ds(ext, height), :]),
        (rims_near_any.at[:, pl.ds(modes, PARTS)], seen_rims_ref.at[0]),
        (rims_far_any.at[:, pl.ds(modes, PARTS)], seen_rims_ref.at[1]),
    ]
    copies = [pltpu.make_async_copy(source, target, sems.at[k]) for k, (source, target) in enumerate(moves)]
    for copy in copies:
        copy.start()

    image_ref[:, rim : rim + height, :] = picture_ref[...]
    image_ref[:, pl.ds(pl.multiple_of(even * (rim + height), ROWS), rim), :] = near_ref[...]
    image_ref[:, pl.ds(pl.multiple_of((1 - even) * (rim + height), ROWS), rim), :] = far_ref[...]

    reach = vertical_ref.shape[1]
    band_ref[...] = within(lags(width, width, margin), taps)
    skew = margin + ext - rim
    inside = within(lags(tall, reach, skew), taps)
    for mode in range(modes):
        ring = ring_of(taps_ref[0, mode : mode + 1], skew)
        vertical_ref[mode * tall : (mode + 1) * tall, :] = (tiled(ring, tall, reach) * inside).astype(BF16)

    group = divisor(modes, 4)
    chunk = group * tall
    for start in range(0, modes * tall, chunk):
        table = vertical_ref[start : start + chunk, :]
        for piece in range(pieces):
            for low in range(0, breadth, width):
                field_ref[piece, start : start + chunk, low : low + width] = jnp.dot(
                    table, image_ref[piece, :, low : low + width], preferred_element_type=F32
                ).astype(BF16)

    def blur(blocks, table, side):
        cuts = [cut for block in blocks for cut in windows_of(block, width, stride)]
        result = lax.dot_general(
            jnp.concatenate(cuts, axis=0), table, (((1,), (side,)), ((), ())), preferred_element_type=F32
        )
        per = len(cuts) // len(blocks)
        outs = [result[k * tall : (k + 1) * tall] for k in range(len(cuts))]
        return [joined(outs[k * per : (k + 1) * per], width, stride) for k in range(len(blocks))]

    for k in range(3):
        copies[k].wait()
    for mode in range(modes):
        start = mode * tall
        across_ref[mode] = (tiled(ring_of(taps_ref[1, mode : mode + 1], margin), width, width) * band_ref[...]).astype(BF16)
        blocks = [field_ref[piece, start : start + tall, :] for piece in range(pieces)]
        for piece, columns in enumerate(blur(blocks, across_ref[mode], 1)):
            weight = coeffs_ref[piece, mode].astype(F32)
            for k, column in enumerate(columns):
                place = slice(k * stride, (k + 1) * stride)
                if mode == 0:
                    model_ref[piece, :, place] = weight[:, place] * column
                else:
                    model_ref[piece, :, place] += weight[:, place] * column
    for k in range(3, 6):
        copies[k].wait()
    for side, start in enumerate((near_at, far_at)):
        total = seen_rims_ref[side, :, 0].astype(F32)
        for part in range(1, PARTS):
            total = total + seen_rims_ref[side, :, part].astype(F32)
        seen_ref[:, pl.ds(start, ext), :] = total
    model_ref[...] = jnp.clip(model_ref[...] - seen_ref[...], -DELTA, DELTA)
    if with_clipped:
        clipped_ref[...] = model_ref[:, ext : ext + height, :]

    total = modes * tall
    for low in range(0, total, LANES):
        high = min(low + LANES, total)
        parts = None
        for mode in range(low // tall, (high - 1) // tall + 1):
            back = taps - 1 - (ext + margin) - mode * tall
            lag = lags(height, LANES, low + back)
            ring = tiled(ring_of(taps_ref[2, mode : mode + 1], low + back), height, LANES) * within(lag, taps)
            parts = ring if parts is None else parts + ring
        side_ref[:, low:high] = parts[:, : high - low].astype(BF16)

    for mode in range(modes):
        start = mode * tall
        blocks = [(coeffs_ref[piece, mode].astype(F32) * model_ref[piece]).astype(BF16) for piece in range(pieces)]
        for piece, columns in enumerate(blur(blocks, across_ref[mode], 0)):
            for k, column in enumerate(columns):
                field_ref[piece, start : start + tall, k * stride : (k + 1) * stride] = column.astype(BF16)
    for piece in range(pieces):
        for low in range(0, breadth, width):
            gradient_ref[piece, :, low : low + width] = jnp.dot(
                side_ref[...], field_ref[piece, :, low : low + width], preferred_element_type=F32
            )
    held = per_tile * patch_rows
    for total_ref in totals:
        total_ref[...] = jnp.zeros(total_ref.shape, F32)
    cols = breadth // patch_cols
    rows = height // patch_rows
    turn = 0
    for row in range(rows):
        for col in range(cols):
            for piece in range(pieces):
                index = ids_ref[(piece * rows + row) * cols + col]
                place = pl.ds(pl.multiple_of(index * patch_rows, patch_rows), patch_rows)
                totals[turn % len(totals)][place, :] += gradient_ref[
                    piece, row * patch_rows : (row + 1) * patch_rows, col * patch_cols : (col + 1) * patch_cols
                ]
                turn += 1
    for owner in range(sums_ref.shape[0] // slot):
        place = slice(owner * held, (owner + 1) * held)
        total = totals[0][place, :]
        for total_ref in totals[1:]:
            total = total + total_ref[place, :]
        sums_ref[owner * slot : owner * slot + held, :] = total.astype(sums_ref.dtype)
        if slot > held:
            named = counted_ref[owner * per_tile : (owner + 1) * per_tile, :]
            sums_ref[owner * slot + held : owner * slot + held + per_tile, :] = named.astype(sums_ref.dtype)


def update_kernel(sky_ref, parts_ref, *refs, slot, first, last):
    refs = list(refs)
    held = sky_ref.shape[0]
    total = parts_ref[:slot, :].astype(F32)
    for start in range(slot, parts_ref.shape[0], slot):
        total = total + parts_ref[start : start + slot, :].astype(F32)
    if first:
        named = total[held:]
        repeat = held // named.shape[0]
        counts = jnp.broadcast_to(named[:, None, :], (named.shape[0], repeat, named.shape[1])).reshape(sky_ref.shape)
        refs.pop()[...] = counts
    else:
        counts = refs.pop(0)[...]
    fresh = sky_ref[...] - ETA * total[:held] / jnp.maximum(counts, 1.0)
    refs[0][...] = fresh
    if not last:
        for start in range(0, refs[1].shape[0], held):
            refs[1][start : start + held, :] = fresh.astype(BF16)


def per_device(sky_map, coeffs, observed, vert_taps, horiz_taps, owner_ids, offset):
    pieces, height, breadth = observed.shape
    modes = coeffs.shape[1]
    per_tile, patch_rows, patch_cols = sky_map.shape[1:]
    patch = (patch_rows, patch_cols)
    margin = (vert_taps.shape[1] - 1) // 2
    exp_count = lax.axis_size("exp")
    held = per_tile * patch_rows
    known = exp_count * held
    ext = round_up(margin, ROWS)
    rim = round_up(ext + margin, ROWS)
    tall = height + 2 * ext
    width = min(breadth, 2 * patch_cols)
    routes = pair_routes("sub")
    vmem = pl.BlockSpec(memory_space=pltpu.VMEM)
    smem = pl.BlockSpec(memory_space=pltpu.SMEM)
    somewhere = pl.BlockSpec(memory_space=pl.ANY)

    def exchange(block):
        return lax.all_to_all(block, "exp", split_axis=0, concat_axis=0, tiled=True)

    sky = pltpu.with_memory_space_constraint(sky_map.reshape(held, patch_cols), pltpu.HBM)
    even = (1 - lax.axis_index("sub") % 2).astype(jnp.int32).reshape(1)
    coeffs = pltpu.with_memory_space_constraint(coeffs, pltpu.HBM)
    observed = pltpu.with_memory_space_constraint(observed, pltpu.HBM)
    rim_shape = jax.ShapeDtypeStruct((pieces, modes + PARTS, ext, breadth), BF16)
    spread, rims_near, rims_far = pl.pallas_call(
        begin_kernel,
        out_shape=(jax.ShapeDtypeStruct((known, patch_cols), BF16), rim_shape, rim_shape),
        in_specs=[smem, somewhere, somewhere, somewhere],
        out_specs=(somewhere, vmem, vmem),
        scratch_shapes=[
            pltpu.VMEM((2, pieces, ext, breadth), F32),
            pltpu.VMEM((held, patch_cols), F32),
            pltpu.VMEM((known, patch_cols), BF16),
            pltpu.SemaphoreType.DMA((6,)),
        ],
        compiler_params=pltpu.CompilerParams(vmem_limit_bytes=8 << 20),
        name="begin",
    )(even, sky, coeffs, observed)
    tiles = exchange(spread)
    ids = (owner_ids.reshape(offset.shape) * per_tile + offset).reshape(-1)
    counted, taps = pl.pallas_call(
        prep_kernel,
        out_shape=(
            jax.ShapeDtypeStruct((exp_count * per_tile, patch_cols), F32),
            jax.ShapeDtypeStruct((3, round_up(modes, 8), LANES), F32),
        ),
        in_specs=[smem, somewhere, somewhere],
        out_specs=(vmem, vmem),
        scratch_shapes=[
            pltpu.VMEM(vert_taps.shape, BF16),
            pltpu.VMEM(horiz_taps.shape, BF16),
            pltpu.SemaphoreType.DMA((2,)),
        ],
        compiler_params=pltpu.CompilerParams(vmem_limit_bytes=4 << 20),
        name="prep",
    )(
        ids,
        pltpu.with_memory_space_constraint(vert_taps, pltpu.HBM),
        pltpu.with_memory_space_constraint(horiz_taps, pltpu.HBM),
    )
    rims_far = lax.ppermute(rims_far, "sub", routes[1])
    rims_near = lax.ppermute(rims_near, "sub", routes[0])
    ids, counted, taps = lax.optimization_barrier((ids, counted, taps))

    clipped, counts = None, None
    for step in range(STEPS):
        first, last = step == 0, step + 1 == STEPS
        picture, near, far = pl.pallas_call(
            functools.partial(picture_kernel, patch=patch),
            out_shape=(
                jax.ShapeDtypeStruct((pieces, height, breadth), BF16),
                jax.ShapeDtypeStruct((pieces, rim, breadth), BF16),
                jax.ShapeDtypeStruct((pieces, rim, breadth), BF16),
            ),
            in_specs=[smem, smem, vmem],
            out_specs=(vmem, vmem, vmem),
            scratch_shapes=[pltpu.VMEM((known, patch_cols), F32)],
            compiler_params=pltpu.CompilerParams(vmem_limit_bytes=8 << 20),
            name="picture",
        )(even, ids, tiles)
        far = lax.ppermute(far, "sub", routes[1])
        near = lax.ppermute(near, "sub", routes[0])
        slot = held + (round_up(per_tile, 8) if first else 0)
        results = [jax.ShapeDtypeStruct((exp_count * slot, patch_cols), F32)]
        if last:
            results.insert(0, jax.ShapeDtypeStruct((pieces, height, breadth), F32))
        answer = pl.pallas_call(
            functools.partial(
                step_kernel, patch=patch, per_tile=per_tile, slot=slot, taps=vert_taps.shape[1], with_clipped=last
            ),
            out_shape=tuple(results),
            in_specs=[smem] * 2 + [vmem] * 5 + [somewhere] * 4,
            out_specs=(vmem,) * len(results),
            scratch_shapes=[
                pltpu.VMEM((pieces, height + 2 * rim, breadth), BF16),
                pltpu.VMEM((pieces, modes * tall, breadth), BF16),
                pltpu.VMEM((pieces, tall, breadth), F32),
                pltpu.VMEM((pieces, height, breadth), F32),
                pltpu.VMEM((pieces, modes, tall, breadth), BF16),
                pltpu.VMEM((pieces, tall, breadth), F32),
                pltpu.VMEM((2, pieces, PARTS, ext, breadth), BF16),
                pltpu.VMEM((modes * tall, height + 2 * rim), BF16),
                pltpu.VMEM((height, modes * tall), BF16),
                pltpu.VMEM((modes, width, width), BF16),
                pltpu.VMEM((width, width), F32),
                pltpu.SemaphoreType.DMA((6,)),
            ]
            + [pltpu.VMEM((known, patch_cols), F32)] * 4,
            compiler_params=pltpu.CompilerParams(vmem_limit_bytes=24 << 20),
            name="step",
        )(even, ids, picture, near, far, counted, taps, coeffs, rims_near, rims_far, observed)
        sums = answer[-1]
        if last:
            clipped = answer[0]
        parts = exchange(sums)
        sky_shape = jax.ShapeDtypeStruct((held, patch_cols), F32)
        results = [sky_shape]
        if not last:
            results.append(jax.ShapeDtypeStruct((known, patch_cols), BF16))
        if first:
            results.append(sky_shape)
        operands = [sky, parts] if first else [sky, parts, counts]
        answer = pl.pallas_call(
            functools.partial(update_kernel, slot=slot, first=first, last=last),
            out_shape=tuple(results),
            in_specs=[vmem] * len(operands),
            out_specs=(vmem,) * len(results),
            compiler_params=pltpu.CompilerParams(vmem_limit_bytes=4 << 20),
            name="update",
        )(*operands)
        sky = answer[0]
        if first:
            counts = answer[-1]
        if not last:
            tiles = exchange(answer[1])
    return sky.reshape(sky_map.shape), clipped


def solution(mesh):
    return jax.shard_map(
        per_device,
        mesh=mesh,
        in_specs=(
            P(("exp", "sub"), None, None, None),
            P("exp", None, "sub", None),
            P("exp", "sub", None),
            P(),
            P(),
            P("exp", "sub", None, None),
            P("exp", "sub", None),
        ),
        out_specs=(P(("exp", "sub"), None, None, None), P("exp", "sub", None)),
        check_vma=False,
    )
```

```python
import functools

import jax
import jax.numpy as jnp
from jax import lax
from jax.experimental import pallas as pl
from jax.experimental.pallas import tpu as pltpu
from jax.sharding import PartitionSpec as P

STEPS = 2
ETA = 0.5
DELTA = 1.0
ROWS = 16
LANES = 128
PARTS = 3
F32 = jnp.float32
BF16 = jnp.bfloat16


def round_up(value, unit):
    return -(-value // unit) * unit


def divisor(value, most):
    return max(k for k in range(1, most + 1) if value % k == 0)


def pair_routes(axis):
    count = lax.axis_size(axis)
    routes = []
    for first in (0, 1):
        pairs = [(k, k + 1) for k in range(first, count - 1, 2)]
        routes.append(pairs + [(b, a) for a, b in pairs])
    return routes


def begin_kernel(even_ref, sky_any, coeffs_ref, observed_ref, spread_any, near_ref, far_ref, seen_ref, sky_ref, spread_ref, sems):
    modes, height = coeffs_ref.shape[1:3]
    ext = near_ref.shape[2]
    held = sky_ref.shape[0]
    even = even_ref[0]
    near_at = pl.multiple_of(even * (height - ext), ROWS)
    far_at = pl.multiple_of((1 - even) * (height - ext), ROWS)
    copies = []
    sky_copy = pltpu.make_async_copy(sky_any, sky_ref, sems.at[4])
    sky_copy.start()
    for side, (start, out_ref) in enumerate(((near_at, near_ref), (far_at, far_ref))):
        copies.append(
            pltpu.make_async_copy(observed_ref.at[:, pl.ds(start, ext), :], seen_ref.at[side], sems.at[2 * side])
        )
        copies.append(
            pltpu.make_async_copy(
                coeffs_ref.at[:, :, pl.ds(start, ext), :], out_ref.at[:, pl.ds(0, modes)], sems.at[2 * side + 1]
            )
        )
    for copy in copies:
        copy.start()
    sky_copy.wait()
    rounded = sky_ref[...].astype(BF16)
    for start in range(0, spread_ref.shape[0], held):
        spread_ref[start : start + held, :] = rounded
    spread_copy = pltpu.make_async_copy(spread_ref, spread_any, sems.at[5])
    spread_copy.start()
    for side, out_ref in enumerate((near_ref, far_ref)):
        copies[2 * side].wait()
        rest = seen_ref[side]
        for part in range(PARTS):
            piece = rest.astype(BF16)
            out_ref[:, modes + part] = piece
            rest = rest - piece.astype(F32)
    copies[1].wait()
    copies[3].wait()
    spread_copy.wait()


def prep_kernel(ids_ref, vert_any, horiz_any, counted_ref, taps_ref, vert_ref, horiz_ref, sems):
    copies = [
        pltpu.make_async_copy(vert_any, vert_ref, sems.at[0]),
        pltpu.make_async_copy(horiz_any, horiz_ref, sems.at[1]),
    ]
    for copy in copies:
        copy.start()
    modes, taps = vert_ref.shape
    counted_ref[...] = jnp.zeros(counted_ref.shape, F32)
    for place in range(ids_ref.shape[0]):
        counted_ref[pl.ds(ids_ref[place], 1), :] += 1.0
    taps_ref[...] = jnp.zeros(taps_ref.shape, F32)
    for copy in copies:
        copy.wait()
    taps_ref[0, :modes, :taps] = vert_ref[...].astype(F32)
    taps_ref[1, :modes, :taps] = horiz_ref[...].astype(F32)
    turn = lax.broadcasted_iota(jnp.int32, (LANES, LANES), 0) + lax.broadcasted_iota(jnp.int32, (LANES, LANES), 1)
    taps_ref[2] = jnp.dot(
        taps_ref[0].astype(BF16), (turn == taps - 1).astype(F32).astype(BF16), preferred_element_type=F32
    )


def picture_kernel(even_ref, ids_ref, tiles_ref, picture_ref, near_ref, far_ref, wide_ref, *, patch):
    pieces, height, breadth = picture_ref.shape
    rim = near_ref.shape[1]
    patch_rows, patch_cols = patch
    wide_ref[...] = tiles_ref[...].astype(F32)
    cols = breadth // patch_cols
    rows = height // patch_rows
    together = ROWS // patch_rows
    for piece in range(pieces):
        for row in range(0, rows, together):
            for col in range(cols):
                parts = []
                for inner in range(row, row + together):
                    index = ids_ref[(piece * rows + inner) * cols + col]
                    start = pl.multiple_of(index * patch_rows, patch_rows)
                    parts.append(wide_ref[pl.ds(start, patch_rows), :])
                picture_ref[
                    piece, row * patch_rows : (row + together) * patch_rows, col * patch_cols : (col + 1) * patch_cols
                ] = jnp.concatenate(parts, axis=0).astype(BF16)
    even = even_ref[0]
    near_ref[...] = picture_ref[:, pl.ds(pl.multiple_of(even * (height - rim), ROWS), rim), :]
    far_ref[...] = picture_ref[:, pl.ds(pl.multiple_of((1 - even) * (height - rim), ROWS), rim), :]


def windows_of(block, width, stride):
    count = max(1, (block.shape[1] - width) // stride + 1)
    return [block[:, k * stride : k * stride + width] for k in range(count)]


def joined(outs, width, stride):
    if len(outs) == 1:
        return [outs[0][:, k : k + stride] for k in range(0, width, stride)]
    lane = lax.broadcasted_iota(jnp.int32, (outs[0].shape[0], stride), 1)
    blocks = [outs[0][:, :stride]]
    for left, right in zip(outs[:-1], outs[1:]):
        blocks.append(jnp.where(lane < stride // 2, left[:, stride:], right[:, :stride]))
    blocks.append(outs[-1][:, stride:])
    return blocks


def lags(rows, cols, shift):
    return (
        lax.broadcasted_iota(jnp.int32, (rows, cols), 1) - lax.broadcasted_iota(jnp.int32, (rows, cols), 0) + shift
    )


def within(lag, taps):
    return ((lag >= 0) & (lag < taps)).astype(F32)


def ring_of(row, shift):
    turned = pltpu.roll(jnp.broadcast_to(row, (8, LANES)), (-shift) % LANES, 1)
    return pltpu.roll(jnp.broadcast_to(turned[:1], (LANES, LANES)), 0, 1, stride=1, stride_axis=0)


def tiled(ring, rows, cols):
    across = jnp.concatenate([ring] * (-(-cols // LANES)), axis=1)[:, :cols]
    return jnp.concatenate([across] * (-(-rows // LANES)), axis=0)[:rows]


def step_kernel(
    even_ref, ids_ref, picture_ref, near_ref, far_ref, counted_ref, taps_ref, coeffs_any, rims_near_any,
    rims_far_any, observed_any, *refs, patch, per_tile, slot, taps, with_clipped,
):
    refs = list(refs)
    clipped_ref = refs.pop(0) if with_clipped else None
    (
        sums_ref, image_ref, field_ref, model_ref, gradient_ref, coeffs_ref, seen_ref, seen_rims_ref,
        vertical_ref, side_ref, across_ref, band_ref, sems, *totals,
    ) = refs
    pieces, height, breadth = picture_ref.shape
    modes = coeffs_ref.shape[1]
    rim = near_ref.shape[1]
    tall = coeffs_ref.shape[2]
    ext = (tall - height) // 2
    margin = (taps - 1) // 2
    patch_rows, patch_cols = patch
    width = across_ref.shape[1]
    stride = patch_cols
    even = even_ref[0]
    near_at = pl.multiple_of(even * (ext + height), ROWS)
    far_at = pl.multiple_of((1 - even) * (ext + height), ROWS)

    moves = [
        (coeffs_any, coeffs_ref.at[:, :, pl.ds(ext, height), :]),
        (rims_near_any.at[:, pl.ds(0, modes)], coeffs_ref.at[:, :, pl.ds(near_at, ext), :]),
        (rims_far_any.at[:, pl.ds(0, modes)], coeffs_ref.at[:, :, pl.ds(far_at, ext), :]),
        (observed_any, seen_ref.at[:, pl.ds(ext, height), :]),
        (rims_near_any.at[:, pl.ds(modes, PARTS)], seen_rims_ref.at[0]),
        (rims_far_any.at[:, pl.ds(modes, PARTS)], seen_rims_ref.at[1]),
    ]
    copies = [pltpu.make_async_copy(source, target, sems.at[k]) for k, (source, target) in enumerate(moves)]
    for copy in copies:
        copy.start()

    image_ref[:, rim : rim + height, :] = picture_ref[...]
    image_ref[:, pl.ds(pl.multiple_of(even * (rim + height), ROWS), rim), :] = near_ref[...]
    image_ref[:, pl.ds(pl.multiple_of((1 - even) * (rim + height), ROWS), rim), :] = far_ref[...]

    reach = vertical_ref.shape[1]
    band_ref[...] = within(lags(width, width, margin), taps)
    skew = margin + ext - rim
    inside = within(lags(tall, reach, skew), taps)
    for mode in range(modes):
        ring = ring_of(taps_ref[0, mode : mode + 1], skew)
        vertical_ref[mode * tall : (mode + 1) * tall, :] = (tiled(ring, tall, reach) * inside).astype(BF16)

    group = divisor(modes, 4)
    chunk = group * tall
    for start in range(0, modes * tall, chunk):
        table = vertical_ref[start : start + chunk, :]
        for piece in range(pieces):
            for low in range(0, breadth, width):
                field_ref[piece, start : start + chunk, low : low + width] = jnp.dot(
                    table, image_ref[piece, :, low : low + width], preferred_element_type=F32
                ).astype(BF16)

    def blur(blocks, table, side):
        cuts = [cut for block in blocks for cut in windows_of(block, width, stride)]
        result = lax.dot_general(
            jnp.concatenate(cuts, axis=0), table, (((1,), (side,)), ((), ())), preferred_element_type=F32
        )
        per = len(cuts) // len(blocks)
        outs = [result[k * tall : (k + 1) * tall] for k in range(len(cuts))]
        return [joined(outs[k * per : (k + 1) * per], width, stride) for k in range(len(blocks))]

    for k in range(3):
        copies[k].wait()
    for mode in range(modes):
        start = mode * tall
        across_ref[mode] = (tiled(ring_of(taps_ref[1, mode : mode + 1], margin), width, width) * band_ref[...]).astype(BF16)
        blocks = [field_ref[piece, start : start + tall, :] for piece in range(pieces)]
        for piece, columns in enumerate(blur(blocks, across_ref[mode], 1)):
            weight = coeffs_ref[piece, mode].astype(F32)
            for k, column in enumerate(columns):
                place = slice(k * stride, (k + 1) * stride)
                if mode == 0:
                    model_ref[piece, :, place] = weight[:, place] * column
                else:
                    model_ref[piece, :, place] += weight[:, place] * column
    for k in range(3, 6):
        copies[k].wait()
    for side, start in enumerate((near_at, far_at)):
        total = seen_rims_ref[side, :, 0].astype(F32)
        for part in range(1, PARTS):
            total = total + seen_rims_ref[side, :, part].astype(F32)
        seen_ref[:, pl.ds(start, ext), :] = total
    model_ref[...] = jnp.clip(model_ref[...] - seen_ref[...], -DELTA, DELTA)
    if with_clipped:
        clipped_ref[...] = model_ref[:, ext : ext + height, :]

    total = modes * tall
    for low in range(0, total, LANES):
        high = min(low + LANES, total)
        parts = None
        for mode in range(low // tall, (high - 1) // tall + 1):
            back = taps - 1 - (ext + margin) - mode * tall
            lag = lags(height, LANES, low + back)
            ring = tiled(ring_of(taps_ref[2, mode : mode + 1], low + back), height, LANES) * within(lag, taps)
            parts = ring if parts is None else parts + ring
        side_ref[:, low:high] = parts[:, : high - low].astype(BF16)

    for mode in range(modes):
        start = mode * tall
        blocks = [(coeffs_ref[piece, mode].astype(F32) * model_ref[piece]).astype(BF16) for piece in range(pieces)]
        for piece, columns in enumerate(blur(blocks, across_ref[mode], 0)):
            for k, column in enumerate(columns):
                field_ref[piece, start : start + tall, k * stride : (k + 1) * stride] = column.astype(BF16)
    for piece in range(pieces):
        for low in range(0, breadth, width):
            gradient_ref[piece, :, low : low + width] = jnp.dot(
                side_ref[...], field_ref[piece, :, low : low + width], preferred_element_type=F32
            )
    held = per_tile * patch_rows
    for total_ref in totals:
        total_ref[...] = jnp.zeros(total_ref.shape, F32)
    cols = breadth // patch_cols
    rows = height // patch_rows
    turn = 0
    for row in range(rows):
        for col in range(cols):
            for piece in range(pieces):
                index = ids_ref[(piece * rows + row) * cols + col]
                place = pl.ds(pl.multiple_of(index * patch_rows, patch_rows), patch_rows)
                totals[turn % len(totals)][place, :] += gradient_ref[
                    piece, row * patch_rows : (row + 1) * patch_rows, col * patch_cols : (col + 1) * patch_cols
                ]
                turn += 1
    for owner in range(sums_ref.shape[0] // slot):
        place = slice(owner * held, (owner + 1) * held)
        total = totals[0][place, :]
        for total_ref in totals[1:]:
            total = total + total_ref[place, :]
        sums_ref[owner * slot : owner * slot + held, :] = total.astype(sums_ref.dtype)
        if slot > held:
            named = counted_ref[owner * per_tile : (owner + 1) * per_tile, :]
            spare = jnp.zeros((slot - held - per_tile, named.shape[1]), F32)
            sums_ref[owner * slot + held : (owner + 1) * slot, :] = jnp.concatenate([named, spare], axis=0).astype(
                sums_ref.dtype
            )


def update_kernel(sky_ref, parts_ref, *refs, per_tile, slot, first, last):
    refs = list(refs)
    held = sky_ref.shape[0]
    total = parts_ref[:slot, :].astype(F32)
    for start in range(slot, parts_ref.shape[0], slot):
        total = total + parts_ref[start : start + slot, :].astype(F32)
    if first:
        named = total[held : held + per_tile]
        repeat = held // per_tile
        counts = jnp.broadcast_to(named[:, None, :], (named.shape[0], repeat, named.shape[1])).reshape(sky_ref.shape)
        refs.pop()[...] = counts
    else:
        counts = refs.pop(0)[...]
    fresh = sky_ref[...] - ETA * total[:held] / jnp.maximum(counts, 1.0)
    refs[0][...] = fresh
    if not last:
        for start in range(0, refs[1].shape[0], held):
            refs[1][start : start + held, :] = fresh.astype(BF16)


def per_device(sky_map, coeffs, observed, vert_taps, horiz_taps, owner_ids, offset):
    pieces, height, breadth = observed.shape
    modes = coeffs.shape[1]
    per_tile, patch_rows, patch_cols = sky_map.shape[1:]
    patch = (patch_rows, patch_cols)
    margin = (vert_taps.shape[1] - 1) // 2
    exp_count = lax.axis_size("exp")
    held = per_tile * patch_rows
    known = exp_count * held
    ext = round_up(margin, ROWS)
    rim = round_up(ext + margin, ROWS)
    tall = height + 2 * ext
    width = min(breadth, 2 * patch_cols)
    routes = pair_routes("sub")
    vmem = pl.BlockSpec(memory_space=pltpu.VMEM)
    smem = pl.BlockSpec(memory_space=pltpu.SMEM)
    somewhere = pl.BlockSpec(memory_space=pl.ANY)

    def exchange(block):
        return lax.all_to_all(block, "exp", split_axis=0, concat_axis=0, tiled=True)

    sky = pltpu.with_memory_space_constraint(sky_map.reshape(held, patch_cols), pltpu.HBM)
    even = (1 - lax.axis_index("sub") % 2).astype(jnp.int32).reshape(1)
    coeffs = pltpu.with_memory_space_constraint(coeffs, pltpu.HBM)
    observed = pltpu.with_memory_space_constraint(observed, pltpu.HBM)
    rim_shape = jax.ShapeDtypeStruct((pieces, modes + PARTS, ext, breadth), BF16)
    spread, rims_near, rims_far = pl.pallas_call(
        begin_kernel,
        out_shape=(jax.ShapeDtypeStruct((known, patch_cols), BF16), rim_shape, rim_shape),
        in_specs=[smem, somewhere, somewhere, somewhere],
        out_specs=(somewhere, vmem, vmem),
        scratch_shapes=[
            pltpu.VMEM((2, pieces, ext, breadth), F32),
            pltpu.VMEM((held, patch_cols), F32),
            pltpu.VMEM((known, patch_cols), BF16),
            pltpu.SemaphoreType.DMA((6,)),
        ],
        compiler_params=pltpu.CompilerParams(vmem_limit_bytes=8 << 20),
        name="begin",
    )(even, sky, coeffs, observed)
    tiles = exchange(spread)
    ids = (owner_ids.reshape(offset.shape) * per_tile + offset).reshape(-1)
    counted, taps = pl.pallas_call(
        prep_kernel,
        out_shape=(
            jax.ShapeDtypeStruct((exp_count * per_tile, patch_cols), F32),
            jax.ShapeDtypeStruct((3, round_up(modes, 8), LANES), F32),
        ),
        in_specs=[smem, somewhere, somewhere],
        out_specs=(vmem, vmem),
        scratch_shapes=[
            pltpu.VMEM(vert_taps.shape, BF16),
            pltpu.VMEM(horiz_taps.shape, BF16),
            pltpu.SemaphoreType.DMA((2,)),
        ],
        compiler_params=pltpu.CompilerParams(vmem_limit_bytes=4 << 20),
        name="prep",
    )(
        ids,
        pltpu.with_memory_space_constraint(vert_taps, pltpu.HBM),
        pltpu.with_memory_space_constraint(horiz_taps, pltpu.HBM),
    )
    rims_far = lax.ppermute(rims_far, "sub", routes[1])
    rims_near = lax.ppermute(rims_near, "sub", routes[0])
    ids, counted, taps = lax.optimization_barrier((ids, counted, taps))

    clipped, counts = None, None
    for step in range(STEPS):
        first, last = step == 0, step + 1 == STEPS
        picture, near, far = pl.pallas_call(
            functools.partial(picture_kernel, patch=patch),
            out_shape=(
                jax.ShapeDtypeStruct((pieces, height, breadth), BF16),
                jax.ShapeDtypeStruct((pieces, rim, breadth), BF16),
                jax.ShapeDtypeStruct((pieces, rim, breadth), BF16),
            ),
            in_specs=[smem, smem, vmem],
            out_specs=(vmem, vmem, vmem),
            scratch_shapes=[pltpu.VMEM((known, patch_cols), F32)],
            compiler_params=pltpu.CompilerParams(vmem_limit_bytes=8 << 20),
            name="picture",
        )(even, ids, tiles)
        far = lax.ppermute(far, "sub", routes[1])
        near = lax.ppermute(near, "sub", routes[0])
        slot = held + (round_up(per_tile, ROWS) if first else 0)
        results = [jax.ShapeDtypeStruct((exp_count * slot, patch_cols), BF16)]
        if last:
            results.insert(0, jax.ShapeDtypeStruct((pieces, height, breadth), F32))
        answer = pl.pallas_call(
            functools.partial(
                step_kernel, patch=patch, per_tile=per_tile, slot=slot, taps=vert_taps.shape[1], with_clipped=last
            ),
            out_shape=tuple(results),
            in_specs=[smem] * 2 + [vmem] * 5 + [somewhere] * 4,
            out_specs=(vmem,) * len(results),
            scratch_shapes=[
                pltpu.VMEM((pieces, height + 2 * rim, breadth), BF16),
                pltpu.VMEM((pieces, modes * tall, breadth), BF16),
                pltpu.VMEM((pieces, tall, breadth), F32),
                pltpu.VMEM((pieces, height, breadth), F32),
                pltpu.VMEM((pieces, modes, tall, breadth), BF16),
                pltpu.VMEM((pieces, tall, breadth), F32),
                pltpu.VMEM((2, pieces, PARTS, ext, breadth), BF16),
                pltpu.VMEM((modes * tall, height + 2 * rim), BF16),
                pltpu.VMEM((height, modes * tall), BF16),
                pltpu.VMEM((modes, width, width), BF16),
                pltpu.VMEM((width, width), F32),
                pltpu.SemaphoreType.DMA((6,)),
            ]
            + [pltpu.VMEM((known, patch_cols), F32)] * 4,
            compiler_params=pltpu.CompilerParams(vmem_limit_bytes=24 << 20),
            name="step",
        )(even, ids, picture, near, far, counted, taps, coeffs, rims_near, rims_far, observed)
        sums = answer[-1]
        if last:
            clipped = answer[0]
        parts = exchange(sums)
        sky_shape = jax.ShapeDtypeStruct((held, patch_cols), F32)
        results = [sky_shape]
        if not last:
            results.append(jax.ShapeDtypeStruct((known, patch_cols), BF16))
        if first:
            results.append(sky_shape)
        operands = [sky, parts] if first else [sky, parts, counts]
        answer = pl.pallas_call(
            functools.partial(update_kernel, per_tile=per_tile, slot=slot, first=first, last=last),
            out_shape=tuple(results),
            in_specs=[vmem] * len(operands),
            out_specs=(vmem,) * len(results),
            compiler_params=pltpu.CompilerParams(vmem_limit_bytes=4 << 20),
            name="update",
        )(*operands)
        sky = answer[0]
        if first:
            counts = answer[-1]
        if not last:
            tiles = exchange(answer[1])
    return sky.reshape(sky_map.shape), clipped


def solution(mesh):
    return jax.shard_map(
        per_device,
        mesh=mesh,
        in_specs=(
            P(("exp", "sub"), None, None, None),
            P("exp", None, "sub", None),
            P("exp", "sub", None),
            P(),
            P(),
            P("exp", "sub", None, None),
            P("exp", "sub", None),
        ),
        out_specs=(P(("exp", "sub"), None, None, None), P("exp", "sub", None)),
        check_vma=False,
    )
```

```python
import functools

import jax
import jax.numpy as jnp
from jax import lax
from jax.experimental import pallas as pl
from jax.experimental.pallas import tpu as pltpu
from jax.sharding import PartitionSpec as P

STEPS = 2
ETA = 0.5
DELTA = 1.0
ROWS = 16
LANES = 128
PARTS = 3
F32 = jnp.float32
BF16 = jnp.bfloat16


def round_up(value, unit):
    return -(-value // unit) * unit


def divisor(value, most):
    return max(k for k in range(1, most + 1) if value % k == 0)


def pair_routes(axis):
    count = lax.axis_size(axis)
    routes = []
    for first in (0, 1):
        pairs = [(k, k + 1) for k in range(first, count - 1, 2)]
        routes.append(pairs + [(b, a) for a, b in pairs])
    return routes


def begin_kernel(even_ref, sky_any, coeffs_ref, observed_ref, spread_any, near_ref, far_ref, seen_ref, sky_ref, spread_ref, sems):
    modes, height = coeffs_ref.shape[1:3]
    ext = near_ref.shape[2]
    held = sky_ref.shape[0]
    even = even_ref[0]
    near_at = pl.multiple_of(even * (height - ext), ROWS)
    far_at = pl.multiple_of((1 - even) * (height - ext), ROWS)
    copies = []
    sky_copy = pltpu.make_async_copy(sky_any, sky_ref, sems.at[4])
    sky_copy.start()
    for side, (start, out_ref) in enumerate(((near_at, near_ref), (far_at, far_ref))):
        copies.append(
            pltpu.make_async_copy(observed_ref.at[:, pl.ds(start, ext), :], seen_ref.at[side], sems.at[2 * side])
        )
        copies.append(
            pltpu.make_async_copy(
                coeffs_ref.at[:, :, pl.ds(start, ext), :], out_ref.at[:, pl.ds(0, modes)], sems.at[2 * side + 1]
            )
        )
    for copy in copies:
        copy.start()
    sky_copy.wait()
    rounded = sky_ref[...].astype(BF16)
    for start in range(0, spread_ref.shape[0], held):
        spread_ref[start : start + held, :] = rounded
    spread_copy = pltpu.make_async_copy(spread_ref, spread_any, sems.at[5])
    spread_copy.start()
    for side, out_ref in enumerate((near_ref, far_ref)):
        copies[2 * side].wait()
        rest = seen_ref[side]
        for part in range(PARTS):
            piece = rest.astype(BF16)
            out_ref[:, modes + part] = piece
            rest = rest - piece.astype(F32)
    copies[1].wait()
    copies[3].wait()
    spread_copy.wait()


def prep_kernel(ids_ref, vert_any, horiz_any, counted_ref, taps_ref, vert_ref, horiz_ref, sems):
    copies = [
        pltpu.make_async_copy(vert_any, vert_ref, sems.at[0]),
        pltpu.make_async_copy(horiz_any, horiz_ref, sems.at[1]),
    ]
    for copy in copies:
        copy.start()
    modes, taps = vert_ref.shape
    counted_ref[...] = jnp.zeros(counted_ref.shape, F32)
    for place in range(ids_ref.shape[0]):
        counted_ref[pl.ds(ids_ref[place], 1), :] += 1.0
    taps_ref[...] = jnp.zeros(taps_ref.shape, F32)
    for copy in copies:
        copy.wait()
    taps_ref[0, :modes, :taps] = vert_ref[...].astype(F32)
    taps_ref[1, :modes, :taps] = horiz_ref[...].astype(F32)
    turn = lax.broadcasted_iota(jnp.int32, (LANES, LANES), 0) + lax.broadcasted_iota(jnp.int32, (LANES, LANES), 1)
    taps_ref[2] = jnp.dot(
        taps_ref[0].astype(BF16), (turn == taps - 1).astype(F32).astype(BF16), preferred_element_type=F32
    )


def picture_kernel(even_ref, ids_ref, tiles_ref, picture_ref, near_ref, far_ref, wide_ref, *, patch):
    pieces, height, breadth = picture_ref.shape
    rim = near_ref.shape[1]
    patch_rows, patch_cols = patch
    wide_ref[...] = tiles_ref[...].astype(F32)
    cols = breadth // patch_cols
    rows = height // patch_rows
    together = ROWS // patch_rows
    for piece in range(pieces):
        for row in range(0, rows, together):
            for col in range(cols):
                parts = []
                for inner in range(row, row + together):
                    index = ids_ref[(piece * rows + inner) * cols + col]
                    start = pl.multiple_of(index * patch_rows, patch_rows)
                    parts.append(wide_ref[pl.ds(start, patch_rows), :])
                picture_ref[
                    piece, row * patch_rows : (row + together) * patch_rows, col * patch_cols : (col + 1) * patch_cols
                ] = jnp.concatenate(parts, axis=0).astype(BF16)
    even = even_ref[0]
    near_ref[...] = picture_ref[:, pl.ds(pl.multiple_of(even * (height - rim), ROWS), rim), :]
    far_ref[...] = picture_ref[:, pl.ds(pl.multiple_of((1 - even) * (height - rim), ROWS), rim), :]


def windows_of(block, width, stride):
    count = max(1, (block.shape[1] - width) // stride + 1)
    return [block[:, k * stride : k * stride + width] for k in range(count)]


def joined(outs, width, stride):
    if len(outs) == 1:
        return [outs[0][:, k : k + stride] for k in range(0, width, stride)]
    lane = lax.broadcasted_iota(jnp.int32, (outs[0].shape[0], stride), 1)
    blocks = [outs[0][:, :stride]]
    for left, right in zip(outs[:-1], outs[1:]):
        blocks.append(jnp.where(lane < stride // 2, left[:, stride:], right[:, :stride]))
    blocks.append(outs[-1][:, stride:])
    return blocks


def lags(rows, cols, shift):
    return (
        lax.broadcasted_iota(jnp.int32, (rows, cols), 1) - lax.broadcasted_iota(jnp.int32, (rows, cols), 0) + shift
    )


def within(lag, taps):
    return ((lag >= 0) & (lag < taps)).astype(F32)


def ring_of(row, shift):
    turned = pltpu.roll(jnp.broadcast_to(row, (8, LANES)), (-shift) % LANES, 1)
    return pltpu.roll(jnp.broadcast_to(turned[:1], (LANES, LANES)), 0, 1, stride=1, stride_axis=0)


def tiled(ring, rows, cols):
    across = jnp.concatenate([ring] * (-(-cols // LANES)), axis=1)[:, :cols]
    return jnp.concatenate([across] * (-(-rows // LANES)), axis=0)[:rows]


def build_side(side_ref, taps_ref, modes, tall, shift, taps):
    height = side_ref.shape[0]
    total = modes * tall
    for low in range(0, total, LANES):
        high = min(low + LANES, total)
        parts = None
        for mode in range(low // tall, (high - 1) // tall + 1):
            back = low + taps - 1 - shift - mode * tall
            ring = tiled(ring_of(taps_ref[2, mode : mode + 1], back), height, LANES)
            place = lax.broadcasted_iota(jnp.int32, (height, LANES), 1) + (low - mode * tall)
            ring = jnp.where((place >= 0) & (place < tall), ring * within(lags(height, LANES, back), taps), 0.0)
            parts = ring if parts is None else parts + ring
        side_ref[:, low:high] = parts[:, : high - low].astype(BF16)


def smooth(images, vertical_ref, field_ref, taps_ref, modes, skew, taps, width):
    tall, reach = vertical_ref.shape[0] // modes, vertical_ref.shape[1]
    inside = within(lags(tall, reach, skew), taps)
    for mode in range(modes):
        ring = ring_of(taps_ref[0, mode : mode + 1], skew)
        vertical_ref[mode * tall : (mode + 1) * tall, :] = (tiled(ring, tall, reach) * inside).astype(BF16)
    chunk = divisor(modes, 4) * tall
    for start in range(0, modes * tall, chunk):
        table = vertical_ref[start : start + chunk, :]
        for block, image in enumerate(images):
            for low in range(0, image.shape[1], width):
                field_ref[block, start : start + chunk, low : low + width] = jnp.dot(
                    table, image[:, low : low + width], preferred_element_type=F32
                ).astype(BF16)


def blur(blocks, table, side, stride):
    tall, width = blocks[0].shape[0], table.shape[0]
    cuts = [cut for block in blocks for cut in windows_of(block, width, stride)]
    result = lax.dot_general(
        jnp.concatenate(cuts, axis=0), table, (((1,), (side,)), ((), ())), preferred_element_type=F32
    )
    per = len(cuts) // len(blocks)
    outs = [result[k * tall : (k + 1) * tall] for k in range(len(cuts))]
    return [joined(outs[k * per : (k + 1) * per], width, stride) for k in range(len(blocks))]


def model_all(field_ref, model_ref, weights, across_of, modes, stride):
    tall = model_ref.shape[1]
    count = model_ref.shape[0]
    for mode in range(modes):
        start = mode * tall
        blocks = [field_ref[block, start : start + tall, :] for block in range(count)]
        for block, columns in enumerate(blur(blocks, across_of(mode), 1, stride)):
            weight = weights(block, mode).astype(F32)
            for k, column in enumerate(columns):
                place = slice(k * stride, (k + 1) * stride)
                if mode == 0:
                    model_ref[block, :, place] = weight[:, place] * column
                else:
                    model_ref[block, :, place] += weight[:, place] * column


def adjoint_all(field_ref, model_ref, weights, across_ref, modes, stride):
    tall = model_ref.shape[1]
    count = model_ref.shape[0]
    for mode in range(modes):
        start = mode * tall
        blocks = [(weights(block, mode).astype(F32) * model_ref[block]).astype(BF16) for block in range(count)]
        for block, columns in enumerate(blur(blocks, across_ref[mode], 0, stride)):
            for k, column in enumerate(columns):
                field_ref[block, start : start + tall, k * stride : (k + 1) * stride] = column.astype(BF16)


def inner_kernel(
    even_ref, picture_ref, taps_ref, coeffs_any, observed_any, rims_near_any, rims_far_any, gradient_ref, across_ref,
    edge_coeffs_ref, edge_seen_ref, *refs, patch, taps, with_clipped,
):
    refs = list(refs)
    clipped_ref = refs.pop(0) if with_clipped else None
    field_ref, model_ref, coeffs_ref, seen_ref, seen_rims_ref, vertical_ref, side_ref, band_ref, sems = refs
    pieces, height, breadth = picture_ref.shape
    modes = coeffs_ref.shape[1]
    tall = coeffs_ref.shape[2]
    ext = (height - tall) // 2
    margin = (taps - 1) // 2
    stride = patch[1]
    width = across_ref.shape[1]
    even = even_ref[0]
    near_row = pl.multiple_of(even * ext, ROWS)
    far_row = pl.multiple_of((1 - even) * ext, ROWS)

    moves = [
        (coeffs_any.at[:, :, pl.ds(ext, tall), :], coeffs_ref),
        (observed_any.at[:, pl.ds(ext, tall), :], seen_ref),
        (coeffs_any.at[:, :, pl.ds(0, ext), :], edge_coeffs_ref.at[0, :, :, pl.ds(ext, ext), :]),
        (coeffs_any.at[:, :, pl.ds(height - ext, ext), :], edge_coeffs_ref.at[1, :, :, pl.ds(0, ext), :]),
        (rims_near_any.at[:, pl.ds(0, modes)], edge_coeffs_ref.at[even, :, :, pl.ds(near_row, ext), :]),
        (rims_far_any.at[:, pl.ds(0, modes)], edge_coeffs_ref.at[1 - even, :, :, pl.ds(far_row, ext), :]),
        (observed_any.at[:, pl.ds(0, ext), :], edge_seen_ref.at[0, :, pl.ds(ext, ext), :]),
        (observed_any.at[:, pl.ds(height - ext, ext), :], edge_seen_ref.at[1, :, pl.ds(0, ext), :]),
        (rims_near_any.at[:, pl.ds(modes, PARTS)], seen_rims_ref.at[0]),
        (rims_far_any.at[:, pl.ds(modes, PARTS)], seen_rims_ref.at[1]),
    ]
    copies = [pltpu.make_async_copy(source, target, sems.at[k]) for k, (source, target) in enumerate(moves)]
    for copy in copies:
        copy.start()

    band_ref[...] = within(lags(width, width, margin), taps)
    images = [picture_ref.at[piece] for piece in range(pieces)]
    smooth(images, vertical_ref, field_ref, taps_ref, modes, margin - ext, taps, width)

    def across_of(mode):
        ring = tiled(ring_of(taps_ref[1, mode : mode + 1], margin), width, width)
        across_ref[mode] = (ring * band_ref[...]).astype(BF16)
        return across_ref[mode]

    def weights(block, mode):
        return coeffs_ref[block, mode]

    copies[0].wait()
    copies[1].wait()
    model_all(field_ref, model_ref, weights, across_of, modes, stride)
    model_ref[...] = jnp.clip(model_ref[...] - seen_ref[...], -DELTA, DELTA)
    if with_clipped:
        clipped_ref[...] = model_ref[...]
    build_side(side_ref, taps_ref, modes, tall, margin - ext, taps)
    adjoint_all(field_ref, model_ref, weights, across_ref, modes, stride)
    for piece in range(pieces):
        for low in range(0, breadth, width):
            gradient_ref[piece, :, low : low + width] = jnp.dot(
                side_ref[...], field_ref[piece, :, low : low + width], preferred_element_type=F32
            )
    for copy in copies[2:]:
        copy.wait()
    for rim, end, row in ((0, even, near_row), (1, 1 - even, far_row)):
        total = seen_rims_ref[rim, :, 0].astype(F32)
        for part in range(1, PARTS):
            total = total + seen_rims_ref[rim, :, part].astype(F32)
        edge_seen_ref[end, :, pl.ds(row, ext), :] = total


def outer_kernel(
    even_ref, ids_ref, picture_ref, near_ref, far_ref, counted_ref, taps_ref, gradient_ref, across_ref,
    edge_coeffs_ref, edge_seen_ref, *refs, patch, per_tile, slot, taps, with_clipped,
):
    refs = list(refs)
    if with_clipped:
        inner_ref, clipped_ref = refs[:2]
        refs = refs[2:]
    sums_ref, image_ref, field_ref, model_ref, edge_ref, vertical_ref, upper_ref, lower_ref, *totals = refs
    pieces, height, breadth = picture_ref.shape
    modes, tall = edge_coeffs_ref.shape[2:4]
    rim = near_ref.shape[1]
    ext = tall // 2
    margin = (taps - 1) // 2
    patch_rows, patch_cols = patch
    stride = patch_cols
    width = across_ref.shape[1]
    even = even_ref[0]
    near_row = pl.multiple_of(even * rim, ROWS)
    far_row = pl.multiple_of((1 - even) * rim, ROWS)

    image_ref[0, :, rim:, :] = picture_ref[:, :rim, :]
    image_ref[1, :, :rim, :] = picture_ref[:, height - rim :, :]
    image_ref[even, :, pl.ds(near_row, rim), :] = near_ref[...]
    image_ref[1 - even, :, pl.ds(far_row, rim), :] = far_ref[...]
    places = [(end, piece) for end in (0, 1) for piece in range(pieces)]
    images = [image_ref.at[end, piece] for end, piece in places]
    smooth(images, vertical_ref, field_ref, taps_ref, modes, margin + ext - rim, taps, width)

    def weights(block, mode):
        end, piece = places[block]
        return edge_coeffs_ref[end, piece, mode]

    model_all(field_ref, model_ref, weights, lambda mode: across_ref[mode], modes, stride)
    for block, (end, piece) in enumerate(places):
        model_ref[block] = jnp.clip(model_ref[block] - edge_seen_ref[end, piece], -DELTA, DELTA)
    if with_clipped:
        for piece in range(pieces):
            clipped_ref[piece, :ext, :] = model_ref[piece, ext:, :]
            clipped_ref[piece, ext : height - ext, :] = inner_ref[piece]
            clipped_ref[piece, height - ext :, :] = model_ref[pieces + piece, :ext, :]
    build_side(upper_ref, taps_ref, modes, tall, margin + ext, taps)
    build_side(lower_ref, taps_ref, modes, tall, margin + ext - rim, taps)
    adjoint_all(field_ref, model_ref, weights, across_ref, modes, stride)
    for block, (end, piece) in enumerate(places):
        side = (upper_ref, lower_ref)[end][...]
        for low in range(0, breadth, width):
            edge_ref[end, piece, :, low : low + width] = jnp.dot(
                side, field_ref[block, :, low : low + width], preferred_element_type=F32
            )

    held = per_tile * patch_rows
    for total_ref in totals:
        total_ref[...] = jnp.zeros(total_ref.shape, F32)
    cols = breadth // patch_cols
    rows = height // patch_rows
    turn = 0
    for row in range(rows):
        top = row * patch_rows
        for col in range(cols):
            across = slice(col * patch_cols, (col + 1) * patch_cols)
            for piece in range(pieces):
                index = ids_ref[(piece * rows + row) * cols + col]
                place = pl.ds(pl.multiple_of(index * patch_rows, patch_rows), patch_rows)
                value = gradient_ref[piece, top : top + patch_rows, across]
                if top < rim:
                    value = value + edge_ref[0, piece, top : top + patch_rows, across]
                if top >= height - rim:
                    start = top - (height - rim)
                    value = value + edge_ref[1, piece, start : start + patch_rows, across]
                totals[turn % len(totals)][place, :] += value
                turn += 1
    for owner in range(sums_ref.shape[0] // slot):
        place = slice(owner * held, (owner + 1) * held)
        total = totals[0][place, :]
        for total_ref in totals[1:]:
            total = total + total_ref[place, :]
        sums_ref[owner * slot : owner * slot + held, :] = total.astype(sums_ref.dtype)
        if slot > held:
            named = counted_ref[owner * per_tile : (owner + 1) * per_tile, :]
            spare = jnp.zeros((slot - held - per_tile, named.shape[1]), F32)
            sums_ref[owner * slot + held : (owner + 1) * slot, :] = jnp.concatenate([named, spare], axis=0).astype(
                sums_ref.dtype
            )


def update_kernel(sky_ref, parts_ref, *refs, per_tile, slot, first, last):
    refs = list(refs)
    held = sky_ref.shape[0]
    total = parts_ref[:slot, :].astype(F32)
    for start in range(slot, parts_ref.shape[0], slot):
        total = total + parts_ref[start : start + slot, :].astype(F32)
    if first:
        named = total[held : held + per_tile]
        repeat = held // per_tile
        counts = jnp.broadcast_to(named[:, None, :], (named.shape[0], repeat, named.shape[1])).reshape(sky_ref.shape)
        refs.pop()[...] = counts
    else:
        counts = refs.pop(0)[...]
    fresh = sky_ref[...] - ETA * total[:held] / jnp.maximum(counts, 1.0)
    refs[0][...] = fresh
    if not last:
        for start in range(0, refs[1].shape[0], held):
            refs[1][start : start + held, :] = fresh.astype(BF16)


def per_device(sky_map, coeffs, observed, vert_taps, horiz_taps, owner_ids, offset):
    pieces, height, breadth = observed.shape
    modes = coeffs.shape[1]
    per_tile, patch_rows, patch_cols = sky_map.shape[1:]
    patch = (patch_rows, patch_cols)
    margin = (vert_taps.shape[1] - 1) // 2
    exp_count = lax.axis_size("exp")
    held = per_tile * patch_rows
    known = exp_count * held
    ext = round_up(margin, ROWS)
    rim = round_up(ext + margin, ROWS)
    width = min(breadth, 2 * patch_cols)
    routes = pair_routes("sub")
    vmem = pl.BlockSpec(memory_space=pltpu.VMEM)
    smem = pl.BlockSpec(memory_space=pltpu.SMEM)
    somewhere = pl.BlockSpec(memory_space=pl.ANY)

    def exchange(block):
        return lax.all_to_all(block, "exp", split_axis=0, concat_axis=0, tiled=True)

    sky = pltpu.with_memory_space_constraint(sky_map.reshape(held, patch_cols), pltpu.HBM)
    even = (1 - lax.axis_index("sub") % 2).astype(jnp.int32).reshape(1)
    coeffs = pltpu.with_memory_space_constraint(coeffs, pltpu.HBM)
    observed = pltpu.with_memory_space_constraint(observed, pltpu.HBM)
    rim_shape = jax.ShapeDtypeStruct((pieces, modes + PARTS, ext, breadth), BF16)
    spread, rims_near, rims_far = pl.pallas_call(
        begin_kernel,
        out_shape=(jax.ShapeDtypeStruct((known, patch_cols), BF16), rim_shape, rim_shape),
        in_specs=[smem, somewhere, somewhere, somewhere],
        out_specs=(somewhere, vmem, vmem),
        scratch_shapes=[
            pltpu.VMEM((2, pieces, ext, breadth), F32),
            pltpu.VMEM((held, patch_cols), F32),
            pltpu.VMEM((known, patch_cols), BF16),
            pltpu.SemaphoreType.DMA((6,)),
        ],
        compiler_params=pltpu.CompilerParams(vmem_limit_bytes=8 << 20),
        name="begin",
    )(even, sky, coeffs, observed)
    tiles = exchange(spread)
    ids = (owner_ids.reshape(offset.shape) * per_tile + offset).reshape(-1)
    counted, taps = pl.pallas_call(
        prep_kernel,
        out_shape=(
            jax.ShapeDtypeStruct((exp_count * per_tile, patch_cols), F32),
            jax.ShapeDtypeStruct((3, round_up(modes, 8), LANES), F32),
        ),
        in_specs=[smem, somewhere, somewhere],
        out_specs=(vmem, vmem),
        scratch_shapes=[
            pltpu.VMEM(vert_taps.shape, BF16),
            pltpu.VMEM(horiz_taps.shape, BF16),
            pltpu.SemaphoreType.DMA((2,)),
        ],
        compiler_params=pltpu.CompilerParams(vmem_limit_bytes=4 << 20),
        name="prep",
    )(
        ids,
        pltpu.with_memory_space_constraint(vert_taps, pltpu.HBM),
        pltpu.with_memory_space_constraint(horiz_taps, pltpu.HBM),
    )
    rims_far = lax.ppermute(rims_far, "sub", routes[1])
    rims_near = lax.ppermute(rims_near, "sub", routes[0])
    ids, counted, taps = lax.optimization_barrier((ids, counted, taps))

    clipped, counts = None, None
    for step in range(STEPS):
        first, last = step == 0, step + 1 == STEPS
        picture, near, far = pl.pallas_call(
            functools.partial(picture_kernel, patch=patch),
            out_shape=(
                jax.ShapeDtypeStruct((pieces, height, breadth), BF16),
                jax.ShapeDtypeStruct((pieces, rim, breadth), BF16),
                jax.ShapeDtypeStruct((pieces, rim, breadth), BF16),
            ),
            in_specs=[smem, smem, vmem],
            out_specs=(vmem, vmem, vmem),
            scratch_shapes=[pltpu.VMEM((known, patch_cols), F32)],
            compiler_params=pltpu.CompilerParams(vmem_limit_bytes=8 << 20),
            name="picture",
        )(even, ids, tiles)
        far = lax.ppermute(far, "sub", routes[1])
        near = lax.ppermute(near, "sub", routes[0])
        slot = held + (round_up(per_tile, ROWS) if first else 0)
        inner = height - 2 * ext
        taken = vert_taps.shape[1]
        results = [
            pltpu.VMEM((pieces, height, breadth), F32),
            pltpu.VMEM((modes, width, width), BF16),
            pltpu.VMEM((2, pieces, modes, 2 * ext, breadth), BF16),
            pltpu.VMEM((2, pieces, 2 * ext, breadth), F32),
        ]
        if last:
            results.append(pltpu.VMEM((pieces, inner, breadth), F32))
        middle = pl.pallas_call(
            functools.partial(inner_kernel, patch=patch, taps=taken, with_clipped=last),
            out_shape=tuple(results),
            in_specs=[smem, vmem, vmem] + [somewhere] * 4,
            out_specs=(vmem,) * len(results),
            scratch_shapes=[
                pltpu.VMEM((pieces, modes * inner, breadth), BF16),
                pltpu.VMEM((pieces, inner, breadth), F32),
                pltpu.VMEM((pieces, modes, inner, breadth), BF16),
                pltpu.VMEM((pieces, inner, breadth), F32),
                pltpu.VMEM((2, pieces, PARTS, ext, breadth), BF16),
                pltpu.VMEM((modes * inner, height), BF16),
                pltpu.VMEM((height, modes * inner), BF16),
                pltpu.VMEM((width, width), F32),
                pltpu.SemaphoreType.DMA((10,)),
            ],
            compiler_params=pltpu.CompilerParams(vmem_limit_bytes=16 << 20),
            cost_estimate=pl.CostEstimate(flops=3 * 10**9, bytes_accessed=5 * 10**6, transcendentals=0),
            name="inner",
        )(even, picture, taps, coeffs, observed, rims_near, rims_far)
        results = [jax.ShapeDtypeStruct((exp_count * slot, patch_cols), BF16)]
        if last:
            results.insert(0, jax.ShapeDtypeStruct((pieces, height, breadth), F32))
        held_here = [pltpu.with_memory_space_constraint(array, pltpu.VMEM) for array in middle]
        answer = pl.pallas_call(
            functools.partial(outer_kernel, patch=patch, per_tile=per_tile, slot=slot, taps=taken, with_clipped=last),
            out_shape=tuple(results),
            in_specs=[smem] * 2 + [vmem] * (5 + len(middle)),
            out_specs=(vmem,) * len(results),
            scratch_shapes=[
                pltpu.VMEM((2, pieces, 2 * rim, breadth), BF16),
                pltpu.VMEM((2 * pieces, modes * 2 * ext, breadth), BF16),
                pltpu.VMEM((2 * pieces, 2 * ext, breadth), F32),
                pltpu.VMEM((2, pieces, rim, breadth), F32),
                pltpu.VMEM((modes * 2 * ext, 2 * rim), BF16),
                pltpu.VMEM((rim, modes * 2 * ext), BF16),
                pltpu.VMEM((rim, modes * 2 * ext), BF16),
            ]
            + [pltpu.VMEM((known, patch_cols), F32)] * 4,
            compiler_params=pltpu.CompilerParams(vmem_limit_bytes=12 << 20),
            name="outer",
        )(even, ids, picture, near, far, counted, taps, *held_here)
        sums = answer[-1]
        if last:
            clipped = answer[0]
        parts = exchange(sums)
        sky_shape = jax.ShapeDtypeStruct((held, patch_cols), F32)
        results = [sky_shape]
        if not last:
            results.append(jax.ShapeDtypeStruct((known, patch_cols), BF16))
        if first:
            results.append(sky_shape)
        operands = [sky, parts] if first else [sky, parts, counts]
        answer = pl.pallas_call(
            functools.partial(update_kernel, per_tile=per_tile, slot=slot, first=first, last=last),
            out_shape=tuple(results),
            in_specs=[vmem] * len(operands),
            out_specs=(vmem,) * len(results),
            compiler_params=pltpu.CompilerParams(vmem_limit_bytes=4 << 20),
            name="update",
        )(*operands)
        sky = answer[0]
        if first:
            counts = answer[-1]
        if not last:
            tiles = exchange(answer[1])
    return sky.reshape(sky_map.shape), clipped


def solution(mesh):
    return jax.shard_map(
        per_device,
        mesh=mesh,
        in_specs=(
            P(("exp", "sub"), None, None, None),
            P("exp", None, "sub", None),
            P("exp", "sub", None),
            P(),
            P(),
            P("exp", "sub", None, None),
            P("exp", "sub", None),
        ),
        out_specs=(P(("exp", "sub"), None, None, None), P("exp", "sub", None)),
        check_vma=False,
    )
```

```python
import functools

import jax
import jax.numpy as jnp
from jax import lax
from jax.experimental import pallas as pl
from jax.experimental.pallas import tpu as pltpu
from jax.sharding import PartitionSpec as P

STEPS = 2
ETA = 0.5
DELTA = 1.0
ROWS = 16
LANES = 128
PARTS = 3
F32 = jnp.float32
BF16 = jnp.bfloat16


def round_up(value, unit):
    return -(-value // unit) * unit


def divisor(value, most):
    return max(k for k in range(1, most + 1) if value % k == 0)


def pair_routes(axis):
    count = lax.axis_size(axis)
    routes = []
    for first in (0, 1):
        pairs = [(k, k + 1) for k in range(first, count - 1, 2)]
        routes.append(pairs + [(b, a) for a, b in pairs])
    return routes


def begin_kernel(even_ref, sky_any, coeffs_ref, observed_ref, spread_any, near_ref, far_ref, seen_ref, sky_ref, spread_ref, sems):
    modes, height = coeffs_ref.shape[1:3]
    ext = near_ref.shape[2]
    held = sky_ref.shape[0]
    even = even_ref[0]
    near_at = pl.multiple_of(even * (height - ext), ROWS)
    far_at = pl.multiple_of((1 - even) * (height - ext), ROWS)
    copies = []
    sky_copy = pltpu.make_async_copy(sky_any, sky_ref, sems.at[4])
    sky_copy.start()
    for side, (start, out_ref) in enumerate(((near_at, near_ref), (far_at, far_ref))):
        copies.append(
            pltpu.make_async_copy(observed_ref.at[:, pl.ds(start, ext), :], seen_ref.at[side], sems.at[2 * side])
        )
        copies.append(
            pltpu.make_async_copy(
                coeffs_ref.at[:, :, pl.ds(start, ext), :], out_ref.at[:, pl.ds(0, modes)], sems.at[2 * side + 1]
            )
        )
    for copy in copies:
        copy.start()
    sky_copy.wait()
    rounded = sky_ref[...].astype(BF16)
    for start in range(0, spread_ref.shape[0], held):
        spread_ref[start : start + held, :] = rounded
    spread_copy = pltpu.make_async_copy(spread_ref, spread_any, sems.at[5])
    spread_copy.start()
    for side, out_ref in enumerate((near_ref, far_ref)):
        copies[2 * side].wait()
        rest = seen_ref[side]
        for part in range(PARTS):
            piece = rest.astype(BF16)
            out_ref[:, modes + part] = piece
            rest = rest - piece.astype(F32)
    copies[1].wait()
    copies[3].wait()
    spread_copy.wait()


def prep_kernel(ids_ref, vert_any, horiz_any, counted_ref, taps_ref, vert_ref, horiz_ref, sems):
    copies = [
        pltpu.make_async_copy(vert_any, vert_ref, sems.at[0]),
        pltpu.make_async_copy(horiz_any, horiz_ref, sems.at[1]),
    ]
    for copy in copies:
        copy.start()
    modes, taps = vert_ref.shape
    counted_ref[...] = jnp.zeros(counted_ref.shape, F32)
    for place in range(ids_ref.shape[0]):
        counted_ref[pl.ds(ids_ref[place], 1), :] += 1.0
    taps_ref[...] = jnp.zeros(taps_ref.shape, F32)
    for copy in copies:
        copy.wait()
    taps_ref[0, :modes, :taps] = vert_ref[...].astype(F32)
    taps_ref[1, :modes, :taps] = horiz_ref[...].astype(F32)
    turn = lax.broadcasted_iota(jnp.int32, (LANES, LANES), 0) + lax.broadcasted_iota(jnp.int32, (LANES, LANES), 1)
    taps_ref[2] = jnp.dot(
        taps_ref[0].astype(BF16), (turn == taps - 1).astype(F32).astype(BF16), preferred_element_type=F32
    )


def picture_kernel(even_ref, ids_ref, tiles_ref, picture_ref, near_ref, far_ref, wide_ref, *, patch):
    pieces, height, breadth = picture_ref.shape
    rim = near_ref.shape[1]
    patch_rows, patch_cols = patch
    wide_ref[...] = tiles_ref[...].astype(F32)
    cols = breadth // patch_cols
    rows = height // patch_rows
    together = ROWS // patch_rows
    for piece in range(pieces):
        for row in range(0, rows, together):
            for col in range(cols):
                parts = []
                for inner in range(row, row + together):
                    index = ids_ref[(piece * rows + inner) * cols + col]
                    start = pl.multiple_of(index * patch_rows, patch_rows)
                    parts.append(wide_ref[pl.ds(start, patch_rows), :])
                picture_ref[
                    piece, row * patch_rows : (row + together) * patch_rows, col * patch_cols : (col + 1) * patch_cols
                ] = jnp.concatenate(parts, axis=0).astype(BF16)
    even = even_ref[0]
    near_ref[...] = picture_ref[:, pl.ds(pl.multiple_of(even * (height - rim), ROWS), rim), :]
    far_ref[...] = picture_ref[:, pl.ds(pl.multiple_of((1 - even) * (height - rim), ROWS), rim), :]


def windows_of(block, width, stride):
    count = max(1, (block.shape[1] - width) // stride + 1)
    return [block[:, k * stride : k * stride + width] for k in range(count)]


def joined(outs, width, stride):
    if len(outs) == 1:
        return [outs[0][:, k : k + stride] for k in range(0, width, stride)]
    lane = lax.broadcasted_iota(jnp.int32, (outs[0].shape[0], stride), 1)
    blocks = [outs[0][:, :stride]]
    for left, right in zip(outs[:-1], outs[1:]):
        blocks.append(jnp.where(lane < stride // 2, left[:, stride:], right[:, :stride]))
    blocks.append(outs[-1][:, stride:])
    return blocks


def lags(rows, cols, shift):
    return (
        lax.broadcasted_iota(jnp.int32, (rows, cols), 1) - lax.broadcasted_iota(jnp.int32, (rows, cols), 0) + shift
    )


def within(lag, taps):
    return ((lag >= 0) & (lag < taps)).astype(F32)


def ring_of(row, shift):
    turned = pltpu.roll(jnp.broadcast_to(row, (8, LANES)), (-shift) % LANES, 1)
    return pltpu.roll(jnp.broadcast_to(turned[:1], (LANES, LANES)), 0, 1, stride=1, stride_axis=0)


def tiled(ring, rows, cols):
    across = jnp.concatenate([ring] * (-(-cols // LANES)), axis=1)[:, :cols]
    return jnp.concatenate([across] * (-(-rows // LANES)), axis=0)[:rows]


def build_vertical(vertical_ref, taps_ref, modes, skew, taps, turned=None):
    tall, reach = vertical_ref.shape[0] // modes, vertical_ref.shape[1]
    inside = within(lags(tall, reach, skew), taps)
    for mode in range(modes):
        ring = ring_of(taps_ref[0, mode : mode + 1], skew)
        table = (tiled(ring, tall, reach) * inside).astype(BF16)
        start = mode * tall
        vertical_ref[start : start + tall, :] = table
        if turned is not None:
            turned[start : start + tall // 2, :] = table[tall // 2 :]
            turned[start + tall // 2 : start + tall, :] = table[: tall // 2]


def smooth(groups, field_ref, modes, tall, width, unroll):
    chunk = divisor(modes, 4) * tall

    def some_modes(turn, carry):
        start = pl.multiple_of(turn * chunk, ROWS)
        block = 0
        for table_ref, images in groups:
            table = table_ref[pl.ds(start, chunk), :]
            for image in images:
                for low in range(0, image.shape[1], width):
                    field_ref[block, pl.ds(start, chunk), low : low + width] = jnp.dot(
                        table, image[:, low : low + width], preferred_element_type=F32
                    ).astype(BF16)
                block += 1
        return carry

    lax.fori_loop(0, modes * tall // chunk, some_modes, 0, unroll=unroll)


def blur(blocks, table, side, stride):
    tall, width = blocks[0].shape[0], table.shape[0]
    cuts = [cut for block in blocks for cut in windows_of(block, width, stride)]
    result = lax.dot_general(
        jnp.concatenate(cuts, axis=0), table, (((1,), (side,)), ((), ())), preferred_element_type=F32
    )
    per = len(cuts) // len(blocks)
    outs = [result[k * tall : (k + 1) * tall] for k in range(len(cuts))]
    return [joined(outs[k * per : (k + 1) * per], width, stride) for k in range(len(blocks))]


def model_all(field_ref, model_ref, weights, across_of, modes, stride):
    tall = model_ref.shape[1]
    count = model_ref.shape[0]
    for mode in range(modes):
        start = mode * tall
        blocks = [field_ref[block, start : start + tall, :] for block in range(count)]
        for block, columns in enumerate(blur(blocks, across_of(mode), 1, stride)):
            weight = weights(block, mode).astype(F32)
            for k, column in enumerate(columns):
                place = slice(k * stride, (k + 1) * stride)
                if mode == 0:
                    model_ref[block, :, place] = weight[:, place] * column
                else:
                    model_ref[block, :, place] += weight[:, place] * column


def adjoint_all(field_ref, model_ref, weights, across_ref, modes, stride):
    tall = model_ref.shape[1]
    count = model_ref.shape[0]
    for mode in range(modes):
        start = mode * tall
        blocks = [(weights(block, mode).astype(F32) * model_ref[block]).astype(BF16) for block in range(count)]
        for block, columns in enumerate(blur(blocks, across_ref[mode], 0, stride)):
            for k, column in enumerate(columns):
                field_ref[block, start : start + tall, k * stride : (k + 1) * stride] = column.astype(BF16)


def gathered(table, field):
    return lax.dot_general(table, field, (((0,), (0,)), ((), ())), preferred_element_type=F32)


def inner_kernel(
    picture_ref, taps_ref, coeffs_any, observed_any, gradient_ref, across_ref, *refs, patch, taps, with_clipped,
):
    refs = list(refs)
    clipped_ref = refs.pop(0) if with_clipped else None
    field_ref, model_ref, coeffs_ref, seen_ref, vertical_ref, band_ref, sems = refs
    pieces, height, breadth = picture_ref.shape
    modes = coeffs_ref.shape[1]
    tall = coeffs_ref.shape[2]
    ext = (height - tall) // 2
    margin = (taps - 1) // 2
    stride = patch[1]
    width = across_ref.shape[1]

    moves = [
        (coeffs_any.at[:, :, pl.ds(ext, tall), :], coeffs_ref),
        (observed_any.at[:, pl.ds(ext, tall), :], seen_ref),
    ]
    copies = [pltpu.make_async_copy(source, target, sems.at[k]) for k, (source, target) in enumerate(moves)]
    for copy in copies:
        copy.start()

    band_ref[...] = within(lags(width, width, margin), taps)
    build_vertical(vertical_ref, taps_ref, modes, margin - ext, taps)
    smooth([(vertical_ref, [picture_ref.at[piece] for piece in range(pieces)])], field_ref, modes, tall, width, False)

    def across_of(mode):
        ring = tiled(ring_of(taps_ref[1, mode : mode + 1], margin), width, width)
        across_ref[mode] = (ring * band_ref[...]).astype(BF16)
        return across_ref[mode]

    def weights(block, mode):
        return coeffs_ref[block, mode]

    for copy in copies:
        copy.wait()
    model_all(field_ref, model_ref, weights, across_of, modes, stride)
    model_ref[...] = jnp.clip(model_ref[...] - seen_ref[...], -DELTA, DELTA)
    if with_clipped:
        clipped_ref[...] = model_ref[...]
    adjoint_all(field_ref, model_ref, weights, across_ref, modes, stride)
    for piece in range(pieces):
        for low in range(0, breadth, width):
            gradient_ref[piece, :, low : low + width] = gathered(vertical_ref[...], field_ref[piece, :, low : low + width])


def outer_kernel(
    even_ref, ids_ref, picture_ref, near_ref, far_ref, counted_ref, taps_ref, own_near_ref, own_far_ref,
    rims_near_ref, rims_far_ref, gradient_ref, across_ref, *refs, patch, per_tile, slot, taps, with_clipped,
):
    refs = list(refs)
    if with_clipped:
        inner_ref, clipped_ref = refs[:2]
        refs = refs[2:]
    sums_ref, image_ref, field_ref, model_ref, edge_ref, vertical_ref, *totals = refs
    pieces, height, breadth = picture_ref.shape
    modes, ext = own_near_ref.shape[1] - PARTS, own_near_ref.shape[2]
    rim = near_ref.shape[1]
    tall = 2 * ext
    margin = (taps - 1) // 2
    patch_rows, patch_cols = patch
    stride = patch_cols
    width = across_ref.shape[1]
    even = even_ref[0]
    near_row = pl.multiple_of(even * rim, ROWS)
    far_row = pl.multiple_of((1 - even) * rim, ROWS)

    image_ref[0, :, rim:, :] = picture_ref[:, :rim, :]
    image_ref[1, :, :rim, :] = picture_ref[:, height - rim :, :]
    image_ref[even, :, pl.ds(near_row, rim), :] = near_ref[...]
    image_ref[1 - even, :, pl.ds(far_row, rim), :] = far_ref[...]
    build_vertical(vertical_ref.at[0], taps_ref, modes, margin + ext - rim, taps, vertical_ref.at[1])
    ends = ((even, 1 - even, own_near_ref, rims_near_ref), (1 - even, even, own_far_ref, rims_far_ref))
    places = [(side, piece) for side in (0, 1) for piece in range(pieces)]
    groups = [
        (vertical_ref.at[order], [image_ref.at[end, piece] for piece in range(pieces)]) for end, order, *_ in ends
    ]
    smooth(groups, field_ref, modes, tall, width, True)

    def weights(block, mode):
        side, piece = places[block]
        return jnp.concatenate([ends[side][2][piece, mode], ends[side][3][piece, mode]], axis=0)

    def seen(block):
        side, piece = places[block]
        halves = []
        for rims_ref in ends[side][2:]:
            total = rims_ref[piece, modes].astype(F32)
            for part in range(1, PARTS):
                total = total + rims_ref[piece, modes + part].astype(F32)
            halves.append(total)
        return jnp.concatenate(halves, axis=0)

    model_all(field_ref, model_ref, weights, lambda mode: across_ref[mode], modes, stride)
    for block in range(len(places)):
        model_ref[block] = jnp.clip(model_ref[block] - seen(block), -DELTA, DELTA)
    if with_clipped:
        for block, (side, piece) in enumerate(places):
            start = pl.multiple_of(ends[side][0] * (height - ext), ROWS)
            clipped_ref[piece, pl.ds(start, ext), :] = model_ref[block, :ext, :]
        for piece in range(pieces):
            clipped_ref[piece, ext : height - ext, :] = inner_ref[piece]
    adjoint_all(field_ref, model_ref, weights, across_ref, modes, stride)
    for block, (side, piece) in enumerate(places):
        end, order = ends[side][:2]
        for low in range(0, breadth, width):
            edge_ref[end, piece, :, low : low + width] = gathered(
                vertical_ref[order], field_ref[block, :, low : low + width]
            )

    held = per_tile * patch_rows
    for total_ref in totals:
        total_ref[...] = jnp.zeros(total_ref.shape, F32)
    cols = breadth // patch_cols
    rows = height // patch_rows
    turn = 0
    for row in range(rows):
        top = row * patch_rows
        for col in range(cols):
            across = slice(col * patch_cols, (col + 1) * patch_cols)
            for piece in range(pieces):
                index = ids_ref[(piece * rows + row) * cols + col]
                place = pl.ds(pl.multiple_of(index * patch_rows, patch_rows), patch_rows)
                value = gradient_ref[piece, top : top + patch_rows, across]
                if top < rim:
                    value = value + edge_ref[0, piece, rim + top : rim + top + patch_rows, across]
                if top >= height - rim:
                    start = top - (height - rim)
                    value = value + edge_ref[1, piece, start : start + patch_rows, across]
                totals[turn % len(totals)][place, :] += value
                turn += 1
    for owner in range(sums_ref.shape[0] // slot):
        place = slice(owner * held, (owner + 1) * held)
        total = totals[0][place, :]
        for total_ref in totals[1:]:
            total = total + total_ref[place, :]
        sums_ref[owner * slot : owner * slot + held, :] = total.astype(sums_ref.dtype)
        if slot > held:
            named = counted_ref[owner * per_tile : (owner + 1) * per_tile, :]
            spare = jnp.zeros((slot - held - per_tile, named.shape[1]), F32)
            sums_ref[owner * slot + held : (owner + 1) * slot, :] = jnp.concatenate([named, spare], axis=0).astype(
                sums_ref.dtype
            )


def update_kernel(sky_ref, parts_ref, *refs, per_tile, slot, first, last):
    refs = list(refs)
    held = sky_ref.shape[0]
    total = parts_ref[:slot, :].astype(F32)
    for start in range(slot, parts_ref.shape[0], slot):
        total = total + parts_ref[start : start + slot, :].astype(F32)
    if first:
        named = total[held : held + per_tile]
        repeat = held // per_tile
        counts = jnp.broadcast_to(named[:, None, :], (named.shape[0], repeat, named.shape[1])).reshape(sky_ref.shape)
        refs.pop()[...] = counts
    else:
        counts = refs.pop(0)[...]
    fresh = sky_ref[...] - ETA * total[:held] / jnp.maximum(counts, 1.0)
    refs[0][...] = fresh
    if not last:
        for start in range(0, refs[1].shape[0], held):
            refs[1][start : start + held, :] = fresh.astype(BF16)


def per_device(sky_map, coeffs, observed, vert_taps, horiz_taps, owner_ids, offset):
    pieces, height, breadth = observed.shape
    modes = coeffs.shape[1]
    per_tile, patch_rows, patch_cols = sky_map.shape[1:]
    patch = (patch_rows, patch_cols)
    margin = (vert_taps.shape[1] - 1) // 2
    exp_count = lax.axis_size("exp")
    held = per_tile * patch_rows
    known = exp_count * held
    ext = round_up(margin, ROWS)
    rim = round_up(ext + margin, ROWS)
    width = min(breadth, 2 * patch_cols)
    routes = pair_routes("sub")
    vmem = pl.BlockSpec(memory_space=pltpu.VMEM)
    smem = pl.BlockSpec(memory_space=pltpu.SMEM)
    somewhere = pl.BlockSpec(memory_space=pl.ANY)

    def exchange(block):
        return lax.all_to_all(block, "exp", split_axis=0, concat_axis=0, tiled=True)

    sky = pltpu.with_memory_space_constraint(sky_map.reshape(held, patch_cols), pltpu.HBM)
    even = (1 - lax.axis_index("sub") % 2).astype(jnp.int32).reshape(1)
    coeffs = pltpu.with_memory_space_constraint(coeffs, pltpu.HBM)
    observed = pltpu.with_memory_space_constraint(observed, pltpu.HBM)
    rim_shape = jax.ShapeDtypeStruct((pieces, modes + PARTS, ext, breadth), BF16)
    spread, own_near, own_far = pl.pallas_call(
        begin_kernel,
        out_shape=(jax.ShapeDtypeStruct((known, patch_cols), BF16), rim_shape, rim_shape),
        in_specs=[smem, somewhere, somewhere, somewhere],
        out_specs=(somewhere, vmem, vmem),
        scratch_shapes=[
            pltpu.VMEM((2, pieces, ext, breadth), F32),
            pltpu.VMEM((held, patch_cols), F32),
            pltpu.VMEM((known, patch_cols), BF16),
            pltpu.SemaphoreType.DMA((6,)),
        ],
        compiler_params=pltpu.CompilerParams(vmem_limit_bytes=8 << 20),
        name="begin",
    )(even, sky, coeffs, observed)
    tiles = exchange(spread)
    ids = (owner_ids.reshape(offset.shape) * per_tile + offset).reshape(-1)
    counted, taps = pl.pallas_call(
        prep_kernel,
        out_shape=(
            jax.ShapeDtypeStruct((exp_count * per_tile, patch_cols), F32),
            jax.ShapeDtypeStruct((3, round_up(modes, 8), LANES), F32),
        ),
        in_specs=[smem, somewhere, somewhere],
        out_specs=(vmem, vmem),
        scratch_shapes=[
            pltpu.VMEM(vert_taps.shape, BF16),
            pltpu.VMEM(horiz_taps.shape, BF16),
            pltpu.SemaphoreType.DMA((2,)),
        ],
        compiler_params=pltpu.CompilerParams(vmem_limit_bytes=4 << 20),
        name="prep",
    )(
        ids,
        pltpu.with_memory_space_constraint(vert_taps, pltpu.HBM),
        pltpu.with_memory_space_constraint(horiz_taps, pltpu.HBM),
    )
    rims_far = lax.ppermute(own_far, "sub", routes[1])
    rims_near = lax.ppermute(own_near, "sub", routes[0])
    ids, counted, taps = lax.optimization_barrier((ids, counted, taps))

    clipped, counts = None, None
    for step in range(STEPS):
        first, last = step == 0, step + 1 == STEPS
        picture, near, far = pl.pallas_call(
            functools.partial(picture_kernel, patch=patch),
            out_shape=(
                jax.ShapeDtypeStruct((pieces, height, breadth), BF16),
                jax.ShapeDtypeStruct((pieces, rim, breadth), BF16),
                jax.ShapeDtypeStruct((pieces, rim, breadth), BF16),
            ),
            in_specs=[smem, smem, vmem],
            out_specs=(vmem, vmem, vmem),
            scratch_shapes=[pltpu.VMEM((known, patch_cols), F32)],
            compiler_params=pltpu.CompilerParams(vmem_limit_bytes=8 << 20),
            name="picture",
        )(even, ids, tiles)
        far = lax.ppermute(far, "sub", routes[1])
        near = lax.ppermute(near, "sub", routes[0])
        slot = held + (round_up(per_tile, ROWS) if first else 0)
        inner = height - 2 * ext
        taken = vert_taps.shape[1]
        results = [
            pltpu.VMEM((pieces, height, breadth), F32),
            pltpu.VMEM((modes, width, width), BF16),
        ]
        if last:
            results.append(pltpu.VMEM((pieces, inner, breadth), F32))
        middle = pl.pallas_call(
            functools.partial(inner_kernel, patch=patch, taps=taken, with_clipped=last),
            out_shape=tuple(results),
            in_specs=[vmem, vmem] + [somewhere] * 2,
            out_specs=(vmem,) * len(results),
            scratch_shapes=[
                pltpu.VMEM((pieces, modes * inner, breadth), BF16),
                pltpu.VMEM((pieces, inner, breadth), F32),
                pltpu.VMEM((pieces, modes, inner, breadth), BF16),
                pltpu.VMEM((pieces, inner, breadth), F32),
                pltpu.VMEM((modes * inner, height), BF16),
                pltpu.VMEM((width, width), F32),
                pltpu.SemaphoreType.DMA((2,)),
            ],
            compiler_params=pltpu.CompilerParams(vmem_limit_bytes=16 << 20),
            cost_estimate=pl.CostEstimate(flops=3 * 10**9, bytes_accessed=5 * 10**6, transcendentals=0),
            name="inner",
        )(picture, taps, coeffs, observed)
        results = [jax.ShapeDtypeStruct((exp_count * slot, patch_cols), BF16)]
        if last:
            results.insert(0, jax.ShapeDtypeStruct((pieces, height, breadth), F32))
        held_here = [pltpu.with_memory_space_constraint(array, pltpu.VMEM) for array in middle]
        answer = pl.pallas_call(
            functools.partial(outer_kernel, patch=patch, per_tile=per_tile, slot=slot, taps=taken, with_clipped=last),
            out_shape=tuple(results),
            in_specs=[smem] * 2 + [vmem] * (9 + len(middle)),
            out_specs=(vmem,) * len(results),
            scratch_shapes=[
                pltpu.VMEM((2, pieces, 2 * rim, breadth), BF16),
                pltpu.VMEM((2 * pieces, modes * 2 * ext, breadth), BF16),
                pltpu.VMEM((2 * pieces, 2 * ext, breadth), F32),
                pltpu.VMEM((2, pieces, 2 * rim, breadth), F32),
                pltpu.VMEM((2, modes * 2 * ext, 2 * rim), BF16),
            ]
            + [pltpu.VMEM((known, patch_cols), F32)] * 4,
            compiler_params=pltpu.CompilerParams(vmem_limit_bytes=12 << 20),
            name="outer",
        )(even, ids, picture, near, far, counted, taps, own_near, own_far, rims_near, rims_far, *held_here)
        sums = answer[-1]
        if last:
            clipped = answer[0]
        parts = exchange(sums)
        sky_shape = jax.ShapeDtypeStruct((held, patch_cols), F32)
        results = [sky_shape]
        if not last:
            results.append(jax.ShapeDtypeStruct((known, patch_cols), BF16))
        if first:
            results.append(sky_shape)
        operands = [sky, parts] if first else [sky, parts, counts]
        answer = pl.pallas_call(
            functools.partial(update_kernel, per_tile=per_tile, slot=slot, first=first, last=last),
            out_shape=tuple(results),
            in_specs=[vmem] * len(operands),
            out_specs=(vmem,) * len(results),
            compiler_params=pltpu.CompilerParams(vmem_limit_bytes=4 << 20),
            name="update",
        )(*operands)
        sky = answer[0]
        if first:
            counts = answer[-1]
        if not last:
            tiles = exchange(answer[1])
    return sky.reshape(sky_map.shape), clipped


def solution(mesh):
    return jax.shard_map(
        per_device,
        mesh=mesh,
        in_specs=(
            P(("exp", "sub"), None, None, None),
            P("exp", None, "sub", None),
            P("exp", "sub", None),
            P(),
            P(),
            P("exp", "sub", None, None),
            P("exp", "sub", None),
        ),
        out_specs=(P(("exp", "sub"), None, None, None), P("exp", "sub", None)),
        check_vma=False,
    )
```

```python
import functools

import jax
import jax.numpy as jnp
from jax import lax
from jax.experimental import pallas as pl
from jax.experimental.pallas import tpu as pltpu
from jax.sharding import PartitionSpec as P

STEPS = 2
ETA = 0.5
DELTA = 1.0
ROWS = 16
LANES = 128
PARTS = 3
F32 = jnp.float32
BF16 = jnp.bfloat16


def round_up(value, unit):
    return -(-value // unit) * unit


def divisor(value, most):
    return max(k for k in range(1, most + 1) if value % k == 0)


def pair_routes(axis):
    count = lax.axis_size(axis)
    routes = []
    for first in (0, 1):
        pairs = [(k, k + 1) for k in range(first, count - 1, 2)]
        routes.append(pairs + [(b, a) for a, b in pairs])
    return routes


def is_even():
    return 1 - lax.rem(lax.axis_index("sub"), 2)


def begin_kernel(
    sky_any, coeffs_ref, observed_ref, vert_any, horiz_any, spread_any, near_ref, far_ref, taps_ref,
    seen_ref, sky_ref, spread_ref, vert_ref, horiz_ref, sems,
):
    modes, height = coeffs_ref.shape[1:3]
    ext = near_ref.shape[2]
    held = sky_ref.shape[0]
    even = is_even()
    near_at = pl.multiple_of(even * (height - ext), ROWS)
    far_at = pl.multiple_of((1 - even) * (height - ext), ROWS)
    copies = []
    sky_copy = pltpu.make_async_copy(sky_any, sky_ref, sems.at[4])
    sky_copy.start()
    for side, (start, out_ref) in enumerate(((near_at, near_ref), (far_at, far_ref))):
        copies.append(
            pltpu.make_async_copy(observed_ref.at[:, pl.ds(start, ext), :], seen_ref.at[side], sems.at[2 * side])
        )
        copies.append(
            pltpu.make_async_copy(
                coeffs_ref.at[:, :, pl.ds(start, ext), :], out_ref.at[:, pl.ds(0, modes)], sems.at[2 * side + 1]
            )
        )
    for copy in copies:
        copy.start()
    filters = [
        pltpu.make_async_copy(vert_any, vert_ref, sems.at[6]),
        pltpu.make_async_copy(horiz_any, horiz_ref, sems.at[7]),
    ]
    for copy in filters:
        copy.start()
    sky_copy.wait()
    rounded = sky_ref[...].astype(BF16)
    for start in range(0, spread_ref.shape[0], held):
        spread_ref[start : start + held, :] = rounded
    spread_copy = pltpu.make_async_copy(spread_ref, spread_any, sems.at[5])
    spread_copy.start()
    for side, out_ref in enumerate((near_ref, far_ref)):
        copies[2 * side].wait()
        rest = seen_ref[side]
        for part in range(PARTS):
            piece = rest.astype(BF16)
            out_ref[:, modes + part] = piece
            rest = rest - piece.astype(F32)
    taps_ref[...] = jnp.zeros(taps_ref.shape, F32)
    for place, (copy, filter_ref) in enumerate(zip(filters, (vert_ref, horiz_ref))):
        copy.wait()
        taps_ref[place, :modes, : filter_ref.shape[1]] = filter_ref[...].astype(F32)
    copies[1].wait()
    copies[3].wait()
    spread_copy.wait()


def picture_kernel(ids_ref, tiles_ref, picture_ref, near_ref, far_ref, wide_ref, *, patch):
    pieces, height, breadth = picture_ref.shape
    rim = near_ref.shape[1]
    patch_rows, patch_cols = patch
    wide_ref[...] = tiles_ref[...].astype(F32)
    cols = breadth // patch_cols
    rows = height // patch_rows
    together = ROWS // patch_rows
    for piece in range(pieces):
        for row in range(0, rows, together):
            for col in range(cols):
                parts = []
                for inner in range(row, row + together):
                    index = ids_ref[(piece * rows + inner) * cols + col]
                    start = pl.multiple_of(index * patch_rows, patch_rows)
                    parts.append(wide_ref[pl.ds(start, patch_rows), :])
                picture_ref[
                    piece, row * patch_rows : (row + together) * patch_rows, col * patch_cols : (col + 1) * patch_cols
                ] = jnp.concatenate(parts, axis=0).astype(BF16)
    even = is_even()
    near_ref[...] = picture_ref[:, pl.ds(pl.multiple_of(even * (height - rim), ROWS), rim), :]
    far_ref[...] = picture_ref[:, pl.ds(pl.multiple_of((1 - even) * (height - rim), ROWS), rim), :]


def windows_of(block, width, stride):
    count = max(1, (block.shape[1] - width) // stride + 1)
    return [block[:, k * stride : k * stride + width] for k in range(count)]


def joined(outs, width, stride):
    if len(outs) == 1:
        return [outs[0][:, k : k + stride] for k in range(0, width, stride)]
    lane = lax.broadcasted_iota(jnp.int32, (outs[0].shape[0], stride), 1)
    blocks = [outs[0][:, :stride]]
    for left, right in zip(outs[:-1], outs[1:]):
        blocks.append(jnp.where(lane < stride // 2, left[:, stride:], right[:, :stride]))
    blocks.append(outs[-1][:, stride:])
    return blocks


def lags(rows, cols, shift):
    return (
        lax.broadcasted_iota(jnp.int32, (rows, cols), 1) - lax.broadcasted_iota(jnp.int32, (rows, cols), 0) + shift
    )


def within(lag, taps):
    return ((lag >= 0) & (lag < taps)).astype(F32)


def ring_of(row, shift):
    turned = pltpu.roll(jnp.broadcast_to(row, (8, LANES)), (-shift) % LANES, 1)
    return pltpu.roll(jnp.broadcast_to(turned[:1], (LANES, LANES)), 0, 1, stride=1, stride_axis=0)


def tiled(ring, rows, cols):
    across = jnp.concatenate([ring] * (-(-cols // LANES)), axis=1)[:, :cols]
    return jnp.concatenate([across] * (-(-rows // LANES)), axis=0)[:rows]


def build_vertical(vertical_ref, taps_ref, modes, skew, taps, turned=None):
    tall, reach = vertical_ref.shape[0] // modes, vertical_ref.shape[1]
    inside = within(lags(tall, reach, skew), taps)
    for mode in range(modes):
        ring = ring_of(taps_ref[0, mode : mode + 1], skew)
        table = (tiled(ring, tall, reach) * inside).astype(BF16)
        start = mode * tall
        vertical_ref[start : start + tall, :] = table
        if turned is not None:
            turned[start : start + tall // 2, :] = table[tall // 2 :]
            turned[start + tall // 2 : start + tall, :] = table[: tall // 2]


def smooth(groups, field_ref, modes, tall, width, unroll):
    chunk = divisor(modes, 4) * tall

    def some_modes(turn, carry):
        start = pl.multiple_of(turn * chunk, ROWS)
        block = 0
        for table_ref, images in groups:
            table = table_ref[pl.ds(start, chunk), :]
            for image in images:
                for low in range(0, image.shape[1], width):
                    field_ref[block, pl.ds(start, chunk), low : low + width] = jnp.dot(
                        table, image[:, low : low + width], preferred_element_type=F32
                    ).astype(BF16)
                block += 1
        return carry

    lax.fori_loop(0, modes * tall // chunk, some_modes, 0, unroll=unroll)


def blur(blocks, table, side, stride):
    tall, width = blocks[0].shape[0], table.shape[0]
    cuts = [cut for block in blocks for cut in windows_of(block, width, stride)]
    result = lax.dot_general(
        jnp.concatenate(cuts, axis=0), table, (((1,), (side,)), ((), ())), preferred_element_type=F32
    )
    per = len(cuts) // len(blocks)
    outs = [result[k * tall : (k + 1) * tall] for k in range(len(cuts))]
    return [joined(outs[k * per : (k + 1) * per], width, stride) for k in range(len(blocks))]


def model_all(field_ref, model_ref, weights, across_of, modes, stride):
    tall = model_ref.shape[1]
    count = model_ref.shape[0]
    for mode in range(modes):
        start = mode * tall
        blocks = [field_ref[block, start : start + tall, :] for block in range(count)]
        for block, columns in enumerate(blur(blocks, across_of(mode), 1, stride)):
            weight = weights(block, mode).astype(F32)
            for k, column in enumerate(columns):
                place = slice(k * stride, (k + 1) * stride)
                if mode == 0:
                    model_ref[block, :, place] = weight[:, place] * column
                else:
                    model_ref[block, :, place] += weight[:, place] * column


def adjoint_all(field_ref, model_ref, weights, across_ref, modes, stride):
    tall = model_ref.shape[1]
    count = model_ref.shape[0]
    for mode in range(modes):
        start = mode * tall
        blocks = [(weights(block, mode).astype(F32) * model_ref[block]).astype(BF16) for block in range(count)]
        for block, columns in enumerate(blur(blocks, across_ref[mode], 0, stride)):
            for k, column in enumerate(columns):
                field_ref[block, start : start + tall, k * stride : (k + 1) * stride] = column.astype(BF16)


def gathered(table, field):
    return lax.dot_general(table, field, (((0,), (0,)), ((), ())), preferred_element_type=F32)


def inner_kernel(
    picture_ref, taps_ref, coeffs_any, observed_any, gradient_ref, across_ref, *refs, patch, taps, with_clipped,
):
    refs = list(refs)
    clipped_ref = refs.pop(0) if with_clipped else None
    field_ref, model_ref, coeffs_ref, seen_ref, vertical_ref, band_ref, sems = refs
    pieces, height, breadth = picture_ref.shape
    modes = coeffs_ref.shape[1]
    tall = coeffs_ref.shape[2]
    ext = (height - tall) // 2
    margin = (taps - 1) // 2
    stride = patch[1]
    width = across_ref.shape[1]

    moves = [
        (coeffs_any.at[:, :, pl.ds(ext, tall), :], coeffs_ref),
        (observed_any.at[:, pl.ds(ext, tall), :], seen_ref),
    ]
    copies = [pltpu.make_async_copy(source, target, sems.at[k]) for k, (source, target) in enumerate(moves)]
    for copy in copies:
        copy.start()

    band_ref[...] = within(lags(width, width, margin), taps)
    build_vertical(vertical_ref, taps_ref, modes, margin - ext, taps)
    smooth([(vertical_ref, [picture_ref.at[piece] for piece in range(pieces)])], field_ref, modes, tall, width, False)

    def across_of(mode):
        ring = tiled(ring_of(taps_ref[1, mode : mode + 1], margin), width, width)
        across_ref[mode] = (ring * band_ref[...]).astype(BF16)
        return across_ref[mode]

    def weights(block, mode):
        return coeffs_ref[block, mode]

    for copy in copies:
        copy.wait()
    model_all(field_ref, model_ref, weights, across_of, modes, stride)
    model_ref[...] = jnp.clip(model_ref[...] - seen_ref[...], -DELTA, DELTA)
    if with_clipped:
        clipped_ref[...] = model_ref[...]
    adjoint_all(field_ref, model_ref, weights, across_ref, modes, stride)
    for piece in range(pieces):
        for low in range(0, breadth, width):
            gradient_ref[piece, :, low : low + width] = gathered(vertical_ref[...], field_ref[piece, :, low : low + width])


def outer_kernel(
    ids_any, picture_ref, near_ref, far_ref, taps_ref, own_near_ref, own_far_ref,
    rims_near_ref, rims_far_ref, gradient_ref, across_ref, *refs, patch, per_tile, slot, taps, with_clipped,
):
    refs = list(refs)
    inner_ref = refs.pop(0) if with_clipped else None
    clipped_ref = refs.pop(0) if with_clipped else None
    sums_ref, image_ref, field_ref, model_ref, edge_ref, vertical_ref, counted_ref, ids_ref, sem, *totals = refs
    listed = pltpu.make_async_copy(ids_any, ids_ref, sem)
    listed.start()
    pieces, height, breadth = picture_ref.shape
    modes, ext = own_near_ref.shape[1] - PARTS, own_near_ref.shape[2]
    rim = near_ref.shape[1]
    tall = 2 * ext
    margin = (taps - 1) // 2
    patch_rows, patch_cols = patch
    stride = patch_cols
    width = across_ref.shape[1]
    even = is_even()
    near_row = pl.multiple_of(even * rim, ROWS)
    far_row = pl.multiple_of((1 - even) * rim, ROWS)

    image_ref[0, :, rim:, :] = picture_ref[:, :rim, :]
    image_ref[1, :, :rim, :] = picture_ref[:, height - rim :, :]
    image_ref[even, :, pl.ds(near_row, rim), :] = near_ref[...]
    image_ref[1 - even, :, pl.ds(far_row, rim), :] = far_ref[...]
    build_vertical(vertical_ref.at[0], taps_ref, modes, margin + ext - rim, taps, vertical_ref.at[1])
    ends = ((even, 1 - even, own_near_ref, rims_near_ref), (1 - even, even, own_far_ref, rims_far_ref))
    places = [(side, piece) for side in (0, 1) for piece in range(pieces)]
    groups = [
        (vertical_ref.at[order], [image_ref.at[end, piece] for piece in range(pieces)]) for end, order, *_ in ends
    ]
    smooth(groups, field_ref, modes, tall, width, True)

    def weights(block, mode):
        side, piece = places[block]
        return jnp.concatenate([ends[side][2][piece, mode], ends[side][3][piece, mode]], axis=0)

    def seen(block):
        side, piece = places[block]
        halves = []
        for rims_ref in ends[side][2:]:
            total = rims_ref[piece, modes].astype(F32)
            for part in range(1, PARTS):
                total = total + rims_ref[piece, modes + part].astype(F32)
            halves.append(total)
        return jnp.concatenate(halves, axis=0)

    listed.wait()
    if slot > per_tile * patch_rows:
        counted_ref[...] = jnp.zeros(counted_ref.shape, F32)
        for place in range(ids_ref.shape[0]):
            counted_ref[pl.ds(ids_ref[place], 1), :] += 1.0
    model_all(field_ref, model_ref, weights, lambda mode: across_ref[mode], modes, stride)
    for block in range(len(places)):
        model_ref[block] = jnp.clip(model_ref[block] - seen(block), -DELTA, DELTA)
    if with_clipped:
        for block, (side, piece) in enumerate(places):
            start = pl.multiple_of(ends[side][0] * (height - ext), ROWS)
            clipped_ref[piece, pl.ds(start, ext), :] = model_ref[block, :ext, :]
        for piece in range(pieces):
            clipped_ref[piece, ext : height - ext, :] = inner_ref[piece]
    adjoint_all(field_ref, model_ref, weights, across_ref, modes, stride)
    for block, (side, piece) in enumerate(places):
        end, order = ends[side][:2]
        for low in range(0, breadth, width):
            edge_ref[end, piece, :, low : low + width] = gathered(
                vertical_ref[order], field_ref[block, :, low : low + width]
            )

    held = per_tile * patch_rows
    for total_ref in totals:
        total_ref[...] = jnp.zeros(total_ref.shape, F32)
    cols = breadth // patch_cols
    rows = height // patch_rows
    turn = 0
    for row in range(rows):
        top = row * patch_rows
        for col in range(cols):
            across = slice(col * patch_cols, (col + 1) * patch_cols)
            for piece in range(pieces):
                index = ids_ref[(piece * rows + row) * cols + col]
                place = pl.ds(pl.multiple_of(index * patch_rows, patch_rows), patch_rows)
                value = gradient_ref[piece, top : top + patch_rows, across]
                if top < rim:
                    value = value + edge_ref[0, piece, rim + top : rim + top + patch_rows, across]
                if top >= height - rim:
                    start = top - (height - rim)
                    value = value + edge_ref[1, piece, start : start + patch_rows, across]
                totals[turn % len(totals)][place, :] += value
                turn += 1
    for owner in range(sums_ref.shape[0] // slot):
        place = slice(owner * held, (owner + 1) * held)
        total = totals[0][place, :]
        for total_ref in totals[1:]:
            total = total + total_ref[place, :]
        sums_ref[owner * slot : owner * slot + held, :] = total.astype(sums_ref.dtype)
        if slot > held:
            named = counted_ref[owner * per_tile : (owner + 1) * per_tile, :]
            spare = jnp.zeros((slot - held - per_tile, named.shape[1]), F32)
            sums_ref[owner * slot + held : (owner + 1) * slot, :] = jnp.concatenate([named, spare], axis=0).astype(
                sums_ref.dtype
            )


def update_kernel(sky_ref, parts_ref, *refs, per_tile, slot, first, last):
    refs = list(refs)
    held = sky_ref.shape[0]
    total = parts_ref[:slot, :].astype(F32)
    for start in range(slot, parts_ref.shape[0], slot):
        total = total + parts_ref[start : start + slot, :].astype(F32)
    if first:
        named = total[held : held + per_tile]
        repeat = held // per_tile
        counts = jnp.broadcast_to(named[:, None, :], (named.shape[0], repeat, named.shape[1])).reshape(sky_ref.shape)
        refs.pop()[...] = counts
    else:
        counts = refs.pop(0)[...]
    fresh = sky_ref[...] - ETA * total[:held] / jnp.maximum(counts, 1.0)
    refs[0][...] = fresh
    if not last:
        for start in range(0, refs[1].shape[0], held):
            refs[1][start : start + held, :] = fresh.astype(BF16)


def per_device(sky_map, coeffs, observed, vert_taps, horiz_taps, owner_ids, offset):
    pieces, height, breadth = observed.shape
    modes = coeffs.shape[1]
    per_tile, patch_rows, patch_cols = sky_map.shape[1:]
    patch = (patch_rows, patch_cols)
    margin = (vert_taps.shape[1] - 1) // 2
    exp_count = lax.axis_size("exp")
    held = per_tile * patch_rows
    known = exp_count * held
    ext = round_up(margin, ROWS)
    rim = round_up(ext + margin, ROWS)
    width = min(breadth, 2 * patch_cols)
    routes = pair_routes("sub")
    vmem = pl.BlockSpec(memory_space=pltpu.VMEM)
    smem = pl.BlockSpec(memory_space=pltpu.SMEM)
    somewhere = pl.BlockSpec(memory_space=pl.ANY)

    def exchange(block):
        return lax.all_to_all(block, "exp", split_axis=0, concat_axis=0, tiled=True)

    sky = pltpu.with_memory_space_constraint(sky_map.reshape(held, patch_cols), pltpu.HBM)
    coeffs = pltpu.with_memory_space_constraint(coeffs, pltpu.HBM)
    observed = pltpu.with_memory_space_constraint(observed, pltpu.HBM)
    rim_shape = jax.ShapeDtypeStruct((pieces, modes + PARTS, ext, breadth), BF16)
    spread, own_near, own_far, taps = pl.pallas_call(
        begin_kernel,
        out_shape=(
            jax.ShapeDtypeStruct((known, patch_cols), BF16),
            rim_shape,
            rim_shape,
            jax.ShapeDtypeStruct((2, round_up(modes, 8), LANES), F32),
        ),
        in_specs=[somewhere] * 5,
        out_specs=(somewhere, vmem, vmem, vmem),
        scratch_shapes=[
            pltpu.VMEM((2, pieces, ext, breadth), F32),
            pltpu.VMEM((held, patch_cols), F32),
            pltpu.VMEM((known, patch_cols), BF16),
            pltpu.VMEM(vert_taps.shape, BF16),
            pltpu.VMEM(horiz_taps.shape, BF16),
            pltpu.SemaphoreType.DMA((8,)),
        ],
        compiler_params=pltpu.CompilerParams(vmem_limit_bytes=8 << 20),
        name="begin",
    )(
        sky, coeffs, observed,
        pltpu.with_memory_space_constraint(vert_taps, pltpu.HBM),
        pltpu.with_memory_space_constraint(horiz_taps, pltpu.HBM),
    )
    tiles = exchange(spread)
    ids = (owner_ids.reshape(offset.shape) * per_tile + offset).reshape(-1)
    rims_far = lax.ppermute(own_far, "sub", routes[1])
    rims_near = lax.ppermute(own_near, "sub", routes[0])

    clipped, counts = None, None
    for step in range(STEPS):
        first, last = step == 0, step + 1 == STEPS
        picture, near, far = pl.pallas_call(
            functools.partial(picture_kernel, patch=patch),
            out_shape=(
                jax.ShapeDtypeStruct((pieces, height, breadth), BF16),
                jax.ShapeDtypeStruct((pieces, rim, breadth), BF16),
                jax.ShapeDtypeStruct((pieces, rim, breadth), BF16),
            ),
            in_specs=[smem, vmem],
            out_specs=(vmem, vmem, vmem),
            scratch_shapes=[pltpu.VMEM((known, patch_cols), F32)],
            compiler_params=pltpu.CompilerParams(vmem_limit_bytes=8 << 20),
            name="picture",
        )(ids, tiles)
        far = lax.ppermute(far, "sub", routes[1])
        near = lax.ppermute(near, "sub", routes[0])
        slot = held + (round_up(per_tile, ROWS) if first else 0)
        inner = height - 2 * ext
        taken = vert_taps.shape[1]
        results = [
            pltpu.VMEM((pieces, height, breadth), F32),
            pltpu.VMEM((modes, width, width), BF16),
        ]
        if last:
            results.append(pltpu.VMEM((pieces, inner, breadth), F32))
        middle = pl.pallas_call(
            functools.partial(inner_kernel, patch=patch, taps=taken, with_clipped=last),
            out_shape=tuple(results),
            in_specs=[vmem, vmem] + [somewhere] * 2,
            out_specs=(vmem,) * len(results),
            scratch_shapes=[
                pltpu.VMEM((pieces, modes * inner, breadth), BF16),
                pltpu.VMEM((pieces, inner, breadth), F32),
                pltpu.VMEM((pieces, modes, inner, breadth), BF16),
                pltpu.VMEM((pieces, inner, breadth), F32),
                pltpu.VMEM((modes * inner, height), BF16),
                pltpu.VMEM((width, width), F32),
                pltpu.SemaphoreType.DMA((2,)),
            ],
            compiler_params=pltpu.CompilerParams(vmem_limit_bytes=16 << 20),
            cost_estimate=pl.CostEstimate(flops=3 * 10**9, bytes_accessed=5 * 10**6, transcendentals=0),
            name="inner",
        )(picture, taps, coeffs, observed)
        results = [jax.ShapeDtypeStruct((exp_count * slot, patch_cols), BF16)]
        if last:
            results.insert(0, jax.ShapeDtypeStruct((pieces, height, breadth), F32))
        held_here = [pltpu.with_memory_space_constraint(array, pltpu.VMEM) for array in middle]
        answer = pl.pallas_call(
            functools.partial(outer_kernel, patch=patch, per_tile=per_tile, slot=slot, taps=taken, with_clipped=last),
            out_shape=tuple(results),
            in_specs=[somewhere] + [vmem] * (8 + len(middle)),
            out_specs=(vmem,) * len(results),
            scratch_shapes=[
                pltpu.VMEM((2, pieces, 2 * rim, breadth), BF16),
                pltpu.VMEM((2 * pieces, modes * 2 * ext, breadth), BF16),
                pltpu.VMEM((2 * pieces, 2 * ext, breadth), F32),
                pltpu.VMEM((2, pieces, 2 * rim, breadth), F32),
                pltpu.VMEM((2, modes * 2 * ext, 2 * rim), BF16),
                pltpu.VMEM((exp_count * per_tile, patch_cols), F32),
                pltpu.SMEM(ids.shape, jnp.int32),
                pltpu.SemaphoreType.DMA,
            ]
            + [pltpu.VMEM((known, patch_cols), F32)] * 4,
            compiler_params=pltpu.CompilerParams(vmem_limit_bytes=12 << 20),
            name="outer",
        )(ids, picture, near, far, taps, own_near, own_far, rims_near, rims_far, *held_here)
        sums = answer[-1]
        if last:
            clipped = answer[0]
        parts = exchange(sums)
        sky_shape = jax.ShapeDtypeStruct((held, patch_cols), F32)
        results = [sky_shape]
        if not last:
            results.append(jax.ShapeDtypeStruct((known, patch_cols), BF16))
        if first:
            results.append(sky_shape)
        operands = [sky, parts] if first else [sky, parts, counts]
        answer = pl.pallas_call(
            functools.partial(update_kernel, per_tile=per_tile, slot=slot, first=first, last=last),
            out_shape=tuple(results),
            in_specs=[vmem] * len(operands),
            out_specs=(vmem,) * len(results),
            compiler_params=pltpu.CompilerParams(vmem_limit_bytes=4 << 20),
            name="update",
        )(*operands)
        sky = answer[0]
        if first:
            counts = answer[-1]
        if not last:
            tiles = exchange(answer[1])
    return sky.reshape(sky_map.shape), clipped


def solution(mesh):
    return jax.shard_map(
        per_device,
        mesh=mesh,
        in_specs=(
            P(("exp", "sub"), None, None, None),
            P("exp", None, "sub", None),
            P("exp", "sub", None),
            P(),
            P(),
            P("exp", "sub", None, None),
            P("exp", "sub", None),
        ),
        out_specs=(P(("exp", "sub"), None, None, None), P("exp", "sub", None)),
        check_vma=False,
    )
```

```python
import functools

import jax
import jax.numpy as jnp
from jax import lax
from jax.experimental import pallas as pl
from jax.experimental.pallas import tpu as pltpu
from jax.sharding import PartitionSpec as P

STEPS = 2
ETA = 0.5
DELTA = 1.0
ROWS = 16
LANES = 128
PARTS = 3
F32 = jnp.float32
BF16 = jnp.bfloat16


def round_up(value, unit):
    return -(-value // unit) * unit


def divisor(value, most):
    return max(k for k in range(1, most + 1) if value % k == 0)


def pair_routes(axis):
    count = lax.axis_size(axis)
    routes = []
    for first in (0, 1):
        pairs = [(k, k + 1) for k in range(first, count - 1, 2)]
        routes.append(pairs + [(b, a) for a, b in pairs])
    return routes


def is_even():
    return 1 - lax.rem(lax.axis_index("sub"), 2)


def begin_kernel(
    sky_any, coeffs_ref, observed_ref, vert_any, horiz_any, spread_any, near_ref, far_ref, taps_ref,
    seen_ref, sky_ref, spread_ref, vert_ref, horiz_ref, sems,
):
    modes, height = coeffs_ref.shape[1:3]
    ext = near_ref.shape[2]
    held = sky_ref.shape[0]
    even = is_even()
    near_at = pl.multiple_of(even * (height - ext), ROWS)
    far_at = pl.multiple_of((1 - even) * (height - ext), ROWS)
    copies = []
    sky_copy = pltpu.make_async_copy(sky_any, sky_ref, sems.at[4])
    sky_copy.start()
    for side, (start, out_ref) in enumerate(((near_at, near_ref), (far_at, far_ref))):
        copies.append(
            pltpu.make_async_copy(observed_ref.at[:, pl.ds(start, ext), :], seen_ref.at[side], sems.at[2 * side])
        )
        copies.append(
            pltpu.make_async_copy(
                coeffs_ref.at[:, :, pl.ds(start, ext), :], out_ref.at[:, pl.ds(0, modes)], sems.at[2 * side + 1]
            )
        )
    for copy in copies:
        copy.start()
    filters = [
        pltpu.make_async_copy(vert_any, vert_ref, sems.at[6]),
        pltpu.make_async_copy(horiz_any, horiz_ref, sems.at[7]),
    ]
    for copy in filters:
        copy.start()
    sky_copy.wait()
    rounded = sky_ref[...].astype(BF16)
    for start in range(0, spread_ref.shape[0], held):
        spread_ref[start : start + held, :] = rounded
    spread_copy = pltpu.make_async_copy(spread_ref, spread_any, sems.at[5])
    spread_copy.start()
    for side, out_ref in enumerate((near_ref, far_ref)):
        copies[2 * side].wait()
        rest = seen_ref[side]
        for part in range(PARTS):
            piece = rest.astype(BF16)
            out_ref[:, modes + part] = piece
            rest = rest - piece.astype(F32)
    taps_ref[...] = jnp.zeros(taps_ref.shape, F32)
    for place, (copy, filter_ref) in enumerate(zip(filters, (vert_ref, horiz_ref))):
        copy.wait()
        taps_ref[place, :modes, : filter_ref.shape[1]] = filter_ref[...].astype(F32)
    copies[1].wait()
    copies[3].wait()
    spread_copy.wait()


def picture_kernel(ids_ref, tiles_ref, picture_ref, near_ref, far_ref, wide_ref, *, patch):
    pieces, height, breadth = picture_ref.shape
    rim = near_ref.shape[1]
    patch_rows, patch_cols = patch
    wide_ref[...] = tiles_ref[...].astype(F32)
    cols = breadth // patch_cols
    rows = height // patch_rows
    together = ROWS // patch_rows
    for piece in range(pieces):
        for row in range(0, rows, together):
            for col in range(cols):
                parts = []
                for inner in range(row, row + together):
                    index = ids_ref[(piece * rows + inner) * cols + col]
                    start = pl.multiple_of(index * patch_rows, patch_rows)
                    parts.append(wide_ref[pl.ds(start, patch_rows), :])
                picture_ref[
                    piece, row * patch_rows : (row + together) * patch_rows, col * patch_cols : (col + 1) * patch_cols
                ] = jnp.concatenate(parts, axis=0).astype(BF16)
    even = is_even()
    near_ref[...] = picture_ref[:, pl.ds(pl.multiple_of(even * (height - rim), ROWS), rim), :]
    far_ref[...] = picture_ref[:, pl.ds(pl.multiple_of((1 - even) * (height - rim), ROWS), rim), :]


def windows_of(block, width, stride):
    count = max(1, (block.shape[1] - width) // stride + 1)
    return [block[:, k * stride : k * stride + width] for k in range(count)]


def joined(outs, width, stride):
    if len(outs) == 1:
        return [outs[0][:, k : k + stride] for k in range(0, width, stride)]
    lane = lax.broadcasted_iota(jnp.int32, (outs[0].shape[0], stride), 1)
    blocks = [outs[0][:, :stride]]
    for left, right in zip(outs[:-1], outs[1:]):
        blocks.append(jnp.where(lane < stride // 2, left[:, stride:], right[:, :stride]))
    blocks.append(outs[-1][:, stride:])
    return blocks


def lags(rows, cols, shift):
    return (
        lax.broadcasted_iota(jnp.int32, (rows, cols), 1) - lax.broadcasted_iota(jnp.int32, (rows, cols), 0) + shift
    )


def within(lag, taps):
    return ((lag >= 0) & (lag < taps)).astype(F32)


def ring_of(row, shift):
    turned = pltpu.roll(jnp.broadcast_to(row, (8, LANES)), (-shift) % LANES, 1)
    return pltpu.roll(jnp.broadcast_to(turned[:1], (LANES, LANES)), 0, 1, stride=1, stride_axis=0)


def tiled(ring, rows, cols):
    across = jnp.concatenate([ring] * (-(-cols // LANES)), axis=1)[:, :cols]
    return jnp.concatenate([across] * (-(-rows // LANES)), axis=0)[:rows]


def build_vertical(vertical_ref, taps_ref, modes, skew, taps, turned=None):
    tall, reach = vertical_ref.shape[0] // modes, vertical_ref.shape[1]
    inside = within(lags(tall, reach, skew), taps)
    for mode in range(modes):
        ring = ring_of(taps_ref[0, mode : mode + 1], skew)
        table = (tiled(ring, tall, reach) * inside).astype(BF16)
        start = mode * tall
        vertical_ref[start : start + tall, :] = table
        if turned is not None:
            turned[start : start + tall // 2, :] = table[tall // 2 :]
            turned[start + tall // 2 : start + tall, :] = table[: tall // 2]


def smooth(groups, field_ref, modes, tall, width, unroll):
    chunk = divisor(modes, 4) * tall

    def some_modes(turn, carry):
        start = pl.multiple_of(turn * chunk, ROWS)
        block = 0
        for table_ref, images in groups:
            table = table_ref[pl.ds(start, chunk), :]
            for image in images:
                for low in range(0, image.shape[1], width):
                    field_ref[block, pl.ds(start, chunk), low : low + width] = jnp.dot(
                        table, image[:, low : low + width], preferred_element_type=F32
                    ).astype(BF16)
                block += 1
        return carry

    lax.fori_loop(0, modes * tall // chunk, some_modes, 0, unroll=unroll)


def blur(blocks, table, side, stride):
    tall, width = blocks[0].shape[0], table.shape[0]
    cuts = [cut for block in blocks for cut in windows_of(block, width, stride)]
    result = lax.dot_general(
        jnp.concatenate(cuts, axis=0), table, (((1,), (side,)), ((), ())), preferred_element_type=F32
    )
    per = len(cuts) // len(blocks)
    outs = [result[k * tall : (k + 1) * tall] for k in range(len(cuts))]
    return [joined(outs[k * per : (k + 1) * per], width, stride) for k in range(len(blocks))]


def model_all(field_ref, model_ref, weights, across_of, modes, stride):
    tall = model_ref.shape[1]
    count = model_ref.shape[0]
    for mode in range(modes):
        start = mode * tall
        blocks = [field_ref[block, start : start + tall, :] for block in range(count)]
        for block, columns in enumerate(blur(blocks, across_of(mode), 1, stride)):
            weight = weights(block, mode).astype(F32)
            for k, column in enumerate(columns):
                place = slice(k * stride, (k + 1) * stride)
                if mode == 0:
                    model_ref[block, :, place] = weight[:, place] * column
                else:
                    model_ref[block, :, place] += weight[:, place] * column


def adjoint_all(field_ref, model_ref, weights, across_ref, modes, stride):
    tall = model_ref.shape[1]
    count = model_ref.shape[0]
    for mode in range(modes):
        start = mode * tall
        blocks = [(weights(block, mode).astype(F32) * model_ref[block]).astype(BF16) for block in range(count)]
        for block, columns in enumerate(blur(blocks, across_ref[mode], 0, stride)):
            for k, column in enumerate(columns):
                field_ref[block, start : start + tall, k * stride : (k + 1) * stride] = column.astype(BF16)


def gathered(table, field):
    return lax.dot_general(table, field, (((0,), (0,)), ((), ())), preferred_element_type=F32)


def inner_kernel(
    picture_ref, taps_ref, coeffs_any, observed_any, gradient_ref, across_ref, *refs, patch, taps, with_clipped,
    resident,
):
    refs = list(refs)
    clipped_ref = refs.pop(0) if with_clipped else None
    field_ref, model_ref, coeffs_ref, seen_ref, vertical_ref, band_ref, sems = refs
    pieces, height, breadth = picture_ref.shape
    modes = coeffs_any.shape[1]
    tall = model_ref.shape[1]
    ext = (height - tall) // 2
    margin = (taps - 1) // 2
    stride = patch[1]
    width = across_ref.shape[1]

    moves = [(observed_any.at[:, pl.ds(ext, tall), :], seen_ref)]
    if not resident:
        moves.append((coeffs_any.at[:, :, pl.ds(ext, tall), :], coeffs_ref))
    copies = [pltpu.make_async_copy(source, target, sems.at[k]) for k, (source, target) in enumerate(moves)]
    for copy in copies:
        copy.start()

    band_ref[...] = within(lags(width, width, margin), taps)
    build_vertical(vertical_ref, taps_ref, modes, margin - ext, taps)
    smooth([(vertical_ref, [picture_ref.at[piece] for piece in range(pieces)])], field_ref, modes, tall, width, resident)

    def across_of(mode):
        ring = tiled(ring_of(taps_ref[1, mode : mode + 1], margin), width, width)
        across_ref[mode] = (ring * band_ref[...]).astype(BF16)
        return across_ref[mode]

    def weights(block, mode):
        return coeffs_any[block, mode, ext : ext + tall] if resident else coeffs_ref[block, mode]

    if not resident:
        for copy in copies:
            copy.wait()
    model_all(field_ref, model_ref, weights, across_of, modes, stride)
    if resident:
        copies[0].wait()
    model_ref[...] = jnp.clip(model_ref[...] - seen_ref[...], -DELTA, DELTA)
    if with_clipped:
        clipped_ref[...] = model_ref[...]
    adjoint_all(field_ref, model_ref, weights, across_ref, modes, stride)
    for piece in range(pieces):
        for low in range(0, breadth, width):
            gradient_ref[piece, :, low : low + width] = gathered(vertical_ref[...], field_ref[piece, :, low : low + width])


def outer_kernel(
    ids_any, picture_ref, near_ref, far_ref, taps_ref, own_near_ref, own_far_ref,
    rims_near_ref, rims_far_ref, gradient_ref, across_ref, *refs, patch, per_tile, slot, taps, with_clipped,
):
    refs = list(refs)
    inner_ref = refs.pop(0) if with_clipped else None
    clipped_ref = refs.pop(0) if with_clipped else None
    sums_ref, image_ref, field_ref, model_ref, edge_ref, vertical_ref, counted_ref, ids_ref, sem, *totals = refs
    listed = pltpu.make_async_copy(ids_any, ids_ref, sem)
    listed.start()
    pieces, height, breadth = picture_ref.shape
    modes, ext = own_near_ref.shape[1] - PARTS, own_near_ref.shape[2]
    rim = near_ref.shape[1]
    tall = 2 * ext
    margin = (taps - 1) // 2
    patch_rows, patch_cols = patch
    stride = patch_cols
    width = across_ref.shape[1]
    even = is_even()
    near_row = pl.multiple_of(even * rim, ROWS)
    far_row = pl.multiple_of((1 - even) * rim, ROWS)

    image_ref[0, :, rim:, :] = picture_ref[:, :rim, :]
    image_ref[1, :, :rim, :] = picture_ref[:, height - rim :, :]
    image_ref[even, :, pl.ds(near_row, rim), :] = near_ref[...]
    image_ref[1 - even, :, pl.ds(far_row, rim), :] = far_ref[...]
    build_vertical(vertical_ref.at[0], taps_ref, modes, margin + ext - rim, taps, vertical_ref.at[1])
    ends = ((even, 1 - even, own_near_ref, rims_near_ref), (1 - even, even, own_far_ref, rims_far_ref))
    places = [(side, piece) for side in (0, 1) for piece in range(pieces)]
    groups = [
        (vertical_ref.at[order], [image_ref.at[end, piece] for piece in range(pieces)]) for end, order, *_ in ends
    ]
    smooth(groups, field_ref, modes, tall, width, True)

    def weights(block, mode):
        side, piece = places[block]
        return jnp.concatenate([ends[side][2][piece, mode], ends[side][3][piece, mode]], axis=0)

    def seen(block):
        side, piece = places[block]
        halves = []
        for rims_ref in ends[side][2:]:
            total = rims_ref[piece, modes].astype(F32)
            for part in range(1, PARTS):
                total = total + rims_ref[piece, modes + part].astype(F32)
            halves.append(total)
        return jnp.concatenate(halves, axis=0)

    listed.wait()
    if slot > per_tile * patch_rows:
        counted_ref[...] = jnp.zeros(counted_ref.shape, F32)
        for place in range(ids_ref.shape[0]):
            counted_ref[pl.ds(ids_ref[place], 1), :] += 1.0
    model_all(field_ref, model_ref, weights, lambda mode: across_ref[mode], modes, stride)
    for block in range(len(places)):
        model_ref[block] = jnp.clip(model_ref[block] - seen(block), -DELTA, DELTA)
    if with_clipped:
        for block, (side, piece) in enumerate(places):
            start = pl.multiple_of(ends[side][0] * (height - ext), ROWS)
            clipped_ref[piece, pl.ds(start, ext), :] = model_ref[block, :ext, :]
        for piece in range(pieces):
            clipped_ref[piece, ext : height - ext, :] = inner_ref[piece]
    adjoint_all(field_ref, model_ref, weights, across_ref, modes, stride)
    for block, (side, piece) in enumerate(places):
        end, order = ends[side][:2]
        for low in range(0, breadth, width):
            edge_ref[end, piece, :, low : low + width] = gathered(
                vertical_ref[order], field_ref[block, :, low : low + width]
            )

    held = per_tile * patch_rows
    for total_ref in totals:
        total_ref[...] = jnp.zeros(total_ref.shape, F32)
    cols = breadth // patch_cols
    rows = height // patch_rows
    turn = 0
    for row in range(rows):
        top = row * patch_rows
        for col in range(cols):
            across = slice(col * patch_cols, (col + 1) * patch_cols)
            for piece in range(pieces):
                index = ids_ref[(piece * rows + row) * cols + col]
                place = pl.ds(pl.multiple_of(index * patch_rows, patch_rows), patch_rows)
                value = gradient_ref[piece, top : top + patch_rows, across]
                if top < rim:
                    value = value + edge_ref[0, piece, rim + top : rim + top + patch_rows, across]
                if top >= height - rim:
                    start = top - (height - rim)
                    value = value + edge_ref[1, piece, start : start + patch_rows, across]
                totals[turn % len(totals)][place, :] += value
                turn += 1
    for owner in range(sums_ref.shape[0] // slot):
        place = slice(owner * held, (owner + 1) * held)
        total = totals[0][place, :]
        for total_ref in totals[1:]:
            total = total + total_ref[place, :]
        sums_ref[owner * slot : owner * slot + held, :] = total.astype(sums_ref.dtype)
        if slot > held:
            named = counted_ref[owner * per_tile : (owner + 1) * per_tile, :]
            spare = jnp.zeros((slot - held - per_tile, named.shape[1]), F32)
            sums_ref[owner * slot + held : (owner + 1) * slot, :] = jnp.concatenate([named, spare], axis=0).astype(
                sums_ref.dtype
            )


def update_kernel(sky_ref, parts_ref, *refs, per_tile, slot, first, last):
    refs = list(refs)
    held = sky_ref.shape[0]
    total = parts_ref[:slot, :].astype(F32)
    for start in range(slot, parts_ref.shape[0], slot):
        total = total + parts_ref[start : start + slot, :].astype(F32)
    if first:
        named = total[held : held + per_tile]
        repeat = held // per_tile
        counts = jnp.broadcast_to(named[:, None, :], (named.shape[0], repeat, named.shape[1])).reshape(sky_ref.shape)
        refs.pop()[...] = counts
    else:
        counts = refs.pop(0)[...]
    fresh = sky_ref[...] - ETA * total[:held] / jnp.maximum(counts, 1.0)
    refs[0][...] = fresh
    if not last:
        for start in range(0, refs[1].shape[0], held):
            refs[1][start : start + held, :] = fresh.astype(BF16)


def per_device(sky_map, coeffs, observed, vert_taps, horiz_taps, owner_ids, offset):
    pieces, height, breadth = observed.shape
    modes = coeffs.shape[1]
    per_tile, patch_rows, patch_cols = sky_map.shape[1:]
    patch = (patch_rows, patch_cols)
    margin = (vert_taps.shape[1] - 1) // 2
    exp_count = lax.axis_size("exp")
    held = per_tile * patch_rows
    known = exp_count * held
    ext = round_up(margin, ROWS)
    rim = round_up(ext + margin, ROWS)
    width = min(breadth, 2 * patch_cols)
    routes = pair_routes("sub")
    vmem = pl.BlockSpec(memory_space=pltpu.VMEM)
    smem = pl.BlockSpec(memory_space=pltpu.SMEM)
    somewhere = pl.BlockSpec(memory_space=pl.ANY)

    def exchange(block):
        return lax.all_to_all(block, "exp", split_axis=0, concat_axis=0, tiled=True)

    sky = pltpu.with_memory_space_constraint(sky_map.reshape(held, patch_cols), pltpu.HBM)
    observed = pltpu.with_memory_space_constraint(observed, pltpu.HBM)
    rim_shape = jax.ShapeDtypeStruct((pieces, modes + PARTS, ext, breadth), BF16)
    spread, own_near, own_far, taps = pl.pallas_call(
        begin_kernel,
        out_shape=(
            jax.ShapeDtypeStruct((known, patch_cols), BF16),
            rim_shape,
            rim_shape,
            jax.ShapeDtypeStruct((2, round_up(modes, 8), LANES), F32),
        ),
        in_specs=[somewhere] * 5,
        out_specs=(somewhere, vmem, vmem, vmem),
        scratch_shapes=[
            pltpu.VMEM((2, pieces, ext, breadth), F32),
            pltpu.VMEM((held, patch_cols), F32),
            pltpu.VMEM((known, patch_cols), BF16),
            pltpu.VMEM(vert_taps.shape, BF16),
            pltpu.VMEM(horiz_taps.shape, BF16),
            pltpu.SemaphoreType.DMA((8,)),
        ],
        compiler_params=pltpu.CompilerParams(vmem_limit_bytes=8 << 20),
        name="begin",
    )(
        sky, pltpu.with_memory_space_constraint(coeffs, pltpu.HBM), observed,
        pltpu.with_memory_space_constraint(vert_taps, pltpu.HBM),
        pltpu.with_memory_space_constraint(horiz_taps, pltpu.HBM),
    )
    tiles = exchange(spread)
    ids = (owner_ids.reshape(offset.shape) * per_tile + offset).reshape(-1)
    rims_far = lax.ppermute(own_far, "sub", routes[1])
    rims_near = lax.ppermute(own_near, "sub", routes[0])

    clipped, counts = None, None
    for step in range(STEPS):
        first, last = step == 0, step + 1 == STEPS
        picture, near, far = pl.pallas_call(
            functools.partial(picture_kernel, patch=patch),
            out_shape=(
                jax.ShapeDtypeStruct((pieces, height, breadth), BF16),
                jax.ShapeDtypeStruct((pieces, rim, breadth), BF16),
                jax.ShapeDtypeStruct((pieces, rim, breadth), BF16),
            ),
            in_specs=[smem, vmem],
            out_specs=(vmem, vmem, vmem),
            scratch_shapes=[pltpu.VMEM((known, patch_cols), F32)],
            compiler_params=pltpu.CompilerParams(vmem_limit_bytes=8 << 20),
            name="picture",
        )(ids, tiles)
        far = lax.ppermute(far, "sub", routes[1])
        near = lax.ppermute(near, "sub", routes[0])
        slot = held + (round_up(per_tile, ROWS) if first else 0)
        inner = height - 2 * ext
        taken = vert_taps.shape[1]
        results = [
            pltpu.VMEM((pieces, height, breadth), F32),
            pltpu.VMEM((modes, width, width), BF16),
        ]
        if last:
            results.append(pltpu.VMEM((pieces, inner, breadth), F32))
        middle = pl.pallas_call(
            functools.partial(inner_kernel, patch=patch, taps=taken, with_clipped=last, resident=last),
            out_shape=tuple(results),
            in_specs=[vmem, vmem, vmem if last else somewhere, somewhere],
            out_specs=(vmem,) * len(results),
            scratch_shapes=[
                pltpu.VMEM((pieces, modes * inner, breadth), BF16),
                pltpu.VMEM((pieces, inner, breadth), F32),
                pltpu.VMEM((1, 1, ROWS, LANES) if last else (pieces, modes, inner, breadth), BF16),
                pltpu.VMEM((pieces, inner, breadth), F32),
                pltpu.VMEM((modes * inner, height), BF16),
                pltpu.VMEM((width, width), F32),
                pltpu.SemaphoreType.DMA((2,)),
            ],
            compiler_params=pltpu.CompilerParams(vmem_limit_bytes=16 << 20),
            cost_estimate=pl.CostEstimate(flops=3 * 10**9, bytes_accessed=5 * 10**6, transcendentals=0),
            name="inner",
        )(picture, taps, pltpu.with_memory_space_constraint(coeffs, pltpu.VMEM if last else pltpu.HBM), observed)
        results = [jax.ShapeDtypeStruct((exp_count * slot, patch_cols), BF16)]
        if last:
            results.insert(0, jax.ShapeDtypeStruct((pieces, height, breadth), F32))
        held_here = [pltpu.with_memory_space_constraint(array, pltpu.VMEM) for array in middle]
        answer = pl.pallas_call(
            functools.partial(outer_kernel, patch=patch, per_tile=per_tile, slot=slot, taps=taken, with_clipped=last),
            out_shape=tuple(results),
            in_specs=[somewhere] + [vmem] * (8 + len(middle)),
            out_specs=(vmem,) * len(results),
            scratch_shapes=[
                pltpu.VMEM((2, pieces, 2 * rim, breadth), BF16),
                pltpu.VMEM((2 * pieces, modes * 2 * ext, breadth), BF16),
                pltpu.VMEM((2 * pieces, 2 * ext, breadth), F32),
                pltpu.VMEM((2, pieces, 2 * rim, breadth), F32),
                pltpu.VMEM((2, modes * 2 * ext, 2 * rim), BF16),
                pltpu.VMEM((exp_count * per_tile, patch_cols), F32),
                pltpu.SMEM(ids.shape, jnp.int32),
                pltpu.SemaphoreType.DMA,
            ]
            + [pltpu.VMEM((known, patch_cols), F32)] * 4,
            compiler_params=pltpu.CompilerParams(vmem_limit_bytes=12 << 20),
            name="outer",
        )(ids, picture, near, far, taps, own_near, own_far, rims_near, rims_far, *held_here)
        sums = answer[-1]
        if last:
            clipped = answer[0]
        parts = exchange(sums)
        sky_shape = jax.ShapeDtypeStruct((held, patch_cols), F32)
        results = [sky_shape]
        if not last:
            results.append(jax.ShapeDtypeStruct((known, patch_cols), BF16))
        if first:
            results.append(sky_shape)
        operands = [sky, parts] if first else [sky, parts, counts]
        answer = pl.pallas_call(
            functools.partial(update_kernel, per_tile=per_tile, slot=slot, first=first, last=last),
            out_shape=tuple(results),
            in_specs=[vmem] * len(operands),
            out_specs=(vmem,) * len(results),
            compiler_params=pltpu.CompilerParams(vmem_limit_bytes=4 << 20),
            name="update",
        )(*operands)
        sky = answer[0]
        if first:
            counts = answer[-1]
        if not last:
            tiles = exchange(answer[1])
    return sky.reshape(sky_map.shape), clipped


def solution(mesh):
    return jax.shard_map(
        per_device,
        mesh=mesh,
        in_specs=(
            P(("exp", "sub"), None, None, None),
            P("exp", None, "sub", None),
            P("exp", "sub", None),
            P(),
            P(),
            P("exp", "sub", None, None),
            P("exp", "sub", None),
        ),
        out_specs=(P(("exp", "sub"), None, None, None), P("exp", "sub", None)),
        check_vma=False,
    )
```

```python
import functools

import jax
import jax.numpy as jnp
from jax import lax
from jax.experimental import pallas as pl
from jax.experimental.pallas import tpu as pltpu
from jax.sharding import PartitionSpec as P

STEPS = 2
ETA = 0.5
DELTA = 1.0
ROWS = 16
LANES = 128
PARTS = 3
F32 = jnp.float32
BF16 = jnp.bfloat16


def round_up(value, unit):
    return -(-value // unit) * unit


def divisor(value, most):
    return max(k for k in range(1, most + 1) if value % k == 0)


def pair_routes(axis):
    count = lax.axis_size(axis)
    routes = []
    for first in (0, 1):
        pairs = [(k, k + 1) for k in range(first, count - 1, 2)]
        routes.append(pairs + [(b, a) for a, b in pairs])
    return routes


def is_even():
    return 1 - lax.rem(lax.axis_index("sub"), 2)


def begin_kernel(
    sky_any, coeffs_ref, observed_ref, vert_any, horiz_any, spread_any, near_ref, far_ref, taps_ref,
    seen_ref, sky_ref, spread_ref, vert_ref, horiz_ref, sems,
):
    modes, height = coeffs_ref.shape[1:3]
    ext = near_ref.shape[2]
    held = sky_ref.shape[0]
    even = is_even()
    near_at = pl.multiple_of(even * (height - ext), ROWS)
    far_at = pl.multiple_of((1 - even) * (height - ext), ROWS)
    copies = []
    sky_copy = pltpu.make_async_copy(sky_any, sky_ref, sems.at[4])
    sky_copy.start()
    for side, (start, out_ref) in enumerate(((near_at, near_ref), (far_at, far_ref))):
        copies.append(
            pltpu.make_async_copy(observed_ref.at[:, pl.ds(start, ext), :], seen_ref.at[side], sems.at[2 * side])
        )
        copies.append(
            pltpu.make_async_copy(
                coeffs_ref.at[:, :, pl.ds(start, ext), :], out_ref.at[:, pl.ds(0, modes)], sems.at[2 * side + 1]
            )
        )
    for copy in copies:
        copy.start()
    filters = [
        pltpu.make_async_copy(vert_any, vert_ref, sems.at[6]),
        pltpu.make_async_copy(horiz_any, horiz_ref, sems.at[7]),
    ]
    for copy in filters:
        copy.start()
    sky_copy.wait()
    rounded = sky_ref[...].astype(BF16)
    for start in range(0, spread_ref.shape[0], held):
        spread_ref[start : start + held, :] = rounded
    spread_copy = pltpu.make_async_copy(spread_ref, spread_any, sems.at[5])
    spread_copy.start()
    for side, out_ref in enumerate((near_ref, far_ref)):
        copies[2 * side].wait()
        rest = seen_ref[side]
        for part in range(PARTS):
            piece = rest.astype(BF16)
            out_ref[:, modes + part] = piece
            rest = rest - piece.astype(F32)
    taps_ref[...] = jnp.zeros(taps_ref.shape, F32)
    for place, (copy, filter_ref) in enumerate(zip(filters, (vert_ref, horiz_ref))):
        copy.wait()
        taps_ref[place, :modes, : filter_ref.shape[1]] = filter_ref[...].astype(F32)
    copies[1].wait()
    copies[3].wait()
    spread_copy.wait()


def picture_kernel(ids_ref, tiles_ref, picture_ref, near_ref, far_ref, wide_ref, *, patch):
    pieces, height, breadth = picture_ref.shape
    rim = near_ref.shape[1]
    patch_rows, patch_cols = patch
    wide_ref[...] = tiles_ref[...].astype(F32)
    cols = breadth // patch_cols
    rows = height // patch_rows
    together = ROWS // patch_rows
    for piece in range(pieces):
        for row in range(0, rows, together):
            for col in range(cols):
                parts = []
                for inner in range(row, row + together):
                    index = ids_ref[(piece * rows + inner) * cols + col]
                    start = pl.multiple_of(index * patch_rows, patch_rows)
                    parts.append(wide_ref[pl.ds(start, patch_rows), :])
                picture_ref[
                    piece, row * patch_rows : (row + together) * patch_rows, col * patch_cols : (col + 1) * patch_cols
                ] = jnp.concatenate(parts, axis=0).astype(BF16)
    even = is_even()
    near_ref[...] = picture_ref[:, pl.ds(pl.multiple_of(even * (height - rim), ROWS), rim), :]
    far_ref[...] = picture_ref[:, pl.ds(pl.multiple_of((1 - even) * (height - rim), ROWS), rim), :]


def windows_of(block, width, stride):
    count = max(1, (block.shape[1] - width) // stride + 1)
    return [block[:, k * stride : k * stride + width] for k in range(count)]


def joined(outs, width, stride):
    if len(outs) == 1:
        return [outs[0][:, k : k + stride] for k in range(0, width, stride)]
    lane = lax.broadcasted_iota(jnp.int32, (outs[0].shape[0], stride), 1)
    blocks = [outs[0][:, :stride]]
    for left, right in zip(outs[:-1], outs[1:]):
        blocks.append(jnp.where(lane < stride // 2, left[:, stride:], right[:, :stride]))
    blocks.append(outs[-1][:, stride:])
    return blocks


def lags(rows, cols, shift):
    return (
        lax.broadcasted_iota(jnp.int32, (rows, cols), 1) - lax.broadcasted_iota(jnp.int32, (rows, cols), 0) + shift
    )


def within(lag, taps):
    return ((lag >= 0) & (lag < taps)).astype(F32)


def ring_of(row, shift):
    turned = pltpu.roll(jnp.broadcast_to(row, (8, LANES)), (-shift) % LANES, 1)
    return pltpu.roll(jnp.broadcast_to(turned[:1], (LANES, LANES)), 0, 1, stride=1, stride_axis=0)


def tiled(ring, rows, cols):
    across = jnp.concatenate([ring] * (-(-cols // LANES)), axis=1)[:, :cols]
    return jnp.concatenate([across] * (-(-rows // LANES)), axis=0)[:rows]


def build_vertical(vertical_ref, taps_ref, modes, skew, taps, turned=None):
    tall, reach = vertical_ref.shape[0] // modes, vertical_ref.shape[1]
    inside = within(lags(tall, reach, skew), taps)
    for mode in range(modes):
        ring = ring_of(taps_ref[0, mode : mode + 1], skew)
        table = (tiled(ring, tall, reach) * inside).astype(BF16)
        start = mode * tall
        vertical_ref[start : start + tall, :] = table
        if turned is not None:
            turned[start : start + tall // 2, :] = table[tall // 2 :]
            turned[start + tall // 2 : start + tall, :] = table[: tall // 2]


def smooth(groups, field_ref, modes, tall, width, unroll):
    chunk = divisor(modes, 4) * tall

    def some_modes(turn, carry):
        start = pl.multiple_of(turn * chunk, ROWS)
        block = 0
        for table_ref, images in groups:
            table = table_ref[pl.ds(start, chunk), :]
            for image in images:
                for low in range(0, image.shape[1], width):
                    field_ref[block, pl.ds(start, chunk), low : low + width] = jnp.dot(
                        table, image[:, low : low + width], preferred_element_type=F32
                    ).astype(BF16)
                block += 1
        return carry

    lax.fori_loop(0, modes * tall // chunk, some_modes, 0, unroll=unroll)


def blur(blocks, table, side, stride):
    tall, width = blocks[0].shape[0], table.shape[0]
    cuts = [cut for block in blocks for cut in windows_of(block, width, stride)]
    result = lax.dot_general(
        jnp.concatenate(cuts, axis=0), table, (((1,), (side,)), ((), ())), preferred_element_type=F32
    )
    per = len(cuts) // len(blocks)
    outs = [result[k * tall : (k + 1) * tall] for k in range(len(cuts))]
    return [joined(outs[k * per : (k + 1) * per], width, stride) for k in range(len(blocks))]


def model_all(field_ref, model_ref, weights, across_of, modes, stride):
    tall = model_ref.shape[1]
    count = model_ref.shape[0]
    for mode in range(modes):
        start = mode * tall
        blocks = [field_ref[block, start : start + tall, :] for block in range(count)]
        for block, columns in enumerate(blur(blocks, across_of(mode), 1, stride)):
            weight = weights(block, mode).astype(F32)
            for k, column in enumerate(columns):
                place = slice(k * stride, (k + 1) * stride)
                if mode == 0:
                    model_ref[block, :, place] = weight[:, place] * column
                else:
                    model_ref[block, :, place] += weight[:, place] * column


def adjoint_all(field_ref, model_ref, weights, across_ref, modes, stride):
    tall = model_ref.shape[1]
    count = model_ref.shape[0]
    for mode in range(modes):
        start = mode * tall
        blocks = [(weights(block, mode).astype(F32) * model_ref[block]).astype(BF16) for block in range(count)]
        for block, columns in enumerate(blur(blocks, across_ref[mode], 0, stride)):
            for k, column in enumerate(columns):
                field_ref[block, start : start + tall, k * stride : (k + 1) * stride] = column.astype(BF16)


def gathered(table, field):
    return lax.dot_general(table, field, (((0,), (0,)), ((), ())), preferred_element_type=F32)


def inner_kernel(
    picture_ref, taps_ref, coeffs_any, observed_any, gradient_ref, across_ref, *refs, patch, taps, with_clipped,
    resident,
):
    refs = list(refs)
    clipped_ref = refs.pop(0) if with_clipped else None
    field_ref, model_ref, coeffs_ref, seen_ref, vertical_ref, band_ref, sems = refs
    pieces, height, breadth = picture_ref.shape
    modes = coeffs_any.shape[1]
    tall = model_ref.shape[1]
    ext = (height - tall) // 2
    margin = (taps - 1) // 2
    stride = patch[1]
    width = across_ref.shape[1]

    moves = []
    if not resident:
        moves.append((observed_any.at[:, pl.ds(ext, tall), :], seen_ref))
        moves.append((coeffs_any.at[:, :, pl.ds(ext, tall), :], coeffs_ref))
    copies = [pltpu.make_async_copy(source, target, sems.at[k]) for k, (source, target) in enumerate(moves)]
    for copy in copies:
        copy.start()

    band_ref[...] = within(lags(width, width, margin), taps)
    build_vertical(vertical_ref, taps_ref, modes, margin - ext, taps)
    smooth([(vertical_ref, [picture_ref.at[piece] for piece in range(pieces)])], field_ref, modes, tall, width, resident)

    def across_of(mode):
        ring = tiled(ring_of(taps_ref[1, mode : mode + 1], margin), width, width)
        across_ref[mode] = (ring * band_ref[...]).astype(BF16)
        return across_ref[mode]

    def weights(block, mode):
        return coeffs_any[block, mode, ext : ext + tall] if resident else coeffs_ref[block, mode]

    if not resident:
        for copy in copies:
            copy.wait()
    model_all(field_ref, model_ref, weights, across_of, modes, stride)
    seen = observed_any[:, ext : ext + tall, :] if resident else seen_ref[...]
    model_ref[...] = jnp.clip(model_ref[...] - seen, -DELTA, DELTA)
    if with_clipped:
        clipped_ref[...] = model_ref[...]
    adjoint_all(field_ref, model_ref, weights, across_ref, modes, stride)
    for piece in range(pieces):
        for low in range(0, breadth, width):
            gradient_ref[piece, :, low : low + width] = gathered(vertical_ref[...], field_ref[piece, :, low : low + width])


def outer_kernel(
    ids_any, picture_ref, near_ref, far_ref, taps_ref, own_near_ref, own_far_ref,
    rims_near_ref, rims_far_ref, gradient_ref, across_ref, *refs, patch, per_tile, slot, taps, with_clipped,
):
    refs = list(refs)
    inner_ref = refs.pop(0) if with_clipped else None
    clipped_ref = refs.pop(0) if with_clipped else None
    sums_ref, image_ref, field_ref, model_ref, edge_ref, vertical_ref, counted_ref, ids_ref, sem, *totals = refs
    listed = pltpu.make_async_copy(ids_any, ids_ref, sem)
    listed.start()
    pieces, height, breadth = picture_ref.shape
    modes, ext = own_near_ref.shape[1] - PARTS, own_near_ref.shape[2]
    rim = near_ref.shape[1]
    tall = 2 * ext
    margin = (taps - 1) // 2
    patch_rows, patch_cols = patch
    stride = patch_cols
    width = across_ref.shape[1]
    even = is_even()
    near_row = pl.multiple_of(even * rim, ROWS)
    far_row = pl.multiple_of((1 - even) * rim, ROWS)

    image_ref[0, :, rim:, :] = picture_ref[:, :rim, :]
    image_ref[1, :, :rim, :] = picture_ref[:, height - rim :, :]
    image_ref[even, :, pl.ds(near_row, rim), :] = near_ref[...]
    image_ref[1 - even, :, pl.ds(far_row, rim), :] = far_ref[...]
    build_vertical(vertical_ref.at[0], taps_ref, modes, margin + ext - rim, taps, vertical_ref.at[1])
    ends = ((even, 1 - even, own_near_ref, rims_near_ref), (1 - even, even, own_far_ref, rims_far_ref))
    places = [(side, piece) for side in (0, 1) for piece in range(pieces)]
    groups = [
        (vertical_ref.at[order], [image_ref.at[end, piece] for piece in range(pieces)]) for end, order, *_ in ends
    ]
    smooth(groups, field_ref, modes, tall, width, True)

    def weights(block, mode):
        side, piece = places[block]
        return jnp.concatenate([ends[side][2][piece, mode], ends[side][3][piece, mode]], axis=0)

    def seen(block):
        side, piece = places[block]
        halves = []
        for rims_ref in ends[side][2:]:
            total = rims_ref[piece, modes].astype(F32)
            for part in range(1, PARTS):
                total = total + rims_ref[piece, modes + part].astype(F32)
            halves.append(total)
        return jnp.concatenate(halves, axis=0)

    listed.wait()
    if slot > per_tile * patch_rows:
        counted_ref[...] = jnp.zeros(counted_ref.shape, F32)
        for place in range(ids_ref.shape[0]):
            counted_ref[pl.ds(ids_ref[place], 1), :] += 1.0
    model_all(field_ref, model_ref, weights, lambda mode: across_ref[mode], modes, stride)
    for block in range(len(places)):
        model_ref[block] = jnp.clip(model_ref[block] - seen(block), -DELTA, DELTA)
    if with_clipped:
        for block, (side, piece) in enumerate(places):
            start = pl.multiple_of(ends[side][0] * (height - ext), ROWS)
            clipped_ref[piece, pl.ds(start, ext), :] = model_ref[block, :ext, :]
        for piece in range(pieces):
            clipped_ref[piece, ext : height - ext, :] = inner_ref[piece]
    adjoint_all(field_ref, model_ref, weights, across_ref, modes, stride)
    for block, (side, piece) in enumerate(places):
        end, order = ends[side][:2]
        for low in range(0, breadth, width):
            edge_ref[end, piece, :, low : low + width] = gathered(
                vertical_ref[order], field_ref[block, :, low : low + width]
            )

    held = per_tile * patch_rows
    for total_ref in totals:
        total_ref[...] = jnp.zeros(total_ref.shape, F32)
    cols = breadth // patch_cols
    rows = height // patch_rows
    turn = 0
    for row in range(rows):
        top = row * patch_rows
        for col in range(cols):
            across = slice(col * patch_cols, (col + 1) * patch_cols)
            for piece in range(pieces):
                index = ids_ref[(piece * rows + row) * cols + col]
                place = pl.ds(pl.multiple_of(index * patch_rows, patch_rows), patch_rows)
                value = gradient_ref[piece, top : top + patch_rows, across]
                if top < rim:
                    value = value + edge_ref[0, piece, rim + top : rim + top + patch_rows, across]
                if top >= height - rim:
                    start = top - (height - rim)
                    value = value + edge_ref[1, piece, start : start + patch_rows, across]
                totals[turn % len(totals)][place, :] += value
                turn += 1
    for owner in range(sums_ref.shape[0] // slot):
        place = slice(owner * held, (owner + 1) * held)
        total = totals[0][place, :]
        for total_ref in totals[1:]:
            total = total + total_ref[place, :]
        sums_ref[owner * slot : owner * slot + held, :] = total.astype(sums_ref.dtype)
        if slot > held:
            named = counted_ref[owner * per_tile : (owner + 1) * per_tile, :]
            spare = jnp.zeros((slot - held - per_tile, named.shape[1]), F32)
            sums_ref[owner * slot + held : (owner + 1) * slot, :] = jnp.concatenate([named, spare], axis=0).astype(
                sums_ref.dtype
            )


def update_kernel(sky_ref, parts_ref, *refs, per_tile, slot, first, last):
    refs = list(refs)
    held = sky_ref.shape[0]
    total = parts_ref[:slot, :].astype(F32)
    for start in range(slot, parts_ref.shape[0], slot):
        total = total + parts_ref[start : start + slot, :].astype(F32)
    if first:
        named = total[held : held + per_tile]
        repeat = held // per_tile
        counts = jnp.broadcast_to(named[:, None, :], (named.shape[0], repeat, named.shape[1])).reshape(sky_ref.shape)
        refs.pop()[...] = counts
    else:
        counts = refs.pop(0)[...]
    fresh = sky_ref[...] - ETA * total[:held] / jnp.maximum(counts, 1.0)
    refs[0][...] = fresh
    if not last:
        for start in range(0, refs[1].shape[0], held):
            refs[1][start : start + held, :] = fresh.astype(BF16)


def per_device(sky_map, coeffs, observed, vert_taps, horiz_taps, owner_ids, offset):
    pieces, height, breadth = observed.shape
    modes = coeffs.shape[1]
    per_tile, patch_rows, patch_cols = sky_map.shape[1:]
    patch = (patch_rows, patch_cols)
    margin = (vert_taps.shape[1] - 1) // 2
    exp_count = lax.axis_size("exp")
    held = per_tile * patch_rows
    known = exp_count * held
    ext = round_up(margin, ROWS)
    rim = round_up(ext + margin, ROWS)
    width = min(breadth, 2 * patch_cols)
    routes = pair_routes("sub")
    vmem = pl.BlockSpec(memory_space=pltpu.VMEM)
    smem = pl.BlockSpec(memory_space=pltpu.SMEM)
    somewhere = pl.BlockSpec(memory_space=pl.ANY)

    def exchange(block):
        return lax.all_to_all(block, "exp", split_axis=0, concat_axis=0, tiled=True)

    sky = pltpu.with_memory_space_constraint(sky_map.reshape(held, patch_cols), pltpu.HBM)
    rim_shape = jax.ShapeDtypeStruct((pieces, modes + PARTS, ext, breadth), BF16)
    spread, own_near, own_far, taps = pl.pallas_call(
        begin_kernel,
        out_shape=(
            jax.ShapeDtypeStruct((known, patch_cols), BF16),
            rim_shape,
            rim_shape,
            jax.ShapeDtypeStruct((2, round_up(modes, 8), LANES), F32),
        ),
        in_specs=[somewhere] * 5,
        out_specs=(somewhere, vmem, vmem, vmem),
        scratch_shapes=[
            pltpu.VMEM((2, pieces, ext, breadth), F32),
            pltpu.VMEM((held, patch_cols), F32),
            pltpu.VMEM((known, patch_cols), BF16),
            pltpu.VMEM(vert_taps.shape, BF16),
            pltpu.VMEM(horiz_taps.shape, BF16),
            pltpu.SemaphoreType.DMA((8,)),
        ],
        compiler_params=pltpu.CompilerParams(vmem_limit_bytes=8 << 20),
        name="begin",
    )(
        sky,
        pltpu.with_memory_space_constraint(coeffs, pltpu.HBM),
        pltpu.with_memory_space_constraint(observed, pltpu.HBM),
        pltpu.with_memory_space_constraint(vert_taps, pltpu.HBM),
        pltpu.with_memory_space_constraint(horiz_taps, pltpu.HBM),
    )
    tiles = exchange(spread)
    ids = (owner_ids.reshape(offset.shape) * per_tile + offset).reshape(-1)
    rims_far = lax.ppermute(own_far, "sub", routes[1])
    rims_near = lax.ppermute(own_near, "sub", routes[0])

    clipped, counts = None, None
    for step in range(STEPS):
        first, last = step == 0, step + 1 == STEPS
        picture, near, far = pl.pallas_call(
            functools.partial(picture_kernel, patch=patch),
            out_shape=(
                jax.ShapeDtypeStruct((pieces, height, breadth), BF16),
                jax.ShapeDtypeStruct((pieces, rim, breadth), BF16),
                jax.ShapeDtypeStruct((pieces, rim, breadth), BF16),
            ),
            in_specs=[smem, vmem],
            out_specs=(vmem, vmem, vmem),
            scratch_shapes=[pltpu.VMEM((known, patch_cols), F32)],
            compiler_params=pltpu.CompilerParams(vmem_limit_bytes=8 << 20),
            name="picture",
        )(ids, tiles)
        far = lax.ppermute(far, "sub", routes[1])
        near = lax.ppermute(near, "sub", routes[0])
        slot = held + (round_up(per_tile, ROWS) if first else 0)
        inner = height - 2 * ext
        taken = vert_taps.shape[1]
        results = [
            pltpu.VMEM((pieces, height, breadth), F32),
            pltpu.VMEM((modes, width, width), BF16),
        ]
        if last:
            results.append(pltpu.VMEM((pieces, inner, breadth), F32))
        middle = pl.pallas_call(
            functools.partial(inner_kernel, patch=patch, taps=taken, with_clipped=last, resident=last),
            out_shape=tuple(results),
            in_specs=[vmem, vmem] + [vmem if last else somewhere] * 2,
            out_specs=(vmem,) * len(results),
            scratch_shapes=[
                pltpu.VMEM((pieces, modes * inner, breadth), BF16),
                pltpu.VMEM((pieces, inner, breadth), F32),
                pltpu.VMEM((1, 1, ROWS, LANES) if last else (pieces, modes, inner, breadth), BF16),
                pltpu.VMEM((pieces, inner, breadth), F32),
                pltpu.VMEM((modes * inner, height), BF16),
                pltpu.VMEM((width, width), F32),
                pltpu.SemaphoreType.DMA((2,)),
            ],
            compiler_params=pltpu.CompilerParams(vmem_limit_bytes=16 << 20),
            cost_estimate=pl.CostEstimate(flops=3 * 10**9, bytes_accessed=5 * 10**6, transcendentals=0),
            name="inner",
        )(
            picture, taps,
            pltpu.with_memory_space_constraint(coeffs, pltpu.VMEM if last else pltpu.HBM),
            pltpu.with_memory_space_constraint(observed, pltpu.VMEM if last else pltpu.HBM),
        )
        results = [jax.ShapeDtypeStruct((exp_count * slot, patch_cols), BF16)]
        if last:
            results.insert(0, jax.ShapeDtypeStruct((pieces, height, breadth), F32))
        held_here = [pltpu.with_memory_space_constraint(array, pltpu.VMEM) for array in middle]
        answer = pl.pallas_call(
            functools.partial(outer_kernel, patch=patch, per_tile=per_tile, slot=slot, taps=taken, with_clipped=last),
            out_shape=tuple(results),
            in_specs=[somewhere] + [vmem] * (8 + len(middle)),
            out_specs=(vmem,) * len(results),
            scratch_shapes=[
                pltpu.VMEM((2, pieces, 2 * rim, breadth), BF16),
                pltpu.VMEM((2 * pieces, modes * 2 * ext, breadth), BF16),
                pltpu.VMEM((2 * pieces, 2 * ext, breadth), F32),
                pltpu.VMEM((2, pieces, 2 * rim, breadth), F32),
                pltpu.VMEM((2, modes * 2 * ext, 2 * rim), BF16),
                pltpu.VMEM((exp_count * per_tile, patch_cols), F32),
                pltpu.SMEM(ids.shape, jnp.int32),
                pltpu.SemaphoreType.DMA,
            ]
            + [pltpu.VMEM((known, patch_cols), F32)] * 4,
            compiler_params=pltpu.CompilerParams(vmem_limit_bytes=12 << 20),
            name="outer",
        )(ids, picture, near, far, taps, own_near, own_far, rims_near, rims_far, *held_here)
        sums = answer[-1]
        if last:
            clipped = answer[0]
        parts = exchange(sums)
        sky_shape = jax.ShapeDtypeStruct((held, patch_cols), F32)
        results = [sky_shape]
        if not last:
            results.append(jax.ShapeDtypeStruct((known, patch_cols), BF16))
        if first:
            results.append(sky_shape)
        operands = [sky, parts] if first else [sky, parts, counts]
        answer = pl.pallas_call(
            functools.partial(update_kernel, per_tile=per_tile, slot=slot, first=first, last=last),
            out_shape=tuple(results),
            in_specs=[vmem] * len(operands),
            out_specs=(vmem,) * len(results),
            compiler_params=pltpu.CompilerParams(vmem_limit_bytes=4 << 20),
            name="update",
        )(*operands)
        sky = answer[0]
        if first:
            counts = answer[-1]
        if not last:
            tiles = exchange(answer[1])
    return sky.reshape(sky_map.shape), clipped


def solution(mesh):
    return jax.shard_map(
        per_device,
        mesh=mesh,
        in_specs=(
            P(("exp", "sub"), None, None, None),
            P("exp", None, "sub", None),
            P("exp", "sub", None),
            P(),
            P(),
            P("exp", "sub", None, None),
            P("exp", "sub", None),
        ),
        out_specs=(P(("exp", "sub"), None, None, None), P("exp", "sub", None)),
        check_vma=False,
    )
```
